32 devices in a mesh: tm: 32 (over z, y, x, core), tensor: 1.
Axes of the slice: x: 2, y: 2, z: 4, core: 2. Of those that a mesh axis runs over, the one named last changes fastest.
Arguments:
- tokens: bfloat16 [32, 768, 2048], P('tm', None, 'tensor'), may hold values from -12 to 12
- action_rows: bfloat16 [32, 2048], P('tm', 'tensor'), may hold values from -6 to 6
- pair_index: int32 [32], P('tm'), may hold values from 0 to 31, each once
- episode_id: int32 [32], replicated, may hold values from 0 to 3, never falling along the last dimension, each value on 1 to 16 neighbouring positions
- space_gain: float32 [2048], replicated, may hold values from 0.25 to 1.75
- space_qkv: bfloat16 [3, 2048, 2048], P(None, None, 'tensor'), as said below
- space_out: bfloat16 [2048, 2048], P('tensor'), may hold values from -0.125 to 0.125
- time_gain: float32 [2048], replicated, may hold values from 0.25 to 1.75
- time_qkv: bfloat16 [3, 2048, 2048], P(None, None, 'tensor'), as said below
- time_out: bfloat16 [2048, 2048], P('tensor'), may hold values from -0.125 to 0.125
Outputs:
- result: bfloat16 [32, 768, 2048], P('tm', None, 'tensor')
The draws below stay inside these ranges and needn't reach their ends.
Inputs may be any that keep to these rules, and one draw needn't show every extreme that they name: pair_index names every encoder row exactly once. episode_id never falls along the frames; an episode has 1 to 16 frames. `space_qkv`: three stacked projection matrices, in the order query, key, value. `time_qkv`: three stacked projection matrices, in the order query, key, value.
All inputs are finite; a program needn't handle non-finite values.
Results may differ from the reference program's by a relative error of at most 0.012.
Values may be sent and summed in bfloat16 or wider, within the bound.
No kernel may reach another device: no remote copies, remote signals or barrier semaphores. Data moves between devices by JAX's collectives and lax.ppermute only.
A program may use at most 192 MiB of HBM per device.

```python
import math
import jax
import jax.numpy as jnp
import numpy as np
from jax import lax

D = 2048
HEADS = 16
HEAD_DIM = 128
FRAME_TOKENS = 768
FRAMES = 32
EPISODES = 4


def stacked_projections(key):
    key_query, key_keys, key_values = jax.random.split(key, 3)
    shape_out = (D, HEADS * HEAD_DIM)
    query = jax.random.normal(key_query, shape_out, jnp.float32) * D ** (-0.5)
    noise = jax.random.normal(key_keys, shape_out, jnp.float32) * D ** (-0.5)
    values = jax.random.normal(key_values, shape_out, jnp.float32) * D ** (-0.5)
    keys = noise
    return jnp.stack([query, keys, values]).astype(jnp.bfloat16)


def draw_space_qkv(key, part):
    return stacked_projections(jax.random.fold_in(key, 11))


def draw_time_qkv(key, part):
    return stacked_projections(jax.random.fold_in(key, 23))


def draw_tokens(key, part):
    inner = jax.random.fold_in(key, 37)
    shape_all = (FRAMES, FRAME_TOKENS, D)
    place = jnp.arange(D, dtype=jnp.float32) / max(D - 1, 1)
    ramp = 0.3 * jnp.exp(place * jnp.log(10.0))
    values = jnp.clip(jax.random.normal(inner, shape_all, jnp.float32), -4.0, 4.0)
    return (values * ramp).astype(jnp.bfloat16)


def shard_levels(own_key, extent, pieces, low, high):
    level, own = 1.0, jax.random.fold_in(own_key, 6)
    for axis_at, shards_of in pieces:
        steps = jnp.exp(jax.random.uniform(jax.random.fold_in(own, axis_at), (shards_of,), jnp.float32, low / len(pieces), high / len(pieces)))
        level = level * jnp.repeat(steps, extent[axis_at] // shards_of).reshape([-1 if axis == axis_at else 1 for axis in range(len(extent))])
    return level


def length_profile(amount, total, bound, lean):
    portions = [(1 << 20) // math.isqrt(grade ** lean) + 1 for grade in range(2, amount + 1)]
    rest, counts = total - bound - (amount - 1), [1] * (amount - 1)
    while rest > 0:
        movable = [i for i in range(amount - 1) if counts[i] < bound]
        mass, remaining = sum([portions[i] for i in movable]), rest
        for i in movable:
            addition = min(bound - counts[i], max(1, remaining * portions[i] // mass), rest)
            counts[i] = counts[i] + addition
            rest = rest - addition
    return np.array([bound] + counts)


def uneven(stream_key, count, total, limit, lean):
    if count == 2:
        one = jax.random.randint(stream_key, (), max(1, total - limit), min(limit, total - 1) + 1)
        return jnp.stack([one, total - one])
    sizes = jnp.asarray(length_profile(count, total, limit, lean), jnp.int32)
    twos = (count - 1) // 2
    giver, receiver = sizes[1:1 + 2 * twos:2], sizes[2:2 + 2 * twos:2]
    room = jnp.minimum(giver - 1, limit - receiver)
    passed = jax.random.randint(jax.random.fold_in(stream_key, 1), (twos,), 0, 1 << 20) % (room + 1)
    sizes = sizes.at[1:1 + 2 * twos:2].set(giver - passed).at[2:2 + 2 * twos:2].set(receiver + passed)
    return sizes[jax.random.permutation(jax.random.fold_in(stream_key, 2), count)]


def centred(stream_key, extent, spread, reach, cuts=(), kind=jnp.bfloat16):
    factor_of = shard_levels(stream_key, extent, cuts, -0.22, 0.18) if cuts else 1.0
    drawn = jax.random.normal(stream_key, extent, jnp.float32) * spread * factor_of
    return jnp.minimum(jnp.maximum(drawn, -reach), reach).astype(kind)


def setup_inputs(seed: int = 0) -> dict:
    arg_keys = jax.random.split(jax.random.key(seed), 11)
    tokens = draw_tokens(jax.random.fold_in(arg_keys[10], 71), 0)
    action_rows = centred(arg_keys[1], (FRAMES, D), 1.0, 6.0, ((0, 32),))
    pair_index = jax.random.permutation(arg_keys[2], FRAMES).astype(jnp.int32)
    episode_id = jnp.searchsorted(jnp.cumsum(uneven(arg_keys[3], EPISODES, FRAMES, FRAMES // 2, 1)), jnp.arange(FRAMES), side="right").astype(jnp.int32)
    space_gain = jnp.clip(1.0 + 0.15 * jax.random.normal(arg_keys[4], (D,), jnp.float32), 0.25, 1.75)
    space_qkv = draw_space_qkv(jax.random.fold_in(arg_keys[10], 71), 0)
    space_out = centred(arg_keys[6], (HEADS * HEAD_DIM, D), (HEADS * HEAD_DIM) ** -0.5, 0.125)
    time_gain = jnp.clip(1.0 + 0.15 * jax.random.normal(arg_keys[7], (D,), jnp.float32), 0.25, 1.75)
    time_qkv = draw_time_qkv(jax.random.fold_in(arg_keys[10], 71), 0)
    time_out = centred(arg_keys[9], (HEADS * HEAD_DIM, D), (HEADS * HEAD_DIM) ** -0.5, 0.125)
    return dict(tokens=tokens, action_rows=action_rows, pair_index=pair_index, episode_id=episode_id, space_gain=space_gain, space_qkv=space_qkv, space_out=space_out, time_gain=time_gain, time_qkv=time_qkv, time_out=time_out)


EPSILON = 1e-06

def root_norm(values, gain):
    return values * lax.rsqrt(lax.optimization_barrier(jnp.mean(values * values, -1, keepdims=True)) + EPSILON) * gain

def reference(tokens, action_rows, pair_index, episode_id, space_gain, space_qkv, space_out, time_gain, time_qkv, time_out):
    frame_count = tokens.shape[0]
    picker = (pair_index[:, None] == jnp.arange(frame_count, dtype=jnp.int32)[None, :]).astype(jnp.bfloat16)
    action = jnp.dot(picker, action_rows, preferred_element_type=jnp.float32)
    start = tokens.astype(jnp.float32) + action[:, None, :]
    space_normed = root_norm(start, space_gain).astype(jnp.bfloat16)

    def space_frame(frame_rows):
        query = jnp.dot(frame_rows, space_qkv[0], preferred_element_type=jnp.float32).astype(jnp.bfloat16)
        keys = jnp.dot(frame_rows, space_qkv[1], preferred_element_type=jnp.float32).astype(jnp.bfloat16)
        values = jnp.dot(frame_rows, space_qkv[2], preferred_element_type=jnp.float32).astype(jnp.bfloat16)
        query = query.reshape(FRAME_TOKENS, HEADS, HEAD_DIM).astype(jnp.float32)
        keys = keys.reshape(FRAME_TOKENS, HEADS, HEAD_DIM).astype(jnp.float32)
        values = values.reshape(FRAME_TOKENS, HEADS, HEAD_DIM).astype(jnp.float32)
        scores = jnp.einsum('qhd,khd->hqk', query, keys) * HEAD_DIM ** (-0.5)
        probabilities = jax.nn.softmax(scores, -1).astype(jnp.bfloat16).astype(jnp.float32)
        mixture = jnp.einsum('hqk,khd->qhd', probabilities, values).astype(jnp.bfloat16)
        return jnp.dot(mixture.reshape(FRAME_TOKENS, HEADS * HEAD_DIM), space_out, preferred_element_type=jnp.float32)
    middle = start + lax.map(space_frame, space_normed)
    time_normed = root_norm(middle, time_gain).astype(jnp.bfloat16).reshape(frame_count * FRAME_TOKENS, D)
    projected = []
    for index in range(3):
        piece_out = jnp.dot(time_normed, time_qkv[index], preferred_element_type=jnp.float32).astype(jnp.bfloat16)
        projected.append(piece_out.reshape(frame_count, FRAME_TOKENS, HEADS, HEAD_DIM).astype(jnp.float32))
    scores = jnp.einsum('fphd,gphd->phfg', projected[0], projected[1]) * HEAD_DIM ** (-0.5)
    order = jnp.arange(frame_count, dtype=jnp.int32)
    allowed = (episode_id[:, None] == episode_id[None, :]) & (order[None, :] <= order[:, None])
    scores = jnp.where(allowed, scores, -1e+30)
    probabilities = jax.nn.softmax(scores, -1).astype(jnp.bfloat16).astype(jnp.float32)
    mixture = jnp.einsum('phfg,gphd->fphd', probabilities, projected[2]).astype(jnp.bfloat16)
    update = jnp.dot(mixture.reshape(frame_count * FRAME_TOKENS, HEADS * HEAD_DIM), time_out, preferred_element_type=jnp.float32)
    return (middle + update.reshape(frame_count, FRAME_TOKENS, D)).astype(jnp.bfloat16)
```

```python
import functools
import jax
import jax.numpy as jnp
from jax import lax
from jax.experimental import pallas as pl
from jax.experimental.pallas import tpu as pltpu
from jax.sharding import PartitionSpec as P

HEAD_DIM = 128


EPSILON = 1e-06
MIB = 1 << 20
SCALE = HEAD_DIM ** (-0.5)


def vmem(limit):
    return pltpu.CompilerParams(vmem_limit_bytes=limit * MIB)


def entry_kernel(blocks, tokens_ref, action_ref, gain_ref, weight_ref, keyval_ref, *rest):
    normed_refs, normed = rest[:-1], rest[-1]
    first = (pl.program_id(0) == 0) & (pl.program_id(1) == 0)

    @pl.when(first)
    def _():
        width = tokens_ref.shape[1]
        step = 128
        action = action_ref[...]
        gain = gain_ref[...]
        at = 0
        for ref in normed_refs:
            for row in range(0, ref.shape[0], step):
                start = tokens_ref[at + row:at + row + step, :].astype(jnp.float32) + action
                factor = lax.rsqrt(jnp.sum(start * start, -1, keepdims=True) / width + EPSILON)
                value = (start * factor * gain).astype(jnp.bfloat16)
                normed[at + row:at + row + step, :] = value
                ref[row:row + step, :] = value
            at += ref.shape[0]

    keyval_ref[0] = jnp.dot(
        normed[...], weight_ref[0], preferred_element_type=jnp.float32
    ).astype(jnp.bfloat16)


def entry(tokens, action, gain, weights, sizes, tile=512):
    rows, width = tokens.shape
    columns = weights.shape[2]
    return pl.pallas_call(
        functools.partial(entry_kernel, sizes),
        grid=(2, columns // tile),
        in_specs=[
            pl.BlockSpec((rows, width), lambda i, j: (0, 0)),
            pl.BlockSpec((1, width), lambda i, j: (0, 0)),
            pl.BlockSpec((1, width), lambda i, j: (0, 0)),
            pl.BlockSpec((1, width, tile), lambda i, j: (i + 1, 0, j)),
        ],
        out_specs=[pl.BlockSpec((1, rows, tile), lambda i, j: (i, 0, j))]
        + [pl.BlockSpec((size, width), lambda i, j: (0, 0)) for size in sizes],
        out_shape=[jax.ShapeDtypeStruct((2, rows, columns), jnp.bfloat16)]
        + [jax.ShapeDtypeStruct((size, width), jnp.bfloat16) for size in sizes],
        scratch_shapes=[pltpu.VMEM((rows, width), jnp.bfloat16)],
        compiler_params=vmem(48),
        cost_estimate=pl.CostEstimate(
            flops=4 * rows * width * columns, bytes_accessed=4 * width * columns, transcendentals=0
        ),
        name="space_keys",
    )(tokens, action, gain, weights)


def attend(query, keys, values, bias=None):
    scores = lax.dot_general(
        query, keys, (((1,), (1,)), ((), ())), preferred_element_type=jnp.float32
    )
    if bias is not None:
        scores = scores + bias
    top = jnp.max(scores, -1, keepdims=True)
    weights = jnp.exp((scores - top) * SCALE)
    total = jnp.sum(weights, -1, keepdims=True)
    mixed = jnp.dot(
        weights.astype(jnp.bfloat16), values, preferred_element_type=jnp.float32
    )
    return (mixed / total).astype(jnp.bfloat16)


def space_kernel(
    normed_ref, tokens_ref, action_ref, gain_ref, wq_ref, keyval_ref, out_hbm,
    time_ref, middle_ref, attended, out_weights, sem
):
    step, steps = pl.program_id(0), pl.num_programs(0)
    tile = wq_ref.shape[2]
    copy = pltpu.make_async_copy(out_hbm, out_weights, sem)

    @pl.when(step == 0)
    def _():
        copy.start()

    query = jnp.dot(
        normed_ref[...], wq_ref[0], preferred_element_type=jnp.float32
    ).astype(jnp.bfloat16)
    parts = []
    for head in range(tile // HEAD_DIM):
        cols = slice(head * HEAD_DIM, (head + 1) * HEAD_DIM)
        parts.append(attend(query[:, cols], keyval_ref[0, :, cols], keyval_ref[1, :, cols]))
    attended[step] = jnp.concatenate(parts, -1)

    @pl.when(step == steps - 1)
    def _():
        copy.wait()
        rows, width = time_ref.shape
        action = action_ref[...]
        gain = gain_ref[...]
        block = 128
        for row in range(0, rows, block):
            here = slice(row, row + block)
            middle = tokens_ref[here, :].astype(jnp.float32) + action
            for part in range(attended.shape[0]):
                middle += jnp.dot(
                    attended[part, here, :], out_weights[part * tile:(part + 1) * tile, :],
                    preferred_element_type=jnp.float32,
                )
            factor = lax.rsqrt(jnp.sum(middle * middle, -1, keepdims=True) / width + EPSILON)
            middle_ref[here, :] = middle.astype(middle_ref.dtype)
            time_ref[here, :] = (middle * factor * gain).astype(jnp.bfloat16)


def space(normed, tokens, action, gain, weights, keyval, out_weights, at, tile=512):
    rows, width = normed.shape
    columns = weights.shape[2]
    frame = keyval.shape[1]
    return pl.pallas_call(
        space_kernel,
        grid=(columns // tile,),
        in_specs=[
            pl.BlockSpec((rows, width), lambda i: (0, 0)),
            pl.BlockSpec((pl.Element(rows), pl.Element(width)), lambda i: (at, 0)),
            pl.BlockSpec((1, width), lambda i: (0, 0)),
            pl.BlockSpec((1, width), lambda i: (0, 0)),
            pl.BlockSpec((1, width, tile), lambda i: (0, 0, i)),
            pl.BlockSpec((2, frame, tile), lambda i: (0, 0, i)),
            pl.BlockSpec(memory_space=pl.ANY),
        ],
        out_specs=[pl.BlockSpec((rows, width), lambda i: (0, 0))] * 2,
        out_shape=[
            jax.ShapeDtypeStruct((rows, width), jnp.bfloat16),
            jax.ShapeDtypeStruct((rows, width), jnp.float32),
        ],
        scratch_shapes=[
            pltpu.VMEM((columns // tile, rows, tile), jnp.bfloat16),
            pltpu.VMEM(out_weights.shape, jnp.bfloat16),
            pltpu.SemaphoreType.DMA,
        ],
        compiler_params=vmem(56),
        cost_estimate=pl.CostEstimate(
            flops=4 * rows * width * columns + 8 * rows * frame * columns,
            bytes_accessed=4 * width * columns, transcendentals=rows * frame * columns // HEAD_DIM
        ),
        name="space_mix",
    )(normed, tokens, action, gain, weights, keyval, out_weights)


def time_kernel(places, received_ref, bias_ref, weight_ref, mixed_ref, ordered):
    frames, per_device, width = received_ref.shape
    tile = weight_ref.shape[2]
    block = frames * places

    if per_device > places:
        @pl.when(pl.program_id(0) == 0)
        def _():
            for part in range(per_device // places):
                ordered[part * block:(part + 1) * block, :] = received_ref[
                    :, part * places:(part + 1) * places, :
                ].reshape(block, width)
        value = ordered[...]
    else:
        value = received_ref[...].reshape(block, width)
    query, keys, values = [
        jnp.dot(value, weight_ref[index], preferred_element_type=jnp.float32).astype(jnp.bfloat16)
        for index in range(3)
    ]
    bias = bias_ref[...]
    for part in range(per_device // places):
        here = slice(part * block, (part + 1) * block)
        for head in range(tile // HEAD_DIM):
            cols = slice(head * HEAD_DIM, (head + 1) * HEAD_DIM)
            mixed = attend(query[here, cols], keys[here, cols], values[here, cols], bias)
            mixed_ref[:, part * places:(part + 1) * places, cols] = mixed.reshape(
                frames, places, HEAD_DIM
            )


def time_mix(received, bias, weights, places, tile=256):
    frames, per_device, width = received.shape
    columns = weights.shape[2]
    rows = frames * per_device
    block = frames * places
    return pl.pallas_call(
        functools.partial(time_kernel, places),
        grid=(columns // tile,),
        in_specs=[
            pl.BlockSpec((frames, per_device, width), lambda i: (0, 0, 0)),
            pl.BlockSpec((block, block), lambda i: (0, 0)),
            pl.BlockSpec((3, width, tile), lambda i: (0, 0, i)),
        ],
        out_specs=pl.BlockSpec((frames, per_device, tile), lambda i: (0, 0, i)),
        out_shape=jax.ShapeDtypeStruct((frames, per_device, columns), jnp.bfloat16),
        scratch_shapes=[pltpu.VMEM((rows, width), jnp.bfloat16)],
        compiler_params=vmem(48),
        cost_estimate=pl.CostEstimate(
            flops=6 * rows * width * columns, bytes_accessed=6 * width * columns,
            transcendentals=rows * block * columns // HEAD_DIM,
        ),
        name="time_mix",
    )(received, bias, weights)


def final_kernel(split, mixed_ref, weight_ref, middle_ref, *rest):
    result_ref = rest[-1]
    rows = result_ref.shape[0]
    here = pl.ds(pl.program_id(1) * rows, rows)
    result_ref[...] = (
        middle_ref[here, :]
        + jnp.dot(mixed_ref[here, :], weight_ref[...], preferred_element_type=jnp.float32)
    ).astype(jnp.bfloat16)


def finish(mixed, weights, middle, earlier, total, at, tile=512, block=256):
    rows, columns = mixed.shape
    width = weights.shape[1]
    extra = [] if earlier is None else [earlier]
    return pl.pallas_call(
        functools.partial(final_kernel, None),
        grid=(width // tile, rows // block),
        in_specs=[
            pl.BlockSpec((rows, columns), lambda j, r: (0, 0)),
            pl.BlockSpec((columns, tile), lambda j, r: (0, j)),
            pl.BlockSpec((rows, tile), lambda j, r: (0, j)),
        ] + [pl.BlockSpec(memory_space=pl.ANY) for _ in extra],
        out_specs=pl.BlockSpec((block, tile), lambda j, r: (at // block + r, j)),
        out_shape=jax.ShapeDtypeStruct((total, width), jnp.bfloat16),
        input_output_aliases={3: 0} if extra else {},
        compiler_params=vmem(40),
        cost_estimate=pl.CostEstimate(
            flops=2 * rows * width * columns, bytes_accessed=2 * width * columns, transcendentals=0
        ),
        name="time_out",
    )(mixed, weights, middle, *extra)


def fold_projection(weights, row_count, segment):
    flat_rows = segment.reshape(row_count, segment.shape[-1])
    return jnp.einsum("rc,icj->irj", flat_rows, weights, preferred_element_type=jnp.float32)


def space_frame(triple):
    query, keys, values = triple
    tokens_frame, columns = query.shape
    query = query.reshape(tokens_frame, columns // HEAD_DIM, HEAD_DIM)
    keys = keys.reshape(tokens_frame, columns // HEAD_DIM, HEAD_DIM)
    values = values.reshape(tokens_frame, columns // HEAD_DIM, HEAD_DIM)
    scores = jnp.einsum(
        "qhd,khd->hqk", query, keys, preferred_element_type=jnp.float32
    ) * HEAD_DIM ** (-0.5)
    probabilities = jax.nn.softmax(scores, -1).astype(jnp.bfloat16)
    mixture = jnp.einsum(
        "hqk,khd->qhd", probabilities, values, preferred_element_type=jnp.float32
    ).astype(jnp.bfloat16)
    return mixture.reshape(tokens_frame, columns)


def body_split_features(
    tokens,
    action_rows,
    pair_index,
    episode_id,
    space_gain,
    space_qkv,
    space_out,
    time_gain,
    time_qkv,
    time_out,
):
    frames_here, per_frame, share_width = tokens.shape
    width = share_width * lax.axis_size("tensor")
    columns = space_qkv.shape[2]
    row_count = frames_here * per_frame
    offset = lax.axis_index("tensor") * share_width
    every_row = lax.all_gather(action_rows, "tm", axis=0, tiled=True)
    frame_count = every_row.shape[0]
    picker = (pair_index[:, None] == jnp.arange(frame_count, dtype=jnp.int32)[None, :]).astype(
        jnp.bfloat16
    )
    action = jnp.dot(picker, every_row, preferred_element_type=jnp.float32)
    start = tokens.astype(jnp.float32) + action[:, None, :]
    squares = lax.psum(jnp.sum(start * start, -1), "tensor")
    factor = lax.rsqrt(squares / width + EPSILON)[..., None]
    space_normed = (
        start * factor * lax.dynamic_slice_in_dim(space_gain, offset, share_width)
    ).astype(jnp.bfloat16)
    space_proj = fold_projection(
        space_qkv, row_count, lax.all_gather(space_normed, "tensor", axis=2, tiled=True)
    ).astype(jnp.bfloat16)
    space_proj = space_proj.reshape(3, frames_here, per_frame, columns)
    attended = lax.map(space_frame, (space_proj[0], space_proj[1], space_proj[2]))
    partial_space = jnp.dot(
        attended.reshape(row_count, columns), space_out, preferred_element_type=jnp.float32
    ).reshape(frames_here, per_frame, width)
    own_part = lax.dynamic_slice_in_dim(partial_space, offset, share_width, 2) + start
    term_full = lax.dynamic_update_slice_in_dim(partial_space, own_part, offset, 2)
    summed = lax.psum(term_full.astype(jnp.bfloat16), "tensor").astype(jnp.float32)
    full_squares = jnp.sum(summed * summed, -1)
    time_normed = (
        summed * lax.rsqrt(full_squares / width + EPSILON)[..., None] * time_gain
    ).astype(jnp.bfloat16)
    time_proj = jnp.einsum(
        "rc,icj->irj",
        time_normed.reshape(row_count, width),
        time_qkv,
        preferred_element_type=jnp.float32,
    ).astype(jnp.bfloat16)
    middle = lax.dynamic_slice_in_dim(summed, offset, share_width, 2)
    time_proj = time_proj.reshape(3, frames_here, per_frame, columns)
    moved = (
        lax.all_to_all(time_proj[0], "tm", split_axis=1, concat_axis=0, tiled=True),
        lax.all_to_all(time_proj[1], "tm", split_axis=1, concat_axis=0, tiled=True),
        lax.all_to_all(time_proj[2], "tm", split_axis=1, concat_axis=0, tiled=True),
    )
    query_time, keys_time, values_time = moved
    places = query_time.shape[1]
    heads_here = columns // HEAD_DIM
    query_time = query_time.reshape(frame_count, places, heads_here, HEAD_DIM)
    keys_time = keys_time.reshape(frame_count, places, heads_here, HEAD_DIM)
    values_time = values_time.reshape(frame_count, places, heads_here, HEAD_DIM)
    scores = jnp.einsum(
        "fphd,gphd->phfg", query_time, keys_time, preferred_element_type=jnp.float32
    ) * HEAD_DIM ** (-0.5)
    order = jnp.arange(frame_count, dtype=jnp.int32)
    allowed = (episode_id[:, None] == episode_id[None, :]) & (order[None, :] <= order[:, None])
    scores = jnp.where(allowed, scores, -1e30)
    probabilities = jax.nn.softmax(scores, -1).astype(jnp.bfloat16)
    mixture = jnp.einsum(
        "phfg,gphd->fphd", probabilities, values_time, preferred_element_type=jnp.float32
    ).astype(jnp.bfloat16)
    returned = lax.all_to_all(
        mixture.reshape(frame_count, places, columns), "tm", split_axis=0, concat_axis=1, tiled=True
    )
    partial_time = jnp.dot(
        returned.reshape(row_count, columns), time_out, preferred_element_type=jnp.float32
    ).reshape(frames_here, per_frame, width)
    return (
        middle
        + lax.psum_scatter(
            partial_time.astype(jnp.bfloat16), "tensor", scatter_dimension=2, tiled=True
        ).astype(jnp.float32)
    ).astype(jnp.bfloat16)


def exchange(parts, groups):
    return lax.all_to_all(parts, "tm", split_axis=0, concat_axis=0, axis_index_groups=groups)


def frame_bias(episodes, places):
    frames = jnp.repeat(jnp.arange(episodes.shape[0], dtype=jnp.int32), places)
    owners = jnp.repeat(episodes, places)
    spots = jnp.tile(jnp.arange(places, dtype=jnp.int32), episodes.shape[0])
    allowed = (
        (spots[:, None] == spots[None, :])
        & (owners[:, None] == owners[None, :])
        & (frames[None, :] <= frames[:, None])
    )
    return jnp.where(allowed, 0.0, -1e30).astype(jnp.float32)


def body_whole_features(
    sizes,
    tokens,
    action_rows,
    pair_index,
    episode_id,
    space_gain,
    space_qkv,
    space_out,
    time_gain,
    time_qkv,
    time_out,
):
    _, per_frame, width = tokens.shape
    columns = space_qkv.shape[2]
    frame_count = lax.axis_size("tm")
    tokens = tokens.reshape(per_frame, width)
    every_row = exchange(
        jnp.broadcast_to(action_rows[None], (frame_count, 1, width)), None
    ).reshape(frame_count, width)
    picker = pair_index[:, None] == jnp.arange(frame_count, dtype=jnp.int32)[None, :]
    action = jnp.sum(
        jnp.where(picker[0, :, None], every_row, jnp.zeros_like(every_row)).astype(jnp.float32),
        0, keepdims=True,
    )
    space_gain = space_gain.reshape(1, width)
    time_gain = time_gain.reshape(1, width)
    keyval, *normed = entry(tokens, action, space_gain, space_qkv, sizes)
    offsets = [sum(sizes[:index]) for index in range(len(sizes))]

    def over(group_size):
        groups = [
            list(range(first, first + group_size))
            for first in range(0, frame_count, group_size)
        ]
        if group_size == frame_count:
            groups = None

        def run(_):
            base = lax.axis_index("tm") // group_size * group_size
            episodes = lax.dynamic_slice_in_dim(episode_id, base, group_size)
            middles, mixed = [], []
            for size, at, part in zip(sizes, offsets, normed):
                time_normed, middle = space(
                    part, tokens, action, time_gain, space_qkv, keyval, space_out, at
                )
                middles.append(middle)
                mixed.append(exchange(time_normed.reshape(group_size, size // group_size, width), groups))
            returned = []
            for size, part in zip(sizes, mixed):
                places = min(size // group_size, 16)
                bias = frame_bias(episodes, places)
                if places % 16:
                    part = part.reshape(size // 16, 16, width)
                    done = time_mix(part, bias, time_qkv, 16)
                else:
                    done = time_mix(part, bias, time_qkv, places)
                returned.append(exchange(done.reshape(group_size, size // group_size, columns), groups))
            result = None
            for size, at, part, middle in zip(sizes, offsets, returned, middles):
                result = finish(
                    part.reshape(size, columns), time_out, middle, result, per_frame, at
                )
            return result.reshape(1, per_frame, width)

        return run

    half = frame_count // 2
    apart = episode_id[half - 1] != episode_id[half]
    return lax.cond(apart, over(half), over(frame_count), 0)


def chunks(per_frame):
    return (per_frame // 3, per_frame - per_frame // 3)


def solution(mesh):
    sizes = dict(mesh.shape)

    def body(*arrays):
        frames_here, per_frame, width = arrays[0].shape
        pieces = chunks(per_frame)
        fits = (
            sizes["tensor"] == 1
            and frames_here == 1
            and sizes["tm"] % 2 == 0
            and all(piece % 256 == 0 and piece % sizes["tm"] == 0 for piece in pieces)
            and width % 512 == 0
            and arrays[5].shape[2] % 512 == 0
        )
        if fits:
            return body_whole_features(pieces, *arrays)
        return body_split_features(*arrays)

    return jax.shard_map(
        body,
        mesh=mesh,
        in_specs=(
            P("tm", None, "tensor"),
            P("tm", "tensor"),
            P("tm"),
            P(),
            P(),
            P(None, None, "tensor"),
            P("tensor", None),
            P(),
            P(None, None, "tensor"),
            P("tensor", None),
        ),
        out_specs=P("tm", None, "tensor"),
        check_vma=False,
    )
```

```python
import functools
import math
import jax
import jax.numpy as jnp
from jax import lax
from jax.experimental import pallas as pl
from jax.experimental.pallas import tpu as pltpu
from jax.sharding import PartitionSpec as P

HEAD_DIM = 128


EPSILON = 1e-06
MIB = 1 << 20
SCALE = HEAD_DIM ** (-0.5)
TILE = 512
ROWS = 128
AHEAD = 3
EXPONENT = SCALE / math.log(2.0)


def limits(mebibytes):
    return pltpu.CompilerParams(vmem_limit_bytes=mebibytes * MIB)


def in_hbm(count):
    return [pl.BlockSpec(memory_space=pl.ANY)] * count


def row_specs(pieces):
    return [
        pl.BlockSpec(pieces.shape, lambda: (0,) * pieces.ndim),
        pl.BlockSpec(memory_space=pltpu.SMEM),
    ]


def norm_rows(value, gain):
    squares = jnp.sum(value * value, -1, keepdims=True)
    factor = lax.rsqrt(squares / value.shape[1] + EPSILON)
    return (value * factor * gain).astype(jnp.bfloat16)


def attend(queries, keys, values, bias=None):
    scores = [
        lax.dot_general(query, key, (((1,), (1,)), ((), ())), preferred_element_type=jnp.float32)
        for query, key in zip(queries, keys)
    ]
    if bias is not None:
        scores = [score + bias for score in scores]
    weights = [
        jnp.exp2(score - jnp.max(score, -1, keepdims=True)).astype(jnp.bfloat16) for score in scores
    ]
    mixed = [
        jnp.dot(weight, value, preferred_element_type=jnp.float32)
        for weight, value in zip(weights, values)
    ]
    return [(part[:, :HEAD_DIM] / part[:, HEAD_DIM:]).astype(jnp.bfloat16) for part in mixed]


def own_row(rows_ref, pair_ref):
    row = rows_ref[pair_ref[0]].astype(jnp.float32)
    return jnp.concatenate([row[piece:piece + 1, :] for piece in range(row.shape[0])], -1)


def project(rows, weight):
    return jnp.dot(rows, weight, preferred_element_type=jnp.float32)


def heads_of(width):
    return [slice(at, at + HEAD_DIM) for at in range(0, width, HEAD_DIM)]


def mix_frame(rows_ref, weights_ref, weight_copy, keys_ref, values_ref, ready, attended_ref):
    tiles = weights_ref.shape[0]
    heads = heads_of(TILE)

    def tile(index, carry):
        weight_copy(index).wait()
        query = (project(rows_ref[...], weights_ref[index]) * EXPONENT).astype(jnp.bfloat16)
        ready(index)
        done = attend(
            [query[:, cols] for cols in heads],
            [keys_ref[index, :, cols] for cols in heads],
            [values_ref[index * len(heads) + head] for head in range(len(heads))],
        )
        for cols, part in zip(heads, done):
            attended_ref[index, :, cols] = part
        return carry

    lax.fori_loop(0, tiles, tile, 0)


def leave_frame(
    tokens_ref, action, gain, attended_ref, weights_ref, time_ref, middle_ref, time_hbm, middle_hbm, sems
):
    rows = time_ref.shape[0]
    copies = []
    for at in range(0, rows, ROWS):
        here = slice(at, at + ROWS)
        middle = tokens_ref[here, :].astype(jnp.float32) + action
        for part in range(attended_ref.shape[0]):
            middle += project(
                attended_ref[part, here, :], weights_ref[part * TILE:(part + 1) * TILE, :]
            )
        middle_ref[here, :] = middle
        time_ref[here, :] = norm_rows(middle, gain)
        for source, target, which in ((time_ref, time_hbm, 0), (middle_ref, middle_hbm, 1)):
            copy = pltpu.make_async_copy(source.at[here, :], target.at[here, :], sems.at[which])
            copy.start()
            copies.append(copy)
    for copy in copies:
        copy.wait()


def first_kernel(
    count, tokens_hbm, rows_ref, pair_ref, space_gain_ref, time_gain_ref, qkv_hbm, out_hbm,
    time_hbm, middle_hbm, normed_hbm, keyval_hbm,
    tokens, normed, wkv, wq, wo, keys, values, attended, time, middle,
    token_sem, wkv_sem, wq_sem, wo_sem, keyval_sem, normed_sem, out_sem
):
    tiles = wq.shape[0]
    heads = TILE // HEAD_DIM

    def cols(index):
        return pl.ds(pl.multiple_of(index * TILE, TILE), TILE)

    def wkv_copy(kind, index):
        slot = kind * tiles + index
        return pltpu.make_async_copy(qkv_hbm.at[kind + 1, :, cols(index)], wkv.at[slot], wkv_sem.at[slot])

    def wq_copy(index):
        return pltpu.make_async_copy(qkv_hbm.at[0, :, cols(index)], wq.at[index], wq_sem.at[index])

    def keys_out(index):
        return pltpu.make_async_copy(keys.at[index], keyval_hbm.at[0, :, cols(index)], keyval_sem)

    def values_out(head):
        return pltpu.make_async_copy(
            values.at[head, :, pl.ds(0, HEAD_DIM)],
            keyval_hbm.at[1, :, pl.ds(pl.multiple_of(head * HEAD_DIM, HEAD_DIM), HEAD_DIM)],
            keyval_sem,
        )

    pieces = tokens.shape[0] // ROWS // 2
    token_copies = [
        pltpu.make_async_copy(
            tokens_hbm.at[pl.ds(at * 2 * ROWS, 2 * ROWS), :],
            tokens.at[pl.ds(at * 2 * ROWS, 2 * ROWS), :], token_sem.at[at],
        )
        for at in range(pieces)
    ]
    out_copy = pltpu.make_async_copy(out_hbm, wo, wo_sem)
    rest = pltpu.make_async_copy(normed.at[pl.ds(count, tokens.shape[0] - count), :], normed_hbm, normed_sem)
    def stream(place):
        pl.when(place < 2 * tiles)(lambda: wkv_copy(place // tiles, place % tiles).start())
        pl.when((place >= 2 * tiles) & (place < 3 * tiles))(lambda: wq_copy(place - 2 * tiles).start())
        pl.when(place == 3 * tiles)(lambda: out_copy.start())

    for copy in token_copies:
        copy.start()
    for index in range(AHEAD):
        wkv_copy(0, index).start()

    action = own_row(rows_ref, pair_ref)
    gain = space_gain_ref[...]
    for at in range(0, tokens.shape[0], ROWS):
        if at % (2 * ROWS) == 0:
            token_copies[at // (2 * ROWS)].wait()
        here = slice(at, at + ROWS)
        normed[here, :] = norm_rows(tokens[here, :].astype(jnp.float32) + action, gain)
    rest.start()

    def key_tile(index, carry):
        stream(index + AHEAD)
        wkv_copy(0, index).wait()
        keys[index] = project(normed[...], wkv[index]).astype(jnp.bfloat16)
        keys_out(index).start()
        return carry

    def value_tile(index, carry):
        stream(tiles + index + AHEAD)
        wkv_copy(1, index).wait()
        value = project(normed[...], wkv[tiles + index]).astype(jnp.bfloat16)
        for head, where in enumerate(heads_of(TILE)):
            values[index * heads + head, :, :HEAD_DIM] = value[:, where]
            values[index * heads + head, :, HEAD_DIM:] = jnp.ones(
                (value.shape[0], HEAD_DIM), jnp.bfloat16
            )
            values_out(index * heads + head).start()
        return carry

    lax.fori_loop(0, tiles, key_tile, 0)
    lax.fori_loop(0, tiles, value_tile, 0)
    mix_frame(
        normed.at[pl.ds(0, count), :], wq, wq_copy, keys, values,
        lambda index: stream(2 * tiles + index + AHEAD), attended,
    )
    out_copy.wait()
    leave_frame(
        tokens, action, time_gain_ref[...], attended, wo, time, middle, time_hbm, middle_hbm, out_sem
    )
    rest.wait()
    for index in range(tiles):
        keys_out(index).wait()
    for head in range(tiles * heads):
        values_out(head).wait()


def first(tokens, action_pieces, pair_index, space_gain, time_gain, qkv, out, count):
    frame, width = tokens.shape
    columns = qkv.shape[2]
    tiles = columns // TILE
    dma = pltpu.SemaphoreType.DMA
    row = pl.BlockSpec((1, width), lambda: (0, 0))
    return pl.pallas_call(
        functools.partial(first_kernel, count),
        in_specs=in_hbm(1) + row_specs(action_pieces) + [row] * 2 + in_hbm(2),
        out_specs=in_hbm(4),
        out_shape=[
            jax.ShapeDtypeStruct((count, width), jnp.bfloat16),
            jax.ShapeDtypeStruct((count, width), jnp.float32),
            jax.ShapeDtypeStruct((frame - count, width), jnp.bfloat16),
            jax.ShapeDtypeStruct((2, frame, columns), jnp.bfloat16),
        ],
        scratch_shapes=[
            pltpu.VMEM((frame, width), jnp.bfloat16),
            pltpu.VMEM((frame, width), jnp.bfloat16),
            pltpu.VMEM((2 * tiles, width, TILE), jnp.bfloat16),
            pltpu.VMEM((tiles, width, TILE), jnp.bfloat16),
            pltpu.VMEM((columns, width), jnp.bfloat16),
            pltpu.VMEM((tiles, frame, TILE), jnp.bfloat16),
            pltpu.VMEM((columns // HEAD_DIM, frame, 2 * HEAD_DIM), jnp.bfloat16),
            pltpu.VMEM((tiles, count, TILE), jnp.bfloat16),
            pltpu.VMEM((count, width), jnp.bfloat16),
            pltpu.VMEM((count, width), jnp.float32),
            dma((frame // ROWS // 2,)), dma((2 * tiles,)), dma((tiles,)), dma, dma, dma, dma((2,)),
        ],
        compiler_params=limits(60),
        cost_estimate=pl.CostEstimate(
            flops=4 * frame * width * columns + 4 * count * width * columns + 8 * count * frame * columns,
            bytes_accessed=8 * width * columns, transcendentals=count * frame * columns // HEAD_DIM,
        ),
        name="space_first",
    )(tokens, action_pieces, pair_index, space_gain, time_gain, qkv, out)


def later_kernel(
    offset, tokens_hbm, rows_ref, pair_ref, time_gain_ref, qkv_hbm, out_hbm, normed_hbm, keyval_hbm,
    time_hbm, middle_hbm,
    tokens, normed, wq, wo, keys, values, attended, time, middle,
    token_sem, normed_sem, wq_sem, wo_sem, key_sem, value_sem, out_sem
):
    tiles = wq.shape[0]
    heads = TILE // HEAD_DIM
    count = tokens.shape[0]

    def cols(index):
        return pl.ds(pl.multiple_of(index * TILE, TILE), TILE)

    def wq_copy(index):
        return pltpu.make_async_copy(qkv_hbm.at[0, :, cols(index)], wq.at[index], wq_sem.at[index])

    def key_copy(index):
        return pltpu.make_async_copy(keyval_hbm.at[0, :, cols(index)], keys.at[index], key_sem.at[index])

    def value_copy(head):
        return pltpu.make_async_copy(
            keyval_hbm.at[1, :, pl.ds(pl.multiple_of(head * HEAD_DIM, HEAD_DIM), HEAD_DIM)],
            values.at[head, :, pl.ds(0, HEAD_DIM)], value_sem.at[head],
        )

    normed_copy = pltpu.make_async_copy(normed_hbm, normed, normed_sem)
    token_copy = pltpu.make_async_copy(tokens_hbm.at[pl.ds(offset, count), :], tokens, token_sem)
    out_copy = pltpu.make_async_copy(out_hbm, wo, wo_sem)
    def fetch(index):
        wq_copy(index).start()
        key_copy(index).start()
        for head in range(heads):
            value_copy(index * heads + head).start()

    normed_copy.start()
    fetch(0)
    fetch(1)
    values[:, :, HEAD_DIM:] = jnp.ones(values.shape[:2] + (HEAD_DIM,), jnp.bfloat16)
    normed_copy.wait()

    def ready(index):
        @pl.when(index + 2 < tiles)
        def _():
            fetch(index + 2)

        @pl.when(index + 2 == tiles)
        def _():
            token_copy.start()
            out_copy.start()

        key_copy(index).wait()
        for head in range(heads):
            value_copy(index * heads + head).wait()

    mix_frame(normed, wq, wq_copy, keys, values, ready, attended)
    token_copy.wait()
    out_copy.wait()
    leave_frame(
        tokens, own_row(rows_ref, pair_ref), time_gain_ref[...], attended, wo, time, middle, time_hbm, middle_hbm, out_sem
    )


def later(tokens, action_pieces, pair_index, time_gain, qkv, out, normed, keyval, offset):
    frame, width = tokens.shape
    count = normed.shape[0]
    columns = qkv.shape[2]
    tiles = columns // TILE
    dma = pltpu.SemaphoreType.DMA
    row = pl.BlockSpec((1, width), lambda: (0, 0))
    return pl.pallas_call(
        functools.partial(later_kernel, offset),
        in_specs=in_hbm(1) + row_specs(action_pieces) + [row] + in_hbm(4),
        out_specs=in_hbm(2),
        out_shape=[
            jax.ShapeDtypeStruct((count, width), jnp.bfloat16),
            jax.ShapeDtypeStruct((count, width), jnp.float32),
        ],
        scratch_shapes=[
            pltpu.VMEM((count, width), jnp.bfloat16),
            pltpu.VMEM((count, width), jnp.bfloat16),
            pltpu.VMEM((tiles, width, TILE), jnp.bfloat16),
            pltpu.VMEM((columns, width), jnp.bfloat16),
            pltpu.VMEM((tiles, frame, TILE), jnp.bfloat16),
            pltpu.VMEM((columns // HEAD_DIM, frame, 2 * HEAD_DIM), jnp.bfloat16),
            pltpu.VMEM((tiles, count, TILE), jnp.bfloat16),
            pltpu.VMEM((count, width), jnp.bfloat16),
            pltpu.VMEM((count, width), jnp.float32),
            dma, dma, dma((tiles,)), dma, dma((tiles,)), dma((columns // HEAD_DIM,)), dma((2,)),
        ],
        compiler_params=limits(60),
        cost_estimate=pl.CostEstimate(
            flops=4 * count * width * columns + 8 * count * frame * columns,
            bytes_accessed=4 * width * columns, transcendentals=count * frame * columns // HEAD_DIM,
        ),
        name="space_later",
    )(tokens, action_pieces, pair_index, time_gain, qkv, out, normed, keyval)


def time_kernel(
    places, received_hbm, bias_ref, qkv_hbm, mixed_hbm,
    received, weights, ordered, values, mixed, received_sem, weight_sem, mixed_sem
):
    frames, per_device, width = received.shape
    tiles = weights.shape[0]
    block = frames * places
    pieces = per_device // places

    def cols(index):
        return pl.ds(pl.multiple_of(index * TILE, TILE), TILE)

    def weight_copy(index, kind):
        return pltpu.make_async_copy(
            qkv_hbm.at[kind, :, cols(index)], weights.at[index, kind], weight_sem.at[index, kind]
        )

    received_copy = pltpu.make_async_copy(received_hbm, received, received_sem)
    received_copy.start()
    for place in range(AHEAD):
        weight_copy(place // 3, place % 3).start()
    values[:, :, HEAD_DIM:] = jnp.ones(values.shape[:2] + (HEAD_DIM,), jnp.bfloat16)
    received_copy.wait()
    for part in range(pieces):
        ordered[part * block:(part + 1) * block, :] = received[
            :, part * places:(part + 1) * places, :
        ].reshape(block, width)
    bias = bias_ref[...]

    def mixed_copy(index):
        return pltpu.make_async_copy(mixed.at[index], mixed_hbm.at[:, :, cols(index)], mixed_sem)

    def tile(index, carry):
        projected = []
        for kind in range(3):
            later = index + (kind + AHEAD) // 3
            pl.when(later < tiles)(lambda: weight_copy(later, (kind + AHEAD) % 3).start())
            weight_copy(index, kind).wait()
            value = project(ordered[...], weights[index, kind])
            if kind == 0:
                value = value * EXPONENT
            projected.append(value.astype(jnp.bfloat16))
        query, keys, value = projected
        heads = heads_of(TILE)
        for head, where in enumerate(heads):
            values[head, :, :HEAD_DIM] = value[:, where]
        for part in range(pieces):
            here = slice(part * block, (part + 1) * block)
            done = attend(
                [query[here, where] for where in heads],
                [keys[here, where] for where in heads],
                [values[head, here, :] for head in range(len(heads))],
                bias,
            )
            for where, value in zip(heads, done):
                mixed[index, :, part * places:(part + 1) * places, where] = value.reshape(
                    frames, places, HEAD_DIM
                )
        mixed_copy(index).start()
        return carry

    lax.fori_loop(0, tiles, tile, 0)
    for index in range(tiles):
        mixed_copy(index).wait()


def time_mix(received, bias, qkv, places):
    frames, per_device, width = received.shape
    columns = qkv.shape[2]
    rows = frames * per_device
    block = frames * places
    tiles = columns // TILE
    dma = pltpu.SemaphoreType.DMA
    return pl.pallas_call(
        functools.partial(time_kernel, places),
        in_specs=in_hbm(1) + [pl.BlockSpec((block, block), lambda: (0, 0))] + in_hbm(1),
        out_specs=in_hbm(1)[0],
        out_shape=jax.ShapeDtypeStruct((frames, per_device, columns), jnp.bfloat16),
        scratch_shapes=[
            pltpu.VMEM((frames, per_device, width), jnp.bfloat16),
            pltpu.VMEM((tiles, 3, width, TILE), jnp.bfloat16),
            pltpu.VMEM((rows, width), jnp.bfloat16),
            pltpu.VMEM((TILE // HEAD_DIM, rows, 2 * HEAD_DIM), jnp.bfloat16),
            pltpu.VMEM((tiles, frames, per_device, TILE), jnp.bfloat16),
            dma, dma((tiles, 3)), dma,
        ],
        compiler_params=limits(56),
        cost_estimate=pl.CostEstimate(
            flops=6 * rows * width * columns, bytes_accessed=6 * width * columns,
            transcendentals=rows * block * columns // HEAD_DIM,
        ),
        name="time_mix",
    )(received, bias, qkv)


def finish_kernel(offset, mixed_hbm, weight_hbm, middle_hbm, *rest):
    result_hbm, mixed, weights, middle, result, mixed_sem, weight_sem, middle_sem, result_sem = rest[-9:]
    rows, width = middle.shape
    tiles = weights.shape[0]
    mixed_copy = pltpu.make_async_copy(mixed_hbm, mixed, mixed_sem)
    middle_copy = pltpu.make_async_copy(middle_hbm, middle, middle_sem)

    def cols(index):
        return slice(index * TILE, (index + 1) * TILE)

    weight_copies = [
        pltpu.make_async_copy(weight_hbm.at[:, cols(index)], weights.at[index], weight_sem.at[index])
        for index in range(tiles)
    ]
    result_copies = [
        pltpu.make_async_copy(
            result.at[index], result_hbm.at[pl.ds(offset, rows), cols(index)], result_sem
        )
        for index in range(tiles)
    ]
    mixed_copy.start()
    for copy in weight_copies[:2]:
        copy.start()
    middle_copy.start()
    mixed_copy.wait()
    for index in range(tiles):
        if index + 2 < tiles:
            weight_copies[index + 2].start()
        weight_copies[index].wait()
        value = project(mixed[...], weights[index])
        if index == 0:
            middle_copy.wait()
        result[index] = (middle[:, cols(index)] + value).astype(jnp.bfloat16)
        result_copies[index].start()
    for copy in result_copies:
        copy.wait()


def finish(mixed, weights, middle, earlier, total, offset):
    rows, columns = mixed.shape
    width = weights.shape[1]
    extra = [] if earlier is None else [earlier]
    dma = pltpu.SemaphoreType.DMA
    return pl.pallas_call(
        functools.partial(finish_kernel, offset),
        in_specs=in_hbm(3 + len(extra)),
        out_specs=in_hbm(1)[0],
        out_shape=jax.ShapeDtypeStruct((total, width), jnp.bfloat16),
        scratch_shapes=[
            pltpu.VMEM((rows, columns), jnp.bfloat16),
            pltpu.VMEM((width // TILE, columns, TILE), jnp.bfloat16),
            pltpu.VMEM((rows, width), jnp.float32),
            pltpu.VMEM((width // TILE, rows, TILE), jnp.bfloat16),
            dma, dma((width // TILE,)), dma, dma,
        ],
        input_output_aliases={3: 0} if extra else {},
        compiler_params=limits(40),
        cost_estimate=pl.CostEstimate(
            flops=2 * rows * width * columns, bytes_accessed=2 * width * columns, transcendentals=0
        ),
        name="time_out",
    )(mixed, weights, middle, *extra)


def fold_projection(weights, row_count, segment):
    flat_rows = segment.reshape(row_count, segment.shape[-1])
    return jnp.einsum("rc,icj->irj", flat_rows, weights, preferred_element_type=jnp.float32)


def space_frame(triple):
    query, keys, values = triple
    tokens_frame, columns = query.shape
    query = query.reshape(tokens_frame, columns // HEAD_DIM, HEAD_DIM)
    keys = keys.reshape(tokens_frame, columns // HEAD_DIM, HEAD_DIM)
    values = values.reshape(tokens_frame, columns // HEAD_DIM, HEAD_DIM)
    scores = jnp.einsum(
        "qhd,khd->hqk", query, keys, preferred_element_type=jnp.float32
    ) * HEAD_DIM ** (-0.5)
    probabilities = jax.nn.softmax(scores, -1).astype(jnp.bfloat16)
    mixture = jnp.einsum(
        "hqk,khd->qhd", probabilities, values, preferred_element_type=jnp.float32
    ).astype(jnp.bfloat16)
    return mixture.reshape(tokens_frame, columns)


def body_split_features(
    tokens,
    action_rows,
    pair_index,
    episode_id,
    space_gain,
    space_qkv,
    space_out,
    time_gain,
    time_qkv,
    time_out,
):
    frames_here, per_frame, share_width = tokens.shape
    width = share_width * lax.axis_size("tensor")
    columns = space_qkv.shape[2]
    row_count = frames_here * per_frame
    offset = lax.axis_index("tensor") * share_width
    every_row = lax.all_gather(action_rows, "tm", axis=0, tiled=True)
    frame_count = every_row.shape[0]
    picker = (pair_index[:, None] == jnp.arange(frame_count, dtype=jnp.int32)[None, :]).astype(
        jnp.bfloat16
    )
    action = jnp.dot(picker, every_row, preferred_element_type=jnp.float32)
    start = tokens.astype(jnp.float32) + action[:, None, :]
    squares = lax.psum(jnp.sum(start * start, -1), "tensor")
    factor = lax.rsqrt(squares / width + EPSILON)[..., None]
    space_normed = (
        start * factor * lax.dynamic_slice_in_dim(space_gain, offset, share_width)
    ).astype(jnp.bfloat16)
    space_proj = fold_projection(
        space_qkv, row_count, lax.all_gather(space_normed, "tensor", axis=2, tiled=True)
    ).astype(jnp.bfloat16)
    space_proj = space_proj.reshape(3, frames_here, per_frame, columns)
    attended = lax.map(space_frame, (space_proj[0], space_proj[1], space_proj[2]))
    partial_space = jnp.dot(
        attended.reshape(row_count, columns), space_out, preferred_element_type=jnp.float32
    ).reshape(frames_here, per_frame, width)
    own_part = lax.dynamic_slice_in_dim(partial_space, offset, share_width, 2) + start
    term_full = lax.dynamic_update_slice_in_dim(partial_space, own_part, offset, 2)
    summed = lax.psum(term_full.astype(jnp.bfloat16), "tensor").astype(jnp.float32)
    full_squares = jnp.sum(summed * summed, -1)
    time_normed = (
        summed * lax.rsqrt(full_squares / width + EPSILON)[..., None] * time_gain
    ).astype(jnp.bfloat16)
    time_proj = jnp.einsum(
        "rc,icj->irj",
        time_normed.reshape(row_count, width),
        time_qkv,
        preferred_element_type=jnp.float32,
    ).astype(jnp.bfloat16)
    middle = lax.dynamic_slice_in_dim(summed, offset, share_width, 2)
    time_proj = time_proj.reshape(3, frames_here, per_frame, columns)
    moved = (
        lax.all_to_all(time_proj[0], "tm", split_axis=1, concat_axis=0, tiled=True),
        lax.all_to_all(time_proj[1], "tm", split_axis=1, concat_axis=0, tiled=True),
        lax.all_to_all(time_proj[2], "tm", split_axis=1, concat_axis=0, tiled=True),
    )
    query_time, keys_time, values_time = moved
    places = query_time.shape[1]
    heads_here = columns // HEAD_DIM
    query_time = query_time.reshape(frame_count, places, heads_here, HEAD_DIM)
    keys_time = keys_time.reshape(frame_count, places, heads_here, HEAD_DIM)
    values_time = values_time.reshape(frame_count, places, heads_here, HEAD_DIM)
    scores = jnp.einsum(
        "fphd,gphd->phfg", query_time, keys_time, preferred_element_type=jnp.float32
    ) * HEAD_DIM ** (-0.5)
    order = jnp.arange(frame_count, dtype=jnp.int32)
    allowed = (episode_id[:, None] == episode_id[None, :]) & (order[None, :] <= order[:, None])
    scores = jnp.where(allowed, scores, -1e30)
    probabilities = jax.nn.softmax(scores, -1).astype(jnp.bfloat16)
    mixture = jnp.einsum(
        "phfg,gphd->fphd", probabilities, values_time, preferred_element_type=jnp.float32
    ).astype(jnp.bfloat16)
    returned = lax.all_to_all(
        mixture.reshape(frame_count, places, columns), "tm", split_axis=0, concat_axis=1, tiled=True
    )
    partial_time = jnp.dot(
        returned.reshape(row_count, columns), time_out, preferred_element_type=jnp.float32
    ).reshape(frames_here, per_frame, width)
    return (
        middle
        + lax.psum_scatter(
            partial_time.astype(jnp.bfloat16), "tensor", scatter_dimension=2, tiled=True
        ).astype(jnp.float32)
    ).astype(jnp.bfloat16)


def exchange(parts, groups):
    return lax.all_to_all(parts, "tm", split_axis=0, concat_axis=0, axis_index_groups=groups)


def frame_bias(episodes, places):
    frames = jnp.repeat(jnp.arange(episodes.shape[0], dtype=jnp.int32), places)
    owners = jnp.repeat(episodes, places)
    spots = jnp.tile(jnp.arange(places, dtype=jnp.int32), episodes.shape[0])
    allowed = (
        (spots[:, None] == spots[None, :])
        & (owners[:, None] == owners[None, :])
        & (frames[None, :] <= frames[:, None])
    )
    return jnp.where(allowed, 0.0, -1e30).astype(jnp.float32)


def body_whole_features(
    sizes,
    tokens,
    action_rows,
    pair_index,
    episode_id,
    space_gain,
    space_qkv,
    space_out,
    time_gain,
    time_qkv,
    time_out,
):
    _, per_frame, width = tokens.shape
    columns = space_qkv.shape[2]
    frame_count = lax.axis_size("tm")
    tokens = tokens.reshape(per_frame, width)
    piece = width // 8
    action_pieces = exchange(
        jnp.broadcast_to(action_rows.reshape(1, 8, piece), (frame_count, 8, piece)), None
    )
    space_gain = space_gain.reshape(1, width)
    time_gain = time_gain.reshape(1, width)
    head, tail = sizes
    early_normed, early_middle, later_rows, keyval = first(
        tokens, action_pieces, pair_index, space_gain, time_gain, space_qkv, space_out, head
    )

    def over(group_size):
        groups = [
            list(range(first, first + group_size))
            for first in range(0, frame_count, group_size)
        ]
        if group_size == frame_count:
            groups = None

        def run(_):
            base = lax.axis_index("tm") // group_size * group_size
            episodes = lax.dynamic_slice_in_dim(episode_id, base, group_size)
            mixed = [exchange(early_normed.reshape(group_size, head // group_size, width), groups)]
            later_normed, later_middle = later(
                tokens, action_pieces, pair_index, time_gain, space_qkv, space_out, later_rows, keyval, head
            )
            mixed.append(exchange(later_normed.reshape(group_size, tail // group_size, width), groups))
            returned = []
            for size, part in zip(sizes, mixed):
                places = min(size // group_size, 16)
                bias = frame_bias(episodes, places)
                if places % 16:
                    part = part.reshape(size // 16, 16, width)
                    done = time_mix(part, bias, time_qkv, 16)
                else:
                    done = time_mix(part, bias, time_qkv, places)
                returned.append(exchange(done.reshape(group_size, size // group_size, columns), groups))
            result = None
            for size, at, part, middle in zip(sizes, (0, head), returned, (early_middle, later_middle)):
                result = finish(
                    part.reshape(size, columns), time_out, middle, result, per_frame, at
                )
            return result.reshape(1, per_frame, width)

        return run

    half = frame_count // 2
    apart = episode_id[half - 1] != episode_id[half]
    return lax.cond(apart, over(half), over(frame_count), 0)


def chunks(per_frame):
    return (per_frame // 3, per_frame - per_frame // 3)


def solution(mesh):
    sizes = dict(mesh.shape)

    def body(*arrays):
        frames_here, per_frame, width = arrays[0].shape
        pieces = chunks(per_frame)
        fits = (
            sizes["tensor"] == 1
            and frames_here == 1
            and sizes["tm"] % 2 == 0
            and all(piece % 256 == 0 and piece % sizes["tm"] == 0 for piece in pieces)
            and width % 512 == 0
            and arrays[5].shape[2] % 512 == 0
        )
        if fits:
            return body_whole_features(pieces, *arrays)
        return body_split_features(*arrays)

    return jax.shard_map(
        body,
        mesh=mesh,
        in_specs=(
            P("tm", None, "tensor"),
            P("tm", "tensor"),
            P("tm"),
            P(),
            P(),
            P(None, None, "tensor"),
            P("tensor", None),
            P(),
            P(None, None, "tensor"),
            P("tensor", None),
        ),
        out_specs=P("tm", None, "tensor"),
        check_vma=False,
    )
```

```python
import functools
import math
import jax
import jax.numpy as jnp
from jax import lax
from jax.experimental import pallas as pl
from jax.experimental.pallas import tpu as pltpu
from jax.sharding import PartitionSpec as P

HEAD_DIM = 128


EPSILON = 1e-06
MIB = 1 << 20
SCALE = HEAD_DIM ** (-0.5)
TILE = 512
ROWS = 128
AHEAD = 3
SLOTS = AHEAD + 1
LIMIT = 60
EXPONENT = SCALE / math.log(2.0)


def limits(mebibytes):
    return pltpu.CompilerParams(vmem_limit_bytes=mebibytes * MIB)


def in_hbm(count):
    return [pl.BlockSpec(memory_space=pl.ANY)] * count


def row_specs(pieces):
    return [
        pl.BlockSpec(pieces.shape, lambda: (0,) * pieces.ndim),
        pl.BlockSpec(memory_space=pltpu.SMEM),
    ]


def norm_rows(value, gain):
    squares = jnp.sum(value * value, -1, keepdims=True)
    factor = lax.rsqrt(squares / value.shape[1] + EPSILON)
    return (value * factor * gain).astype(jnp.bfloat16)


def attend(queries, keys, values, bias=None):
    scores = [
        lax.dot_general(query, key, (((1,), (1,)), ((), ())), preferred_element_type=jnp.float32)
        for query, key in zip(queries, keys)
    ]
    if bias is not None:
        scores = [score + bias for score in scores]
    weights = [
        jnp.exp2(score - jnp.max(score, -1, keepdims=True)).astype(jnp.bfloat16) for score in scores
    ]
    mixed = [
        jnp.dot(weight, value, preferred_element_type=jnp.float32)
        for weight, value in zip(weights, values)
    ]
    return [part[:, :HEAD_DIM] / part[:, HEAD_DIM:] for part in mixed]


def own_row(rows_ref, pair_ref):
    row = rows_ref[pair_ref[0]].astype(jnp.float32)
    return jnp.concatenate([row[piece:piece + 1, :] for piece in range(row.shape[0])], -1)


def project(rows, weight):
    return jnp.dot(rows, weight, preferred_element_type=jnp.float32)


def heads_of(width):
    return [slice(at, at + HEAD_DIM) for at in range(0, width, HEAD_DIM)]


def with_ones(value):
    return jnp.concatenate([value, jnp.ones(value.shape, value.dtype)], -1)


def tile_at(index):
    return pl.ds(pl.multiple_of(index * TILE, TILE), TILE)


def ring_of(width):
    return [pltpu.VMEM((SLOTS, width, TILE), jnp.bfloat16), pltpu.SemaphoreType.DMA((SLOTS,))]


def weight_stream(qkv_hbm, out_hbm, ring, sems, kinds):
    tiles = out_hbm.shape[1] // TILE

    def copy(source, place):
        slot = place % SLOTS
        return pltpu.make_async_copy(source, ring.at[slot], sems.at[slot])

    def fetch(place):
        for order, kind in enumerate(kinds):
            pl.when(place // tiles == order)(
                lambda: copy(qkv_hbm.at[kind, :, tile_at(place % tiles)], place).start()
            )
        pl.when(place // tiles == len(kinds))(
            lambda: copy(out_hbm.at[:, tile_at(place % tiles)], place).start()
        )

    def take(place):
        fetch(place + AHEAD)
        copy(out_hbm.at[:, tile_at(0)], place).wait()
        return ring.at[place % SLOTS]

    return fetch, take


def mix_frame(rows_ref, take, base, tiles, keys_ref, values_ref, ready, attended_ref):
    heads = heads_of(TILE)

    def tile(index, carry):
        ready(index)
        weight = take(base + index)
        query = (project(rows_ref[...], weight[...]) * EXPONENT).astype(jnp.bfloat16)
        done = attend(
            [query[:, cols] for cols in heads],
            [keys_ref[index, :, cols] for cols in heads],
            [with_ones(values_ref[index, :, cols]) for cols in heads],
        )
        attended_ref[:, tile_at(index)] = jnp.concatenate(done, -1).astype(jnp.bfloat16)
        return carry

    lax.fori_loop(0, tiles, tile, 0)


def leave_frame(
    tokens_ref, action_ref, gain_ref, attended_ref, take, base, tiles,
    time_ref, middle_ref, squares_ref, time_hbm, middle_hbm, sems
):
    width = middle_ref.shape[1]
    squares_ref[...] = jnp.zeros_like(squares_ref)

    def middle_copy(index):
        return pltpu.make_async_copy(
            middle_ref.at[:, tile_at(index)], middle_hbm.at[:, tile_at(index)], sems.at[1]
        )

    def tile(index, carry):
        weight = take(base + index)
        cols = tile_at(index)
        start = tokens_ref[:, cols].astype(jnp.float32) + action_ref[:, cols]
        middle = start + project(attended_ref[...], weight[...])
        middle_ref[:, cols] = middle
        squares_ref[...] += jnp.sum(middle * middle, -1, keepdims=True)
        middle_copy(index).start()
        return carry

    lax.fori_loop(0, tiles, tile, 0)
    blocks = time_ref.shape[0] // ROWS

    def time_copy(index):
        here = pl.ds(pl.multiple_of(index * ROWS, ROWS), ROWS)
        return pltpu.make_async_copy(time_ref.at[here, :], time_hbm.at[here, :], sems.at[0])

    def block(index, carry):
        here = pl.ds(pl.multiple_of(index * ROWS, ROWS), ROWS)
        factor = lax.rsqrt(squares_ref[here, :] / width + EPSILON)
        time_ref[here, :] = (middle_ref[here, :] * factor * gain_ref[...]).astype(jnp.bfloat16)
        time_copy(index).start()
        return carry

    lax.fori_loop(0, blocks, block, 0)
    for index in range(tiles):
        middle_copy(index).wait()
    for index in range(blocks):
        time_copy(index).wait()


def first_kernel(
    count, tokens_hbm, rows_ref, pair_ref, space_gain_ref, time_gain_ref, qkv_hbm, out_hbm,
    time_hbm, middle_hbm, normed_hbm, keyval_hbm,
    tokens, normed, ring, ring_sem, keyval, attended, time, middle, squares, action_ref,
    token_sem, keyval_sem, normed_sem, out_sem
):
    tiles = keyval.shape[1]
    blocks = tokens.shape[0] // ROWS
    fetch, take = weight_stream(qkv_hbm, out_hbm, ring, ring_sem, (1, 2, 0))

    def token_rows(index):
        return pl.ds(pl.multiple_of(index * ROWS, ROWS), ROWS)

    def token_copy(index):
        here = token_rows(index)
        return pltpu.make_async_copy(tokens_hbm.at[here, :], tokens.at[here, :], token_sem.at[index])

    def keyval_copy(kind, index):
        return pltpu.make_async_copy(
            keyval.at[kind, index], keyval_hbm.at[kind, :, tile_at(index)], keyval_sem
        )

    rest = pltpu.make_async_copy(normed.at[pl.ds(count, tokens.shape[0] - count), :], normed_hbm, normed_sem)
    for index in range(blocks):
        token_copy(index).start()
    fetch(0)
    action_ref[...] = own_row(rows_ref, pair_ref)

    def norm_block(index, carry):
        token_copy(index).wait()
        here = token_rows(index)
        normed[here, :] = norm_rows(
            tokens[here, :].astype(jnp.float32) + action_ref[...], space_gain_ref[...]
        )
        return carry

    norm_block(0, 0)
    for place in range(1, AHEAD):
        fetch(place)
    lax.fori_loop(1, blocks, norm_block, 0)
    rest.start()

    def keyval_tile(place, carry):
        kind, index = place // tiles, place % tiles
        weight = take(place)
        keyval[kind, index] = project(normed[...], weight[...]).astype(jnp.bfloat16)
        keyval_copy(kind, index).start()
        return carry

    lax.fori_loop(0, 2 * tiles, keyval_tile, 0)
    mix_frame(
        normed.at[pl.ds(0, count), :], take, 2 * tiles, tiles, keyval.at[0], keyval.at[1],
        lambda index: None, attended,
    )
    leave_frame(
        tokens.at[pl.ds(0, count), :], action_ref, time_gain_ref, attended, take, 3 * tiles, tiles,
        time, middle, squares, time_hbm, middle_hbm, out_sem,
    )
    rest.wait()
    for kind in range(2):
        for index in range(tiles):
            keyval_copy(kind, index).wait()


def first(tokens, action_pieces, pair_index, space_gain, time_gain, qkv, out, count):
    frame, width = tokens.shape
    columns = qkv.shape[2]
    tiles = columns // TILE
    dma = pltpu.SemaphoreType.DMA
    row = pl.BlockSpec((1, width), lambda: (0, 0))
    return pl.pallas_call(
        functools.partial(first_kernel, count),
        in_specs=in_hbm(1) + row_specs(action_pieces) + [row] * 2 + in_hbm(2),
        out_specs=in_hbm(4),
        out_shape=[
            jax.ShapeDtypeStruct((count, width), jnp.bfloat16),
            jax.ShapeDtypeStruct((count, width), jnp.float32),
            jax.ShapeDtypeStruct((frame - count, width), jnp.bfloat16),
            jax.ShapeDtypeStruct((2, frame, columns), jnp.bfloat16),
        ],
        scratch_shapes=[
            pltpu.VMEM((frame, width), jnp.bfloat16),
            pltpu.VMEM((frame, width), jnp.bfloat16),
            *ring_of(width),
            pltpu.VMEM((2, tiles, frame, TILE), jnp.bfloat16),
            pltpu.VMEM((count, columns), jnp.bfloat16),
            pltpu.VMEM((count, width), jnp.bfloat16),
            pltpu.VMEM((count, width), jnp.float32),
            pltpu.VMEM((count, 1), jnp.float32),
            pltpu.VMEM((1, width), jnp.float32),
            dma((frame // ROWS,)), dma, dma, dma((2,)),
        ],
        compiler_params=limits(LIMIT),
        cost_estimate=pl.CostEstimate(
            flops=4 * frame * width * columns + 4 * count * width * columns + 8 * count * frame * columns,
            bytes_accessed=8 * width * columns, transcendentals=count * frame * columns // HEAD_DIM,
        ),
        name="space_first",
    )(tokens, action_pieces, pair_index, space_gain, time_gain, qkv, out)


def later_kernel(
    offset, tokens_hbm, rows_ref, pair_ref, time_gain_ref, qkv_hbm, out_hbm, normed_hbm, keyval_hbm,
    time_hbm, middle_hbm,
    tokens, normed, ring, ring_sem, keyval, attended, time, middle, squares, action_ref,
    token_sem, normed_sem, keyval_sem, out_sem
):
    tiles = keyval.shape[1]
    count = tokens.shape[0]
    fetch, take = weight_stream(qkv_hbm, out_hbm, ring, ring_sem, (0,))

    def keyval_copy(kind, index):
        return pltpu.make_async_copy(
            keyval_hbm.at[kind, :, tile_at(index)], keyval.at[kind, index], keyval_sem.at[kind, index]
        )

    normed_copy = pltpu.make_async_copy(normed_hbm, normed, normed_sem)
    token_copy = pltpu.make_async_copy(tokens_hbm.at[pl.ds(offset, count), :], tokens, token_sem)
    normed_copy.start()
    for place in range(AHEAD):
        fetch(place)
        for kind in range(2):
            keyval_copy(kind, place).start()
    action_ref[...] = own_row(rows_ref, pair_ref)
    normed_copy.wait()

    def ready(index):
        @pl.when(index + AHEAD < tiles)
        def _():
            for kind in range(2):
                keyval_copy(kind, index + AHEAD).start()

        pl.when(index == tiles - 1)(lambda: token_copy.start())
        for kind in range(2):
            keyval_copy(kind, index).wait()

    mix_frame(normed, take, 0, tiles, keyval.at[0], keyval.at[1], ready, attended)
    token_copy.wait()
    leave_frame(
        tokens, action_ref, time_gain_ref, attended, take, tiles, tiles,
        time, middle, squares, time_hbm, middle_hbm, out_sem,
    )


def later(tokens, action_pieces, pair_index, time_gain, qkv, out, normed, keyval, offset):
    frame, width = tokens.shape
    count = normed.shape[0]
    columns = qkv.shape[2]
    tiles = columns // TILE
    dma = pltpu.SemaphoreType.DMA
    row = pl.BlockSpec((1, width), lambda: (0, 0))
    return pl.pallas_call(
        functools.partial(later_kernel, offset),
        in_specs=in_hbm(1) + row_specs(action_pieces) + [row] + in_hbm(4),
        out_specs=in_hbm(2),
        out_shape=[
            jax.ShapeDtypeStruct((count, width), jnp.bfloat16),
            jax.ShapeDtypeStruct((count, width), jnp.float32),
        ],
        scratch_shapes=[
            pltpu.VMEM((count, width), jnp.bfloat16),
            pltpu.VMEM((count, width), jnp.bfloat16),
            *ring_of(width),
            pltpu.VMEM((2, tiles, frame, TILE), jnp.bfloat16),
            pltpu.VMEM((count, columns), jnp.bfloat16),
            pltpu.VMEM((count, width), jnp.bfloat16),
            pltpu.VMEM((count, width), jnp.float32),
            pltpu.VMEM((count, 1), jnp.float32),
            pltpu.VMEM((1, width), jnp.float32),
            dma, dma, dma((2, tiles)), dma((2,)),
        ],
        compiler_params=limits(LIMIT),
        cost_estimate=pl.CostEstimate(
            flops=4 * count * width * columns + 8 * count * frame * columns,
            bytes_accessed=4 * width * columns, transcendentals=count * frame * columns // HEAD_DIM,
        ),
        name="space_later",
    )(tokens, action_pieces, pair_index, time_gain, qkv, out, normed, keyval)


def time_kernel(
    places, received_hbm, bias_ref, qkv_hbm, mixed_hbm,
    received, mixed, weights, received_sem, mixed_sem, weight_sem
):
    frames, per_device, width = received.shape
    tiles = mixed.shape[0]
    pieces = per_device // places
    heads = heads_of(TILE)
    received_copy = pltpu.make_async_copy(received_hbm, received, received_sem)

    def weight_copies(index):
        return [
            pltpu.make_async_copy(
                qkv_hbm.at[kind, :, tile_at(index)], weights.at[index, kind], weight_sem.at[index, kind]
            )
            for kind in range(3)
        ]

    def mixed_copy(index):
        return pltpu.make_async_copy(mixed.at[index], mixed_hbm.at[:, :, tile_at(index)], mixed_sem)

    def split(value):
        value = value.reshape(frames, per_device, TILE)
        return [
            value[:, part * places:(part + 1) * places, :]
            .reshape(frames * places, TILE).astype(jnp.bfloat16)
            for part in range(pieces)
        ]

    def tile(index, carry):
        @pl.when(index + 2 < tiles)
        def _():
            for copy in weight_copies(index + 2):
                copy.start()

        for copy in weight_copies(index):
            copy.wait()
        rows = received[...].reshape(frames * per_device, width)
        query = split(project(rows, weights[index, 0]) * EXPONENT)
        keys = split(project(rows, weights[index, 1]))
        value = split(project(rows, weights[index, 2]))
        parts = []
        for part in range(pieces):
            done = attend(
                [query[part][:, cols] for cols in heads],
                [keys[part][:, cols] for cols in heads],
                [with_ones(value[part][:, cols]) for cols in heads],
                bias_ref[...],
            )
            parts.append(jnp.concatenate(done, -1).reshape(frames, places, TILE))
        mixed[index] = jnp.concatenate(parts, 1).astype(jnp.bfloat16)
        mixed_copy(index).start()
        return carry

    received_copy.start()
    for copy in weight_copies(0):
        copy.start()
    received_copy.wait()
    for copy in weight_copies(1):
        copy.start()
    lax.fori_loop(0, tiles, tile, 0)
    for index in range(tiles):
        mixed_copy(index).wait()


def time_mix(received, bias, qkv, places):
    frames, per_device, width = received.shape
    columns = qkv.shape[2]
    rows = frames * per_device
    block = frames * places
    tiles = columns // TILE
    dma = pltpu.SemaphoreType.DMA
    return pl.pallas_call(
        functools.partial(time_kernel, places),
        in_specs=in_hbm(1) + [pl.BlockSpec(memory_space=pltpu.VMEM)] + in_hbm(1),
        out_specs=in_hbm(1)[0],
        out_shape=jax.ShapeDtypeStruct((frames, per_device, columns), jnp.bfloat16),
        scratch_shapes=[
            pltpu.VMEM((frames, per_device, width), jnp.bfloat16),
            pltpu.VMEM((tiles, frames, per_device, TILE), jnp.bfloat16),
            pltpu.VMEM((tiles, 3, width, TILE), jnp.bfloat16),
            dma, dma, dma((tiles, 3)),
        ],
        compiler_params=limits(LIMIT),
        cost_estimate=pl.CostEstimate(
            flops=6 * rows * width * columns, bytes_accessed=6 * width * columns,
            transcendentals=rows * block * columns // HEAD_DIM,
        ),
        name="time_mix",
    )(received, bias, qkv)


def finish_kernel(offset, mixed_hbm, weight_hbm, middle_hbm, *rest):
    result_hbm, mixed, middle, result, mixed_sem, middle_sem, result_sem, ring, ring_sem = rest[-9:]
    rows, width = middle.shape
    tiles = result.shape[0]
    mixed_copy = pltpu.make_async_copy(mixed_hbm, mixed, mixed_sem)
    middle_copy = pltpu.make_async_copy(middle_hbm, middle, middle_sem)

    def result_copy(index):
        return pltpu.make_async_copy(
            result.at[index], result_hbm.at[pl.ds(offset, rows), tile_at(index)], result_sem
        )

    def weight_copy(index):
        return pltpu.make_async_copy(
            weight_hbm.at[:, tile_at(index)], ring.at[index], ring_sem.at[index]
        )

    mixed_copy.start()
    weight_copy(0).start()
    weight_copy(1).start()
    middle_copy.start()
    mixed_copy.wait()

    def tile(index, carry):
        pl.when(index + 2 < tiles)(lambda: weight_copy(index + 2).start())
        weight_copy(index).wait()
        value = project(mixed[...], ring[index])
        pl.when(index == 0)(lambda: middle_copy.wait())
        result[index] = (middle[:, tile_at(index)] + value).astype(jnp.bfloat16)
        result_copy(index).start()
        return carry

    lax.fori_loop(0, tiles, tile, 0)
    for index in range(tiles):
        result_copy(index).wait()


def finish(mixed, weights, middle, earlier, total, offset):
    rows, columns = mixed.shape
    width = weights.shape[1]
    extra = [] if earlier is None else [earlier]
    dma = pltpu.SemaphoreType.DMA
    return pl.pallas_call(
        functools.partial(finish_kernel, offset),
        in_specs=in_hbm(3 + len(extra)),
        out_specs=in_hbm(1)[0],
        out_shape=jax.ShapeDtypeStruct((total, width), jnp.bfloat16),
        scratch_shapes=[
            pltpu.VMEM((rows, columns), jnp.bfloat16),
            pltpu.VMEM((rows, width), jnp.float32),
            pltpu.VMEM((width // TILE, rows, TILE), jnp.bfloat16),
            dma, dma, dma,
            pltpu.VMEM((width // TILE, columns, TILE), jnp.bfloat16), dma((width // TILE,)),
        ],
        input_output_aliases={3: 0} if extra else {},
        compiler_params=limits(LIMIT),
        cost_estimate=pl.CostEstimate(
            flops=2 * rows * width * columns, bytes_accessed=8 * rows * width, transcendentals=0
        ),
        name="time_out",
    )(mixed, weights, middle, *extra)


def fold_projection(weights, row_count, segment):
    flat_rows = segment.reshape(row_count, segment.shape[-1])
    return jnp.einsum("rc,icj->irj", flat_rows, weights, preferred_element_type=jnp.float32)


def space_frame(triple):
    query, keys, values = triple
    tokens_frame, columns = query.shape
    query = query.reshape(tokens_frame, columns // HEAD_DIM, HEAD_DIM)
    keys = keys.reshape(tokens_frame, columns // HEAD_DIM, HEAD_DIM)
    values = values.reshape(tokens_frame, columns // HEAD_DIM, HEAD_DIM)
    scores = jnp.einsum(
        "qhd,khd->hqk", query, keys, preferred_element_type=jnp.float32
    ) * HEAD_DIM ** (-0.5)
    probabilities = jax.nn.softmax(scores, -1).astype(jnp.bfloat16)
    mixture = jnp.einsum(
        "hqk,khd->qhd", probabilities, values, preferred_element_type=jnp.float32
    ).astype(jnp.bfloat16)
    return mixture.reshape(tokens_frame, columns)


def body_split_features(
    tokens,
    action_rows,
    pair_index,
    episode_id,
    space_gain,
    space_qkv,
    space_out,
    time_gain,
    time_qkv,
    time_out,
):
    frames_here, per_frame, share_width = tokens.shape
    width = share_width * lax.axis_size("tensor")
    columns = space_qkv.shape[2]
    row_count = frames_here * per_frame
    offset = lax.axis_index("tensor") * share_width
    every_row = lax.all_gather(action_rows, "tm", axis=0, tiled=True)
    frame_count = every_row.shape[0]
    picker = (pair_index[:, None] == jnp.arange(frame_count, dtype=jnp.int32)[None, :]).astype(
        jnp.bfloat16
    )
    action = jnp.dot(picker, every_row, preferred_element_type=jnp.float32)
    start = tokens.astype(jnp.float32) + action[:, None, :]
    squares = lax.psum(jnp.sum(start * start, -1), "tensor")
    factor = lax.rsqrt(squares / width + EPSILON)[..., None]
    space_normed = (
        start * factor * lax.dynamic_slice_in_dim(space_gain, offset, share_width)
    ).astype(jnp.bfloat16)
    space_proj = fold_projection(
        space_qkv, row_count, lax.all_gather(space_normed, "tensor", axis=2, tiled=True)
    ).astype(jnp.bfloat16)
    space_proj = space_proj.reshape(3, frames_here, per_frame, columns)
    attended = lax.map(space_frame, (space_proj[0], space_proj[1], space_proj[2]))
    partial_space = jnp.dot(
        attended.reshape(row_count, columns), space_out, preferred_element_type=jnp.float32
    ).reshape(frames_here, per_frame, width)
    own_part = lax.dynamic_slice_in_dim(partial_space, offset, share_width, 2) + start
    term_full = lax.dynamic_update_slice_in_dim(partial_space, own_part, offset, 2)
    summed = lax.psum(term_full.astype(jnp.bfloat16), "tensor").astype(jnp.float32)
    full_squares = jnp.sum(summed * summed, -1)
    time_normed = (
        summed * lax.rsqrt(full_squares / width + EPSILON)[..., None] * time_gain
    ).astype(jnp.bfloat16)
    time_proj = jnp.einsum(
        "rc,icj->irj",
        time_normed.reshape(row_count, width),
        time_qkv,
        preferred_element_type=jnp.float32,
    ).astype(jnp.bfloat16)
    middle = lax.dynamic_slice_in_dim(summed, offset, share_width, 2)
    time_proj = time_proj.reshape(3, frames_here, per_frame, columns)
    moved = (
        lax.all_to_all(time_proj[0], "tm", split_axis=1, concat_axis=0, tiled=True),
        lax.all_to_all(time_proj[1], "tm", split_axis=1, concat_axis=0, tiled=True),
        lax.all_to_all(time_proj[2], "tm", split_axis=1, concat_axis=0, tiled=True),
    )
    query_time, keys_time, values_time = moved
    places = query_time.shape[1]
    heads_here = columns // HEAD_DIM
    query_time = query_time.reshape(frame_count, places, heads_here, HEAD_DIM)
    keys_time = keys_time.reshape(frame_count, places, heads_here, HEAD_DIM)
    values_time = values_time.reshape(frame_count, places, heads_here, HEAD_DIM)
    scores = jnp.einsum(
        "fphd,gphd->phfg", query_time, keys_time, preferred_element_type=jnp.float32
    ) * HEAD_DIM ** (-0.5)
    order = jnp.arange(frame_count, dtype=jnp.int32)
    allowed = (episode_id[:, None] == episode_id[None, :]) & (order[None, :] <= order[:, None])
    scores = jnp.where(allowed, scores, -1e30)
    probabilities = jax.nn.softmax(scores, -1).astype(jnp.bfloat16)
    mixture = jnp.einsum(
        "phfg,gphd->fphd", probabilities, values_time, preferred_element_type=jnp.float32
    ).astype(jnp.bfloat16)
    returned = lax.all_to_all(
        mixture.reshape(frame_count, places, columns), "tm", split_axis=0, concat_axis=1, tiled=True
    )
    partial_time = jnp.dot(
        returned.reshape(row_count, columns), time_out, preferred_element_type=jnp.float32
    ).reshape(frames_here, per_frame, width)
    return (
        middle
        + lax.psum_scatter(
            partial_time.astype(jnp.bfloat16), "tensor", scatter_dimension=2, tiled=True
        ).astype(jnp.float32)
    ).astype(jnp.bfloat16)


def exchange(parts, groups):
    return lax.all_to_all(parts, "tm", split_axis=0, concat_axis=0, axis_index_groups=groups)


def frame_bias(episodes, places):
    frames = jnp.repeat(jnp.arange(episodes.shape[0], dtype=jnp.int32), places)
    owners = jnp.repeat(episodes, places)
    spots = jnp.tile(jnp.arange(places, dtype=jnp.int32), episodes.shape[0])
    allowed = (
        (spots[:, None] == spots[None, :])
        & (owners[:, None] == owners[None, :])
        & (frames[None, :] <= frames[:, None])
    )
    return jnp.where(allowed, 0.0, -1e30).astype(jnp.float32)


def body_whole_features(
    sizes,
    tokens,
    action_rows,
    pair_index,
    episode_id,
    space_gain,
    space_qkv,
    space_out,
    time_gain,
    time_qkv,
    time_out,
):
    _, per_frame, width = tokens.shape
    columns = space_qkv.shape[2]
    frame_count = lax.axis_size("tm")
    tokens = tokens.reshape(per_frame, width)
    piece = width // 8
    action_pieces = exchange(
        jnp.broadcast_to(action_rows.reshape(1, 8, piece), (frame_count, 8, piece)), None
    )
    space_gain = space_gain.reshape(1, width)
    time_gain = time_gain.reshape(1, width)
    head, tail = sizes
    early_normed, early_middle, later_rows, keyval = first(
        tokens, action_pieces, pair_index, space_gain, time_gain, space_qkv, space_out, head
    )

    def over(group_size):
        groups = [
            list(range(first, first + group_size))
            for first in range(0, frame_count, group_size)
        ]
        if group_size == frame_count:
            groups = None

        def run(_):
            base = lax.axis_index("tm") // group_size * group_size
            episodes = lax.dynamic_slice_in_dim(episode_id, base, group_size)
            mixed = [exchange(early_normed.reshape(group_size, head // group_size, width), groups)]
            later_normed, later_middle = later(
                tokens, action_pieces, pair_index, time_gain, space_qkv, space_out, later_rows, keyval, head
            )
            mixed.append(exchange(later_normed.reshape(group_size, tail // group_size, width), groups))
            returned = []
            for size, part in zip(sizes, mixed):
                places = size // group_size
                if places >= 16:
                    places = 256 // group_size
                    bias = frame_bias(episodes, places)
                    done = time_mix(part, bias, time_qkv, places)
                else:
                    bias = frame_bias(episodes, places)
                    done = time_mix(part.reshape(size // 16, 16, width), bias, time_qkv, 16)
                returned.append(exchange(done.reshape(group_size, size // group_size, columns), groups))
            result = None
            for size, at, part, middle in zip(sizes, (0, head), returned, (early_middle, later_middle)):
                result = finish(
                    part.reshape(size, columns), time_out, middle, result, per_frame, at
                )
            return result.reshape(1, per_frame, width)

        return run

    half = frame_count // 2
    apart = episode_id[half - 1] != episode_id[half]
    return lax.cond(apart, over(half), over(frame_count), 0)


def chunks(per_frame):
    return (per_frame // 3, per_frame - per_frame // 3)


def solution(mesh):
    sizes = dict(mesh.shape)

    def body(*arrays):
        frames_here, per_frame, width = arrays[0].shape
        pieces = chunks(per_frame)
        fits = (
            sizes["tensor"] == 1
            and frames_here == 1
            and sizes["tm"] % 2 == 0
            and all(piece % 256 == 0 and piece % sizes["tm"] == 0 for piece in pieces)
            and width % 512 == 0
            and arrays[5].shape[2] % 512 == 0
        )
        if fits:
            return body_whole_features(pieces, *arrays)
        return body_split_features(*arrays)

    return jax.shard_map(
        body,
        mesh=mesh,
        in_specs=(
            P("tm", None, "tensor"),
            P("tm", "tensor"),
            P("tm"),
            P(),
            P(),
            P(None, None, "tensor"),
            P("tensor", None),
            P(),
            P(None, None, "tensor"),
            P("tensor", None),
        ),
        out_specs=P("tm", None, "tensor"),
        check_vma=False,
    )
```

```python
import functools
import math
import jax
import jax.numpy as jnp
from jax import lax
from jax.experimental import pallas as pl
from jax.experimental.pallas import tpu as pltpu
from jax.sharding import PartitionSpec as P

HEAD_DIM = 128


EPSILON = 1e-06
MIB = 1 << 20
SCALE = HEAD_DIM ** (-0.5)
TILE = 512
ROWS = 128
AHEAD = 3
SLOTS = AHEAD + 1
LIMIT = 60
EXPONENT = SCALE / math.log(2.0)


def limits(mebibytes):
    return pltpu.CompilerParams(vmem_limit_bytes=mebibytes * MIB)


def in_hbm(count):
    return [pl.BlockSpec(memory_space=pl.ANY)] * count


def row_specs(pieces):
    return [
        pl.BlockSpec(pieces.shape, lambda: (0,) * pieces.ndim),
        pl.BlockSpec(memory_space=pltpu.SMEM),
    ]


def norm_rows(value, gain):
    squares = jnp.sum(value * value, -1, keepdims=True)
    factor = lax.rsqrt(squares / value.shape[1] + EPSILON)
    return (value * factor * gain).astype(jnp.bfloat16)


def attend(queries, keys, values, bias=None):
    scores = [
        lax.dot_general(query, key, (((1,), (1,)), ((), ())), preferred_element_type=jnp.float32)
        for query, key in zip(queries, keys)
    ]
    if bias is not None:
        scores = [score + bias for score in scores]
    weights = [
        jnp.exp2(score - jnp.max(score, -1, keepdims=True)).astype(jnp.bfloat16) for score in scores
    ]
    mixed = [
        jnp.dot(weight, value, preferred_element_type=jnp.float32)
        for weight, value in zip(weights, values)
    ]
    return [part[:, :HEAD_DIM] / part[:, HEAD_DIM:] for part in mixed]


def own_row(rows_ref, pair_ref):
    row = rows_ref[pair_ref[0]].astype(jnp.float32)
    return jnp.concatenate([row[piece:piece + 1, :] for piece in range(row.shape[0])], -1)


def project(rows, weight):
    return jnp.dot(rows, weight, preferred_element_type=jnp.float32)


def heads_of(width):
    return [slice(at, at + HEAD_DIM) for at in range(0, width, HEAD_DIM)]


def with_ones(value):
    return jnp.concatenate([value, jnp.ones(value.shape, value.dtype)], -1)


def tile_at(index):
    return pl.ds(pl.multiple_of(index * TILE, TILE), TILE)


def ring_of(width):
    return [pltpu.VMEM((SLOTS, width, TILE), jnp.bfloat16), pltpu.SemaphoreType.DMA((SLOTS,))]


def weight_stream(qkv_hbm, out_hbm, ring, sems, kinds):
    tiles = out_hbm.shape[1] // TILE

    def copy(source, place):
        slot = place % SLOTS
        return pltpu.make_async_copy(source, ring.at[slot], sems.at[slot])

    def fetch(place):
        for order, kind in enumerate(kinds):
            pl.when(place // tiles == order)(
                lambda: copy(qkv_hbm.at[kind, :, tile_at(place % tiles)], place).start()
            )
        pl.when(place // tiles == len(kinds))(
            lambda: copy(out_hbm.at[:, tile_at(place % tiles)], place).start()
        )

    def take(place):
        fetch(place + AHEAD)
        copy(out_hbm.at[:, tile_at(0)], place).wait()
        return ring.at[place % SLOTS]

    return fetch, take


def mix_frame(rows_ref, take, base, tiles, keys_ref, values_ref, ready, attended_ref):
    heads = heads_of(TILE)

    def tile(index, carry):
        ready(index)
        weight = take(base + index)
        query = (project(rows_ref[...], weight[...]) * EXPONENT).astype(jnp.bfloat16)
        done = attend(
            [query[:, cols] for cols in heads],
            [keys_ref[index, :, cols] for cols in heads],
            [with_ones(values_ref[index, :, cols]) for cols in heads],
        )
        attended_ref[:, tile_at(index)] = jnp.concatenate(done, -1).astype(jnp.bfloat16)
        return carry

    lax.fori_loop(0, tiles, tile, 0)


def leave_frame(
    tokens_ref, action_ref, gain_ref, attended_ref, take, base, tiles,
    time_ref, middle_ref, rounded_ref, squares_ref, time_hbm, middle_hbm, sems
):
    width = middle_ref.shape[1]
    squares_ref[...] = jnp.zeros_like(squares_ref)

    def middle_copy(index):
        return pltpu.make_async_copy(
            rounded_ref.at[:, tile_at(index)], middle_hbm.at[:, tile_at(index)], sems.at[1]
        )

    def tile(index, carry):
        weight = take(base + index)
        cols = tile_at(index)
        start = tokens_ref[:, cols].astype(jnp.float32) + action_ref[:, cols]
        middle = start + project(attended_ref[...], weight[...])
        middle_ref[:, cols] = middle
        rounded_ref[:, cols] = middle.astype(jnp.bfloat16)
        squares_ref[...] += jnp.sum(middle * middle, -1, keepdims=True)
        middle_copy(index).start()
        return carry

    lax.fori_loop(0, tiles, tile, 0)
    blocks = time_ref.shape[0] // ROWS

    def time_copy(index):
        here = pl.ds(pl.multiple_of(index * ROWS, ROWS), ROWS)
        return pltpu.make_async_copy(time_ref.at[here, :], time_hbm.at[here, :], sems.at[0])

    def block(index, carry):
        here = pl.ds(pl.multiple_of(index * ROWS, ROWS), ROWS)
        factor = lax.rsqrt(squares_ref[here, :] / width + EPSILON)
        time_ref[here, :] = (middle_ref[here, :] * factor * gain_ref[...]).astype(jnp.bfloat16)
        time_copy(index).start()
        return carry

    lax.fori_loop(0, blocks, block, 0)
    for index in range(tiles):
        middle_copy(index).wait()
    for index in range(blocks):
        time_copy(index).wait()


def first_kernel(
    count, tokens_hbm, rows_ref, pair_ref, space_gain_ref, time_gain_ref, qkv_hbm, out_hbm,
    time_hbm, middle_hbm, normed_hbm, keyval_hbm,
    tokens, normed, ring, ring_sem, keyval, attended, time, middle, rounded, squares, action_ref,
    token_sem, keyval_sem, normed_sem, out_sem
):
    tiles = keyval.shape[1]
    blocks = tokens.shape[0] // ROWS
    fetch, take = weight_stream(qkv_hbm, out_hbm, ring, ring_sem, (1, 2, 0))

    def token_rows(index):
        return pl.ds(pl.multiple_of(index * ROWS, ROWS), ROWS)

    def token_copy(index):
        here = token_rows(index)
        return pltpu.make_async_copy(tokens_hbm.at[here, :], tokens.at[here, :], token_sem.at[index])

    def keyval_copy(kind, index):
        return pltpu.make_async_copy(
            keyval.at[kind, index], keyval_hbm.at[kind, :, tile_at(index)], keyval_sem
        )

    rest = pltpu.make_async_copy(normed.at[pl.ds(count, tokens.shape[0] - count), :], normed_hbm, normed_sem)
    for index in range(blocks):
        token_copy(index).start()
    action_ref[...] = own_row(rows_ref, pair_ref)

    def norm_block(index, carry):
        token_copy(index).wait()
        here = token_rows(index)
        normed[here, :] = norm_rows(
            tokens[here, :].astype(jnp.float32) + action_ref[...], space_gain_ref[...]
        )
        return carry

    fetch(0)
    norm_block(0, 0)
    for place in range(1, AHEAD):
        fetch(place)
    lax.fori_loop(1, blocks, norm_block, 0)
    rest.start()

    def keyval_tile(place, carry):
        kind, index = place // tiles, place % tiles
        weight = take(place)
        keyval[kind, index] = project(normed[...], weight[...]).astype(jnp.bfloat16)
        keyval_copy(kind, index).start()
        return carry

    lax.fori_loop(0, 2 * tiles, keyval_tile, 0)
    mix_frame(
        normed.at[pl.ds(0, count), :], take, 2 * tiles, tiles, keyval.at[0], keyval.at[1],
        lambda index: None, attended,
    )
    leave_frame(
        tokens.at[pl.ds(0, count), :], action_ref, time_gain_ref, attended, take, 3 * tiles, tiles,
        time, middle, rounded, squares, time_hbm, middle_hbm, out_sem,
    )
    rest.wait()
    for kind in range(2):
        for index in range(tiles):
            keyval_copy(kind, index).wait()


def first(tokens, action_pieces, pair_index, space_gain, time_gain, qkv, out, count):
    frame, width = tokens.shape
    columns = qkv.shape[2]
    tiles = columns // TILE
    dma = pltpu.SemaphoreType.DMA
    row = pl.BlockSpec((1, width), lambda: (0, 0))
    return pl.pallas_call(
        functools.partial(first_kernel, count),
        in_specs=in_hbm(1) + row_specs(action_pieces) + [row] * 2 + in_hbm(2),
        out_specs=in_hbm(4),
        out_shape=[
            jax.ShapeDtypeStruct((count, width), jnp.bfloat16),
            jax.ShapeDtypeStruct((count, width), jnp.bfloat16),
            jax.ShapeDtypeStruct((frame - count, width), jnp.bfloat16),
            jax.ShapeDtypeStruct((2, frame, columns), jnp.bfloat16),
        ],
        scratch_shapes=[
            pltpu.VMEM((frame, width), jnp.bfloat16),
            pltpu.VMEM((frame, width), jnp.bfloat16),
            *ring_of(width),
            pltpu.VMEM((2, tiles, frame, TILE), jnp.bfloat16),
            pltpu.VMEM((count, columns), jnp.bfloat16),
            pltpu.VMEM((count, width), jnp.bfloat16),
            pltpu.VMEM((count, width), jnp.float32),
            pltpu.VMEM((count, width), jnp.bfloat16),
            pltpu.VMEM((count, 1), jnp.float32),
            pltpu.VMEM((1, width), jnp.float32),
            dma((frame // ROWS,)), dma, dma, dma((2,)),
        ],
        compiler_params=limits(LIMIT),
        cost_estimate=pl.CostEstimate(
            flops=4 * frame * width * columns + 4 * count * width * columns + 8 * count * frame * columns,
            bytes_accessed=8 * width * columns, transcendentals=count * frame * columns // HEAD_DIM,
        ),
        name="space_first",
    )(tokens, action_pieces, pair_index, space_gain, time_gain, qkv, out)


def later_kernel(
    offset, tokens_hbm, rows_ref, pair_ref, time_gain_ref, qkv_hbm, out_hbm, normed_hbm, keyval_hbm,
    time_hbm, middle_hbm,
    tokens, normed, ring, ring_sem, keyval, attended, time, middle, rounded, squares, action_ref,
    token_sem, normed_sem, keyval_sem, out_sem
):
    tiles = keyval.shape[1]
    count = tokens.shape[0]
    fetch, take = weight_stream(qkv_hbm, out_hbm, ring, ring_sem, (0,))

    def keyval_copy(kind, index):
        return pltpu.make_async_copy(
            keyval_hbm.at[kind, :, tile_at(index)], keyval.at[kind, index], keyval_sem.at[kind, index]
        )

    normed_copy = pltpu.make_async_copy(normed_hbm, normed, normed_sem)
    token_copy = pltpu.make_async_copy(tokens_hbm.at[pl.ds(offset, count), :], tokens, token_sem)
    def fetch_keyval(index):
        for kind in range(2):
            keyval_copy(kind, index).start()

    normed_copy.start()
    fetch(0)
    fetch_keyval(0)
    action_ref[...] = own_row(rows_ref, pair_ref)
    normed_copy.wait()
    for place in range(1, AHEAD):
        fetch(place)

    def ready(index):
        for kind in range(2):
            keyval_copy(kind, index).wait()
        pl.when(index + 1 < tiles)(lambda: fetch_keyval(index + 1))
        pl.when(index == tiles - 1)(lambda: token_copy.start())

    mix_frame(normed, take, 0, tiles, keyval.at[0], keyval.at[1], ready, attended)
    token_copy.wait()
    leave_frame(
        tokens, action_ref, time_gain_ref, attended, take, tiles, tiles,
        time, middle, rounded, squares, time_hbm, middle_hbm, out_sem,
    )


def later(tokens, action_pieces, pair_index, time_gain, qkv, out, normed, keyval, offset):
    frame, width = tokens.shape
    count = normed.shape[0]
    columns = qkv.shape[2]
    tiles = columns // TILE
    dma = pltpu.SemaphoreType.DMA
    row = pl.BlockSpec((1, width), lambda: (0, 0))
    return pl.pallas_call(
        functools.partial(later_kernel, offset),
        in_specs=in_hbm(1) + row_specs(action_pieces) + [row] + in_hbm(4),
        out_specs=in_hbm(2),
        out_shape=[
            jax.ShapeDtypeStruct((count, width), jnp.bfloat16),
            jax.ShapeDtypeStruct((count, width), jnp.bfloat16),
        ],
        scratch_shapes=[
            pltpu.VMEM((count, width), jnp.bfloat16),
            pltpu.VMEM((count, width), jnp.bfloat16),
            *ring_of(width),
            pltpu.VMEM((2, tiles, frame, TILE), jnp.bfloat16),
            pltpu.VMEM((count, columns), jnp.bfloat16),
            pltpu.VMEM((count, width), jnp.bfloat16),
            pltpu.VMEM((count, width), jnp.float32),
            pltpu.VMEM((count, width), jnp.bfloat16),
            pltpu.VMEM((count, 1), jnp.float32),
            pltpu.VMEM((1, width), jnp.float32),
            dma, dma, dma((2, tiles)), dma((2,)),
        ],
        compiler_params=limits(LIMIT),
        cost_estimate=pl.CostEstimate(
            flops=4 * count * width * columns + 8 * count * frame * columns,
            bytes_accessed=4 * width * columns, transcendentals=count * frame * columns // HEAD_DIM,
        ),
        name="space_later",
    )(tokens, action_pieces, pair_index, time_gain, qkv, out, normed, keyval)


def time_kernel(
    frames, places, received_hbm, bias_ref, qkv_hbm, out_hbm, update_hbm,
    received, mixed, update, weights, out_weights, received_sem, update_sem, weight_sem, out_sem
):
    rows, per_device = received.shape[0], received.shape[0] // frames
    tiles = weights.shape[0]
    heads = heads_of(TILE)
    received_copy = pltpu.make_async_copy(received_hbm, received, received_sem)

    def weight_copies(index):
        return [
            pltpu.make_async_copy(
                qkv_hbm.at[kind, :, tile_at(index)], weights.at[index, kind], weight_sem.at[index, kind]
            )
            for kind in range(3)
        ]

    def out_copy(index):
        return pltpu.make_async_copy(
            out_hbm.at[:, tile_at(index)], out_weights.at[index], out_sem.at[index]
        )

    def update_copy(index):
        return pltpu.make_async_copy(update.at[index], update_hbm.at[:, tile_at(index)], update_sem)

    def split(value):
        return [
            jnp.concatenate(
                [value[start + at:start + at + places, :] for start in range(0, rows, per_device)], 0
            ).astype(jnp.bfloat16)
            for at in range(0, per_device, places)
        ]

    def join(parts):
        return jnp.concatenate(
            [part[at:at + places, :] for at in range(0, frames * places, places) for part in parts], 0
        )

    def mix_tile(index, carry):
        @pl.when(index + 2 < tiles)
        def _():
            for copy in weight_copies(index + 2):
                copy.start()

        @pl.when(index + 2 >= tiles)
        def _():
            for half in range(2):
                out_copy(2 * (index + 2 - tiles) + half).start()

        for copy in weight_copies(index):
            copy.wait()
        entered = received[...]
        query = split(project(entered, weights[index, 0]) * EXPONENT)
        keys = split(project(entered, weights[index, 1]))
        value = split(project(entered, weights[index, 2]))
        parts = []
        for part in range(len(query)):
            done = attend(
                [query[part][:, cols] for cols in heads],
                [keys[part][:, cols] for cols in heads],
                [with_ones(value[part][:, cols]) for cols in heads],
                bias_ref[...],
            )
            parts.append(jnp.concatenate(done, -1))
        mixed[:, tile_at(index)] = join(parts).astype(jnp.bfloat16)
        return carry

    def out_tile(index, carry):
        out_copy(index).wait()
        update[index] = project(mixed[...], out_weights[index]).astype(jnp.bfloat16)
        update_copy(index).start()
        return carry

    received_copy.start()
    for copy in weight_copies(0):
        copy.start()
    received_copy.wait()
    for copy in weight_copies(1):
        copy.start()
    lax.fori_loop(0, tiles, mix_tile, 0)
    lax.fori_loop(0, out_weights.shape[0], out_tile, 0)
    for index in range(out_weights.shape[0]):
        update_copy(index).wait()


def time_mix(received, bias, qkv, out, frames, places):
    rows, width = received.shape
    columns = qkv.shape[2]
    block = frames * places
    tiles, out_tiles = columns // TILE, width // TILE
    dma = pltpu.SemaphoreType.DMA
    return pl.pallas_call(
        functools.partial(time_kernel, frames, places),
        in_specs=in_hbm(1) + [pl.BlockSpec(memory_space=pltpu.VMEM)] + in_hbm(2),
        out_specs=in_hbm(1)[0],
        out_shape=jax.ShapeDtypeStruct((rows, width), jnp.bfloat16),
        scratch_shapes=[
            pltpu.VMEM((rows, width), jnp.bfloat16),
            pltpu.VMEM((rows, columns), jnp.bfloat16),
            pltpu.VMEM((out_tiles, rows, TILE), jnp.bfloat16),
            pltpu.VMEM((tiles, 3, width, TILE), jnp.bfloat16),
            pltpu.VMEM((out_tiles, columns, TILE), jnp.bfloat16),
            dma, dma, dma((tiles, 3)), dma((out_tiles,)),
        ],
        compiler_params=limits(LIMIT),
        cost_estimate=pl.CostEstimate(
            flops=8 * rows * width * columns, bytes_accessed=8 * width * columns,
            transcendentals=rows * block * columns // HEAD_DIM,
        ),
        name="time_mix",
    )(received, bias, qkv, out)


def add_kernel(offset, update_hbm, middle_hbm, *rest):
    result_hbm, update, middle, result, in_sem, result_sem = rest[-6:]
    blocks = update.shape[0] // ROWS

    def block_at(index, base=0):
        return pl.ds(pl.multiple_of(base + index * ROWS, ROWS), ROWS)

    def in_copies(index):
        here = block_at(index)
        return (
            pltpu.make_async_copy(update_hbm.at[here, :], update.at[here, :], in_sem.at[0, index]),
            pltpu.make_async_copy(middle_hbm.at[here, :], middle.at[here, :], in_sem.at[1, index]),
        )

    def result_copy(index):
        return pltpu.make_async_copy(
            result.at[block_at(index), :], result_hbm.at[block_at(index, offset), :], result_sem
        )

    def block(index, carry):
        for copy in in_copies(index):
            copy.wait()
        here = block_at(index)
        result[here, :] = (
            middle[here, :].astype(jnp.float32) + update[here, :].astype(jnp.float32)
        ).astype(jnp.bfloat16)
        result_copy(index).start()
        return carry

    for index in range(blocks):
        for copy in in_copies(index):
            copy.start()
    lax.fori_loop(0, blocks, block, 0)
    for index in range(blocks):
        result_copy(index).wait()


def add_update(update, middle, earlier, total, offset):
    rows, width = middle.shape
    extra = [] if earlier is None else [earlier]
    dma = pltpu.SemaphoreType.DMA
    return pl.pallas_call(
        functools.partial(add_kernel, offset),
        in_specs=in_hbm(2 + len(extra)),
        out_specs=in_hbm(1)[0],
        out_shape=jax.ShapeDtypeStruct((total, width), jnp.bfloat16),
        scratch_shapes=[pltpu.VMEM((rows, width), jnp.bfloat16)] * 3 + [dma((2, rows // ROWS)), dma],
        input_output_aliases={2: 0} if extra else {},
        compiler_params=limits(LIMIT),
        cost_estimate=pl.CostEstimate(
            flops=rows * width, bytes_accessed=6 * rows * width, transcendentals=0
        ),
        name="time_add",
    )(update, middle, *extra)


def fold_projection(weights, row_count, segment):
    flat_rows = segment.reshape(row_count, segment.shape[-1])
    return jnp.einsum("rc,icj->irj", flat_rows, weights, preferred_element_type=jnp.float32)


def space_frame(triple):
    query, keys, values = triple
    tokens_frame, columns = query.shape
    query = query.reshape(tokens_frame, columns // HEAD_DIM, HEAD_DIM)
    keys = keys.reshape(tokens_frame, columns // HEAD_DIM, HEAD_DIM)
    values = values.reshape(tokens_frame, columns // HEAD_DIM, HEAD_DIM)
    scores = jnp.einsum(
        "qhd,khd->hqk", query, keys, preferred_element_type=jnp.float32
    ) * HEAD_DIM ** (-0.5)
    probabilities = jax.nn.softmax(scores, -1).astype(jnp.bfloat16)
    mixture = jnp.einsum(
        "hqk,khd->qhd", probabilities, values, preferred_element_type=jnp.float32
    ).astype(jnp.bfloat16)
    return mixture.reshape(tokens_frame, columns)


def body_split_features(
    tokens,
    action_rows,
    pair_index,
    episode_id,
    space_gain,
    space_qkv,
    space_out,
    time_gain,
    time_qkv,
    time_out,
):
    frames_here, per_frame, share_width = tokens.shape
    width = share_width * lax.axis_size("tensor")
    columns = space_qkv.shape[2]
    row_count = frames_here * per_frame
    offset = lax.axis_index("tensor") * share_width
    every_row = lax.all_gather(action_rows, "tm", axis=0, tiled=True)
    frame_count = every_row.shape[0]
    picker = (pair_index[:, None] == jnp.arange(frame_count, dtype=jnp.int32)[None, :]).astype(
        jnp.bfloat16
    )
    action = jnp.dot(picker, every_row, preferred_element_type=jnp.float32)
    start = tokens.astype(jnp.float32) + action[:, None, :]
    squares = lax.psum(jnp.sum(start * start, -1), "tensor")
    factor = lax.rsqrt(squares / width + EPSILON)[..., None]
    space_normed = (
        start * factor * lax.dynamic_slice_in_dim(space_gain, offset, share_width)
    ).astype(jnp.bfloat16)
    space_proj = fold_projection(
        space_qkv, row_count, lax.all_gather(space_normed, "tensor", axis=2, tiled=True)
    ).astype(jnp.bfloat16)
    space_proj = space_proj.reshape(3, frames_here, per_frame, columns)
    attended = lax.map(space_frame, (space_proj[0], space_proj[1], space_proj[2]))
    partial_space = jnp.dot(
        attended.reshape(row_count, columns), space_out, preferred_element_type=jnp.float32
    ).reshape(frames_here, per_frame, width)
    own_part = lax.dynamic_slice_in_dim(partial_space, offset, share_width, 2) + start
    term_full = lax.dynamic_update_slice_in_dim(partial_space, own_part, offset, 2)
    summed = lax.psum(term_full.astype(jnp.bfloat16), "tensor").astype(jnp.float32)
    full_squares = jnp.sum(summed * summed, -1)
    time_normed = (
        summed * lax.rsqrt(full_squares / width + EPSILON)[..., None] * time_gain
    ).astype(jnp.bfloat16)
    time_proj = jnp.einsum(
        "rc,icj->irj",
        time_normed.reshape(row_count, width),
        time_qkv,
        preferred_element_type=jnp.float32,
    ).astype(jnp.bfloat16)
    middle = lax.dynamic_slice_in_dim(summed, offset, share_width, 2)
    time_proj = time_proj.reshape(3, frames_here, per_frame, columns)
    moved = (
        lax.all_to_all(time_proj[0], "tm", split_axis=1, concat_axis=0, tiled=True),
        lax.all_to_all(time_proj[1], "tm", split_axis=1, concat_axis=0, tiled=True),
        lax.all_to_all(time_proj[2], "tm", split_axis=1, concat_axis=0, tiled=True),
    )
    query_time, keys_time, values_time = moved
    places = query_time.shape[1]
    heads_here = columns // HEAD_DIM
    query_time = query_time.reshape(frame_count, places, heads_here, HEAD_DIM)
    keys_time = keys_time.reshape(frame_count, places, heads_here, HEAD_DIM)
    values_time = values_time.reshape(frame_count, places, heads_here, HEAD_DIM)
    scores = jnp.einsum(
        "fphd,gphd->phfg", query_time, keys_time, preferred_element_type=jnp.float32
    ) * HEAD_DIM ** (-0.5)
    order = jnp.arange(frame_count, dtype=jnp.int32)
    allowed = (episode_id[:, None] == episode_id[None, :]) & (order[None, :] <= order[:, None])
    scores = jnp.where(allowed, scores, -1e30)
    probabilities = jax.nn.softmax(scores, -1).astype(jnp.bfloat16)
    mixture = jnp.einsum(
        "phfg,gphd->fphd", probabilities, values_time, preferred_element_type=jnp.float32
    ).astype(jnp.bfloat16)
    returned = lax.all_to_all(
        mixture.reshape(frame_count, places, columns), "tm", split_axis=0, concat_axis=1, tiled=True
    )
    partial_time = jnp.dot(
        returned.reshape(row_count, columns), time_out, preferred_element_type=jnp.float32
    ).reshape(frames_here, per_frame, width)
    return (
        middle
        + lax.psum_scatter(
            partial_time.astype(jnp.bfloat16), "tensor", scatter_dimension=2, tiled=True
        ).astype(jnp.float32)
    ).astype(jnp.bfloat16)


def exchange(parts, groups):
    return lax.all_to_all(parts, "tm", split_axis=0, concat_axis=0, axis_index_groups=groups)


def frame_bias(episodes, places):
    frames = jnp.repeat(jnp.arange(episodes.shape[0], dtype=jnp.int32), places)
    owners = jnp.repeat(episodes, places)
    spots = jnp.tile(jnp.arange(places, dtype=jnp.int32), episodes.shape[0])
    allowed = (
        (spots[:, None] == spots[None, :])
        & (owners[:, None] == owners[None, :])
        & (frames[None, :] <= frames[:, None])
    )
    return jnp.where(allowed, 0.0, -1e30).astype(jnp.float32)


def body_whole_features(
    half_head,
    whole_head,
    tokens,
    action_rows,
    pair_index,
    episode_id,
    space_gain,
    space_qkv,
    space_out,
    time_gain,
    time_qkv,
    time_out,
):
    _, per_frame, width = tokens.shape
    columns = space_qkv.shape[2]
    frame_count = lax.axis_size("tm")
    tokens = tokens.reshape(per_frame, width)
    piece = width // 8
    action_pieces = exchange(
        jnp.broadcast_to(action_rows.reshape(1, 8, piece), (frame_count, 8, piece)), None
    )
    space_gain = space_gain.reshape(1, width)
    time_gain = time_gain.reshape(1, width)

    def over(group_size, head):
        groups = [
            list(range(start, start + group_size)) for start in range(0, frame_count, group_size)
        ]
        if group_size == frame_count:
            groups = None

        def turn(rows):
            parts = rows.reshape(group_size, rows.shape[0] // group_size, rows.shape[1])
            return exchange(parts, groups).reshape(rows.shape)

        def temporal(rows):
            places = rows.shape[0] // group_size
            if places > 8:
                places = 16 if places % 16 == 0 and group_size * 16 <= 256 else 8
            return time_mix(
                rows, frame_bias(episodes, places), time_qkv, time_out, group_size, places
            )

        start = lax.axis_index("tm") // group_size * group_size
        episodes = lax.dynamic_slice_in_dim(episode_id, start, group_size)
        early_normed, early_middle, later_rows, keyval = first(
            tokens, action_pieces, pair_index, space_gain, time_gain, space_qkv, space_out, head
        )
        early = turn(early_normed)
        late_normed, late_middle = later(
            tokens, action_pieces, pair_index, time_gain, space_qkv, space_out, later_rows, keyval, head
        )
        late = turn(late_normed)
        early_update = turn(temporal(early))
        late_update = turn(temporal(late))
        result = add_update(early_update, early_middle, None, per_frame, 0)
        result = add_update(late_update, late_middle, result, per_frame, head)
        return result.reshape(1, per_frame, width)

    half = frame_count // 2
    apart = episode_id[half - 1] != episode_id[half]
    return lax.cond(
        apart, lambda: over(half, half_head), lambda: over(frame_count, whole_head)
    )


def head_rows(per_frame, group_size, share):
    unit = math.lcm(ROWS, 8 * group_size)
    return max(unit, per_frame * share // 12 // unit * unit)


def solution(mesh):
    sizes = dict(mesh.shape)

    def body(*arrays):
        frames_here, per_frame, width = arrays[0].shape
        frame_count = sizes["tm"]
        heads = [head_rows(per_frame, frame_count // 2, 6), head_rows(per_frame, frame_count, 4)]
        fits = (
            sizes["tensor"] == 1
            and frames_here == 1
            and frame_count % 2 == 0
            and per_frame % math.lcm(ROWS, 8 * frame_count) == 0
            and all(head < per_frame for head in heads)
            and width % TILE == 0
            and arrays[5].shape[2] == width
        )
        if fits:
            return body_whole_features(*heads, *arrays)
        return body_split_features(*arrays)

    return jax.shard_map(
        body,
        mesh=mesh,
        in_specs=(
            P("tm", None, "tensor"),
            P("tm", "tensor"),
            P("tm"),
            P(),
            P(),
            P(None, None, "tensor"),
            P("tensor", None),
            P(),
            P(None, None, "tensor"),
            P("tensor", None),
        ),
        out_specs=P("tm", None, "tensor"),
        check_vma=False,
    )
```

```python
import functools
import math
import jax
import jax.numpy as jnp
from jax import lax
from jax.experimental import pallas as pl
from jax.experimental.pallas import tpu as pltpu
from jax.sharding import PartitionSpec as P

HEAD_DIM = 128


EPSILON = 1e-06
MIB = 1 << 20
SCALE = HEAD_DIM ** (-0.5)
TILE = 512
ROWS = 128
AHEAD = 3
SLOTS = AHEAD + 1
LIMIT = 60
EXPONENT = SCALE / math.log(2.0)


def limits(mebibytes):
    return pltpu.CompilerParams(vmem_limit_bytes=mebibytes * MIB)


def in_hbm(count):
    return [pl.BlockSpec(memory_space=pltpu.HBM)] * count


def row_specs(pieces):
    return [
        pl.BlockSpec(pieces.shape, lambda: (0,) * pieces.ndim),
        pl.BlockSpec(memory_space=pltpu.SMEM),
    ]


def norm_rows(value, gain):
    squares = jnp.sum(value * value, -1, keepdims=True)
    factor = lax.rsqrt(squares / value.shape[1] + EPSILON)
    return (value * factor * gain).astype(jnp.bfloat16)


def attend(queries, keys, values, bias=None):
    scores = [
        lax.dot_general(query, key, (((1,), (1,)), ((), ())), preferred_element_type=jnp.float32)
        for query, key in zip(queries, keys)
    ]
    if bias is not None:
        scores = [score + bias for score in scores]
    weights = [
        jnp.exp2(score - jnp.max(score, -1, keepdims=True)).astype(jnp.bfloat16) for score in scores
    ]
    mixed = [
        jnp.dot(weight, value, preferred_element_type=jnp.float32)
        for weight, value in zip(weights, values)
    ]
    return [part[:, :HEAD_DIM] / part[:, HEAD_DIM:] for part in mixed]


def own_row(rows_ref, pair_ref):
    row = rows_ref[pair_ref[0]].astype(jnp.float32)
    return jnp.concatenate([row[piece:piece + 1, :] for piece in range(row.shape[0])], -1)


def project(rows, weight):
    return jnp.dot(rows, weight, preferred_element_type=jnp.float32)


def heads_of(width):
    return [slice(at, at + HEAD_DIM) for at in range(0, width, HEAD_DIM)]


def with_ones(value):
    return jnp.concatenate([value, jnp.ones(value.shape, value.dtype)], -1)


def tile_at(index):
    return pl.ds(pl.multiple_of(index * TILE, TILE), TILE)


def ring_of(width):
    return [pltpu.VMEM((SLOTS, width, TILE), jnp.bfloat16), pltpu.SemaphoreType.DMA((SLOTS,))]


def weight_stream(qkv_hbm, out_hbm, ring, sems, kinds):
    tiles = out_hbm.shape[1] // TILE

    def copy(source, place):
        slot = place % SLOTS
        return pltpu.make_async_copy(source, ring.at[slot], sems.at[slot])

    def fetch(place):
        for order, kind in enumerate(kinds):
            pl.when(place // tiles == order)(
                lambda: copy(qkv_hbm.at[kind, :, tile_at(place % tiles)], place).start()
            )
        pl.when(place // tiles == len(kinds))(
            lambda: copy(out_hbm.at[:, tile_at(place % tiles)], place).start()
        )

    def take(place):
        fetch(place + AHEAD)
        copy(out_hbm.at[:, tile_at(0)], place).wait()
        return ring.at[place % SLOTS]

    return fetch, take


def mix_frame(rows_ref, take, base, tiles, keys_ref, values_ref, ready, attended_ref):
    heads = heads_of(TILE)

    def tile(index, carry):
        ready(index)
        weight = take(base + index)
        query = (project(rows_ref[...], weight[...]) * EXPONENT).astype(jnp.bfloat16)
        done = attend(
            [query[:, cols] for cols in heads],
            [keys_ref[index, :, cols] for cols in heads],
            [with_ones(values_ref[index, :, cols]) for cols in heads],
        )
        attended_ref[:, tile_at(index)] = jnp.concatenate(done, -1).astype(jnp.bfloat16)
        return carry

    lax.fori_loop(0, tiles, tile, 0)


def leave_frame(
    tokens_ref, action_ref, gain_ref, attended_ref, take, base, tiles,
    time_ref, middle_ref, rounded_ref, squares_ref, time_hbm, middle_hbm, sems, offset
):
    width = middle_ref.shape[1]
    squares_ref[...] = jnp.zeros_like(squares_ref)

    def middle_copy(index):
        return pltpu.make_async_copy(
            rounded_ref.at[:, tile_at(index)],
            middle_hbm.at[pl.ds(offset, rounded_ref.shape[0]), tile_at(index)], sems.at[1],
        )

    def tile(index, carry):
        weight = take(base + index)
        cols = tile_at(index)
        start = tokens_ref[:, cols].astype(jnp.float32) + action_ref[:, cols]
        middle = start + project(attended_ref[...], weight[...])
        middle_ref[:, cols] = middle
        rounded_ref[:, cols] = middle.astype(jnp.bfloat16)
        squares_ref[...] += jnp.sum(middle * middle, -1, keepdims=True)
        middle_copy(index).start()
        return carry

    lax.fori_loop(0, tiles, tile, 0)
    blocks = time_ref.shape[0] // ROWS

    def time_copy(index):
        here = pl.ds(pl.multiple_of(index * ROWS, ROWS), ROWS)
        return pltpu.make_async_copy(time_ref.at[here, :], time_hbm.at[here, :], sems.at[0])

    def block(index, carry):
        here = pl.ds(pl.multiple_of(index * ROWS, ROWS), ROWS)
        factor = lax.rsqrt(squares_ref[here, :] / width + EPSILON)
        time_ref[here, :] = (middle_ref[here, :] * factor * gain_ref[...]).astype(jnp.bfloat16)
        time_copy(index).start()
        return carry

    lax.fori_loop(0, blocks, block, 0)
    for index in range(tiles):
        middle_copy(index).wait()
    for index in range(blocks):
        time_copy(index).wait()


def first_kernel(
    count, tokens_hbm, rows_ref, pair_ref, space_gain_ref, time_gain_ref, qkv_hbm, out_hbm,
    time_hbm, middle_hbm, normed_hbm, keyval_hbm,
    tokens, normed, ring, ring_sem, keyval, attended, time, middle, rounded, squares, action_ref,
    token_sem, keyval_sem, normed_sem, out_sem
):
    tiles = keyval.shape[1]
    blocks = tokens.shape[0] // ROWS
    fetch, take = weight_stream(qkv_hbm, out_hbm, ring, ring_sem, (1, 2, 0))

    def token_rows(index):
        return pl.ds(pl.multiple_of(index * ROWS, ROWS), ROWS)

    def token_copy(index):
        here = token_rows(index)
        return pltpu.make_async_copy(tokens_hbm.at[here, :], tokens.at[here, :], token_sem.at[index])

    def keyval_copy(kind, index):
        return pltpu.make_async_copy(
            keyval.at[kind, index], keyval_hbm.at[kind, :, tile_at(index)], keyval_sem
        )

    rest = pltpu.make_async_copy(normed.at[pl.ds(count, tokens.shape[0] - count), :], normed_hbm, normed_sem)
    for index in range(blocks):
        token_copy(index).start()
    action_ref[...] = own_row(rows_ref, pair_ref)

    def norm_block(index, carry):
        token_copy(index).wait()
        here = token_rows(index)
        normed[here, :] = norm_rows(
            tokens[here, :].astype(jnp.float32) + action_ref[...], space_gain_ref[...]
        )
        return carry

    fetch(0)
    norm_block(0, 0)
    for place in range(1, AHEAD):
        fetch(place)
    lax.fori_loop(1, blocks, norm_block, 0)
    rest.start()

    def keyval_tile(place, carry):
        kind, index = place // tiles, place % tiles
        weight = take(place)
        keyval[kind, index] = project(normed[...], weight[...]).astype(jnp.bfloat16)
        keyval_copy(kind, index).start()
        return carry

    lax.fori_loop(0, 2 * tiles, keyval_tile, 0)
    mix_frame(
        normed.at[pl.ds(0, count), :], take, 2 * tiles, tiles, keyval.at[0], keyval.at[1],
        lambda index: None, attended,
    )
    leave_frame(
        tokens.at[pl.ds(0, count), :], action_ref, time_gain_ref, attended, take, 3 * tiles, tiles,
        time, middle, rounded, squares, time_hbm, middle_hbm, out_sem, 0,
    )
    rest.wait()
    for kind in range(2):
        for index in range(tiles):
            keyval_copy(kind, index).wait()


def first(tokens, action_pieces, pair_index, space_gain, time_gain, qkv, out, count):
    frame, width = tokens.shape
    columns = qkv.shape[2]
    tiles = columns // TILE
    dma = pltpu.SemaphoreType.DMA
    row = pl.BlockSpec((1, width), lambda: (0, 0))
    return pl.pallas_call(
        functools.partial(first_kernel, count),
        in_specs=in_hbm(1) + row_specs(action_pieces) + [row] * 2 + in_hbm(2),
        out_specs=in_hbm(4),
        out_shape=[
            jax.ShapeDtypeStruct((count, width), jnp.bfloat16),
            jax.ShapeDtypeStruct((frame, width), jnp.bfloat16),
            jax.ShapeDtypeStruct((frame - count, width), jnp.bfloat16),
            jax.ShapeDtypeStruct((2, frame, columns), jnp.bfloat16),
        ],
        scratch_shapes=[
            pltpu.VMEM((frame, width), jnp.bfloat16),
            pltpu.VMEM((frame, width), jnp.bfloat16),
            *ring_of(width),
            pltpu.VMEM((2, tiles, frame, TILE), jnp.bfloat16),
            pltpu.VMEM((count, columns), jnp.bfloat16),
            pltpu.VMEM((count, width), jnp.bfloat16),
            pltpu.VMEM((count, width), jnp.float32),
            pltpu.VMEM((count, width), jnp.bfloat16),
            pltpu.VMEM((count, 1), jnp.float32),
            pltpu.VMEM((1, width), jnp.float32),
            dma((frame // ROWS,)), dma, dma, dma((2,)),
        ],
        compiler_params=limits(LIMIT),
        cost_estimate=pl.CostEstimate(
            flops=4 * frame * width * columns + 4 * count * width * columns + 8 * count * frame * columns,
            bytes_accessed=8 * width * columns, transcendentals=count * frame * columns // HEAD_DIM,
        ),
        name="space_first",
    )(tokens, action_pieces, pair_index, space_gain, time_gain, qkv, out)


def later_kernel(
    offset, tokens_hbm, rows_ref, pair_ref, time_gain_ref, qkv_hbm, out_hbm, normed_hbm, keyval_hbm, _,
    time_hbm, middle_hbm,
    tokens, normed, ring, ring_sem, keyval, attended, time, middle, rounded, squares, action_ref,
    token_sem, normed_sem, keyval_sem, out_sem
):
    tiles = keyval.shape[1]
    count = tokens.shape[0]
    fetch, take = weight_stream(qkv_hbm, out_hbm, ring, ring_sem, (0,))

    def keyval_copy(kind, index):
        return pltpu.make_async_copy(
            keyval_hbm.at[kind, :, tile_at(index)], keyval.at[kind, index], keyval_sem.at[kind, index]
        )

    normed_copy = pltpu.make_async_copy(normed_hbm, normed, normed_sem)
    token_copy = pltpu.make_async_copy(tokens_hbm.at[pl.ds(offset, count), :], tokens, token_sem)
    def fetch_keyval(index):
        for kind in range(2):
            keyval_copy(kind, index).start()

    normed_copy.start()
    fetch(0)
    fetch_keyval(0)
    action_ref[...] = own_row(rows_ref, pair_ref)
    normed_copy.wait()
    for place in range(1, AHEAD):
        fetch(place)

    def ready(index):
        for kind in range(2):
            keyval_copy(kind, index).wait()
        pl.when(index + 1 < tiles)(lambda: fetch_keyval(index + 1))
        pl.when(index == tiles - 1)(lambda: token_copy.start())

    mix_frame(normed, take, 0, tiles, keyval.at[0], keyval.at[1], ready, attended)
    token_copy.wait()
    leave_frame(
        tokens, action_ref, time_gain_ref, attended, take, tiles, tiles,
        time, middle, rounded, squares, time_hbm, middle_hbm, out_sem, offset,
    )


def later(tokens, action_pieces, pair_index, time_gain, qkv, out, normed, keyval, middle, offset):
    frame, width = tokens.shape
    count = normed.shape[0]
    columns = qkv.shape[2]
    tiles = columns // TILE
    dma = pltpu.SemaphoreType.DMA
    row = pl.BlockSpec((1, width), lambda: (0, 0))
    return pl.pallas_call(
        functools.partial(later_kernel, offset),
        in_specs=in_hbm(1) + row_specs(action_pieces) + [row] + in_hbm(5),
        out_specs=in_hbm(2),
        out_shape=[
            jax.ShapeDtypeStruct((count, width), jnp.bfloat16),
            jax.ShapeDtypeStruct((frame, width), jnp.bfloat16),
        ],
        input_output_aliases={8: 1},
        scratch_shapes=[
            pltpu.VMEM((count, width), jnp.bfloat16),
            pltpu.VMEM((count, width), jnp.bfloat16),
            *ring_of(width),
            pltpu.VMEM((2, tiles, frame, TILE), jnp.bfloat16),
            pltpu.VMEM((count, columns), jnp.bfloat16),
            pltpu.VMEM((count, width), jnp.bfloat16),
            pltpu.VMEM((count, width), jnp.float32),
            pltpu.VMEM((count, width), jnp.bfloat16),
            pltpu.VMEM((count, 1), jnp.float32),
            pltpu.VMEM((1, width), jnp.float32),
            dma, dma, dma((2, tiles)), dma((2,)),
        ],
        compiler_params=limits(LIMIT),
        cost_estimate=pl.CostEstimate(
            flops=4 * count * width * columns + 8 * count * frame * columns,
            bytes_accessed=4 * width * columns, transcendentals=count * frame * columns // HEAD_DIM,
        ),
        name="space_later",
    )(tokens, action_pieces, pair_index, time_gain, qkv, out, normed, keyval, middle)


def time_kernel(
    frames, places, received_hbm, bias_ref, qkv_hbm, out_hbm, update_hbm,
    received, mixed, update, weights, out_weights, received_sem, update_sem, weight_sem, out_sem
):
    rows, per_device = received.shape[0], received.shape[0] // frames
    tiles = weights.shape[0]
    heads = heads_of(TILE)
    received_copy = pltpu.make_async_copy(received_hbm, received, received_sem)

    def weight_copies(index):
        return [
            pltpu.make_async_copy(
                qkv_hbm.at[kind, :, tile_at(index)], weights.at[index, kind], weight_sem.at[index, kind]
            )
            for kind in range(3)
        ]

    def out_copy(index):
        return pltpu.make_async_copy(
            out_hbm.at[:, tile_at(index)], out_weights.at[index], out_sem.at[index]
        )

    def update_copy(index):
        return pltpu.make_async_copy(update.at[index], update_hbm.at[:, tile_at(index)], update_sem)

    def split(value):
        return [
            jnp.concatenate(
                [value[start + at:start + at + places, :] for start in range(0, rows, per_device)], 0
            ).astype(jnp.bfloat16)
            for at in range(0, per_device, places)
        ]

    def join(parts):
        return jnp.concatenate(
            [part[at:at + places, :] for at in range(0, frames * places, places) for part in parts], 0
        )

    def mix_tile(index, carry):
        @pl.when(index + 2 < tiles)
        def _():
            for copy in weight_copies(index + 2):
                copy.start()

        @pl.when(index + 2 >= tiles)
        def _():
            for half in range(2):
                out_copy(2 * (index + 2 - tiles) + half).start()

        for copy in weight_copies(index):
            copy.wait()
        entered = received[...]
        query = split(project(entered, weights[index, 0]) * EXPONENT)
        keys = split(project(entered, weights[index, 1]))
        value = split(project(entered, weights[index, 2]))
        parts = []
        for part in range(len(query)):
            done = attend(
                [query[part][:, cols] for cols in heads],
                [keys[part][:, cols] for cols in heads],
                [with_ones(value[part][:, cols]) for cols in heads],
                bias_ref[...],
            )
            parts.append(jnp.concatenate(done, -1))
        mixed[:, tile_at(index)] = join(parts).astype(jnp.bfloat16)
        return carry

    def out_tile(index, carry):
        out_copy(index).wait()
        update[index] = project(mixed[...], out_weights[index]).astype(jnp.bfloat16)
        update_copy(index).start()
        return carry

    received_copy.start()
    for copy in weight_copies(0):
        copy.start()
    received_copy.wait()
    for copy in weight_copies(1):
        copy.start()
    lax.fori_loop(0, tiles, mix_tile, 0)
    lax.fori_loop(0, out_weights.shape[0], out_tile, 0)
    for index in range(out_weights.shape[0]):
        update_copy(index).wait()


def time_mix(received, bias, qkv, out, frames, places):
    rows, width = received.shape
    columns = qkv.shape[2]
    block = frames * places
    tiles, out_tiles = columns // TILE, width // TILE
    dma = pltpu.SemaphoreType.DMA
    return pl.pallas_call(
        functools.partial(time_kernel, frames, places),
        in_specs=in_hbm(1) + [pl.BlockSpec(memory_space=pltpu.VMEM)] + in_hbm(2),
        out_specs=in_hbm(1)[0],
        out_shape=jax.ShapeDtypeStruct((rows, width), jnp.bfloat16),
        scratch_shapes=[
            pltpu.VMEM((rows, width), jnp.bfloat16),
            pltpu.VMEM((rows, columns), jnp.bfloat16),
            pltpu.VMEM((out_tiles, rows, TILE), jnp.bfloat16),
            pltpu.VMEM((tiles, 3, width, TILE), jnp.bfloat16),
            pltpu.VMEM((out_tiles, columns, TILE), jnp.bfloat16),
            dma, dma, dma((tiles, 3)), dma((out_tiles,)),
        ],
        compiler_params=limits(LIMIT),
        cost_estimate=pl.CostEstimate(
            flops=8 * rows * width * columns, bytes_accessed=8 * width * columns,
            transcendentals=rows * block * columns // HEAD_DIM,
        ),
        name="time_mix",
    )(received, bias, qkv, out)


def add_kernel(offset, update_ref, middle_hbm, result_hbm, middle, result, in_sem, result_sem):
    blocks = update_ref.shape[0] // ROWS

    def block_at(index, base=0):
        return pl.ds(pl.multiple_of(base + index * ROWS, ROWS), ROWS)

    def in_copy(index):
        return pltpu.make_async_copy(
            middle_hbm.at[block_at(index, offset), :], middle.at[block_at(index), :], in_sem.at[index]
        )

    def result_copy(index):
        return pltpu.make_async_copy(
            result.at[block_at(index), :], result_hbm.at[block_at(index, offset), :], result_sem
        )

    def block(index, carry):
        in_copy(index).wait()
        here = block_at(index)
        result[here, :] = (
            middle[here, :].astype(jnp.float32) + update_ref[here, :].astype(jnp.float32)
        ).astype(jnp.bfloat16)
        result_copy(index).start()
        return carry

    for index in range(blocks):
        in_copy(index).start()
    lax.fori_loop(0, blocks, block, 0)
    for index in range(blocks):
        result_copy(index).wait()


def add_update(update, middle, offset):
    rows, width = update.shape
    dma = pltpu.SemaphoreType.DMA
    return pl.pallas_call(
        functools.partial(add_kernel, offset),
        in_specs=[pl.BlockSpec(memory_space=pltpu.VMEM)] + in_hbm(1),
        out_specs=in_hbm(1)[0],
        out_shape=jax.ShapeDtypeStruct(middle.shape, jnp.bfloat16),
        scratch_shapes=[pltpu.VMEM((rows, width), jnp.bfloat16)] * 2 + [dma((rows // ROWS,)), dma],
        input_output_aliases={1: 0},
        compiler_params=limits(16),
        cost_estimate=pl.CostEstimate(
            flops=rows * width, bytes_accessed=6 * rows * width, transcendentals=0
        ),
        name="time_add",
    )(update, middle)


def fold_projection(weights, row_count, segment):
    flat_rows = segment.reshape(row_count, segment.shape[-1])
    return jnp.einsum("rc,icj->irj", flat_rows, weights, preferred_element_type=jnp.float32)


def space_frame(triple):
    query, keys, values = triple
    tokens_frame, columns = query.shape
    query = query.reshape(tokens_frame, columns // HEAD_DIM, HEAD_DIM)
    keys = keys.reshape(tokens_frame, columns // HEAD_DIM, HEAD_DIM)
    values = values.reshape(tokens_frame, columns // HEAD_DIM, HEAD_DIM)
    scores = jnp.einsum(
        "qhd,khd->hqk", query, keys, preferred_element_type=jnp.float32
    ) * HEAD_DIM ** (-0.5)
    probabilities = jax.nn.softmax(scores, -1).astype(jnp.bfloat16)
    mixture = jnp.einsum(
        "hqk,khd->qhd", probabilities, values, preferred_element_type=jnp.float32
    ).astype(jnp.bfloat16)
    return mixture.reshape(tokens_frame, columns)


def body_split_features(
    tokens,
    action_rows,
    pair_index,
    episode_id,
    space_gain,
    space_qkv,
    space_out,
    time_gain,
    time_qkv,
    time_out,
):
    frames_here, per_frame, share_width = tokens.shape
    width = share_width * lax.axis_size("tensor")
    columns = space_qkv.shape[2]
    row_count = frames_here * per_frame
    offset = lax.axis_index("tensor") * share_width
    every_row = lax.all_gather(action_rows, "tm", axis=0, tiled=True)
    frame_count = every_row.shape[0]
    picker = (pair_index[:, None] == jnp.arange(frame_count, dtype=jnp.int32)[None, :]).astype(
        jnp.bfloat16
    )
    action = jnp.dot(picker, every_row, preferred_element_type=jnp.float32)
    start = tokens.astype(jnp.float32) + action[:, None, :]
    squares = lax.psum(jnp.sum(start * start, -1), "tensor")
    factor = lax.rsqrt(squares / width + EPSILON)[..., None]
    space_normed = (
        start * factor * lax.dynamic_slice_in_dim(space_gain, offset, share_width)
    ).astype(jnp.bfloat16)
    space_proj = fold_projection(
        space_qkv, row_count, lax.all_gather(space_normed, "tensor", axis=2, tiled=True)
    ).astype(jnp.bfloat16)
    space_proj = space_proj.reshape(3, frames_here, per_frame, columns)
    attended = lax.map(space_frame, (space_proj[0], space_proj[1], space_proj[2]))
    partial_space = jnp.dot(
        attended.reshape(row_count, columns), space_out, preferred_element_type=jnp.float32
    ).reshape(frames_here, per_frame, width)
    own_part = lax.dynamic_slice_in_dim(partial_space, offset, share_width, 2) + start
    term_full = lax.dynamic_update_slice_in_dim(partial_space, own_part, offset, 2)
    summed = lax.psum(term_full.astype(jnp.bfloat16), "tensor").astype(jnp.float32)
    full_squares = jnp.sum(summed * summed, -1)
    time_normed = (
        summed * lax.rsqrt(full_squares / width + EPSILON)[..., None] * time_gain
    ).astype(jnp.bfloat16)
    time_proj = jnp.einsum(
        "rc,icj->irj",
        time_normed.reshape(row_count, width),
        time_qkv,
        preferred_element_type=jnp.float32,
    ).astype(jnp.bfloat16)
    middle = lax.dynamic_slice_in_dim(summed, offset, share_width, 2)
    time_proj = time_proj.reshape(3, frames_here, per_frame, columns)
    moved = (
        lax.all_to_all(time_proj[0], "tm", split_axis=1, concat_axis=0, tiled=True),
        lax.all_to_all(time_proj[1], "tm", split_axis=1, concat_axis=0, tiled=True),
        lax.all_to_all(time_proj[2], "tm", split_axis=1, concat_axis=0, tiled=True),
    )
    query_time, keys_time, values_time = moved
    places = query_time.shape[1]
    heads_here = columns // HEAD_DIM
    query_time = query_time.reshape(frame_count, places, heads_here, HEAD_DIM)
    keys_time = keys_time.reshape(frame_count, places, heads_here, HEAD_DIM)
    values_time = values_time.reshape(frame_count, places, heads_here, HEAD_DIM)
    scores = jnp.einsum(
        "fphd,gphd->phfg", query_time, keys_time, preferred_element_type=jnp.float32
    ) * HEAD_DIM ** (-0.5)
    order = jnp.arange(frame_count, dtype=jnp.int32)
    allowed = (episode_id[:, None] == episode_id[None, :]) & (order[None, :] <= order[:, None])
    scores = jnp.where(allowed, scores, -1e30)
    probabilities = jax.nn.softmax(scores, -1).astype(jnp.bfloat16)
    mixture = jnp.einsum(
        "phfg,gphd->fphd", probabilities, values_time, preferred_element_type=jnp.float32
    ).astype(jnp.bfloat16)
    returned = lax.all_to_all(
        mixture.reshape(frame_count, places, columns), "tm", split_axis=0, concat_axis=1, tiled=True
    )
    partial_time = jnp.dot(
        returned.reshape(row_count, columns), time_out, preferred_element_type=jnp.float32
    ).reshape(frames_here, per_frame, width)
    return (
        middle
        + lax.psum_scatter(
            partial_time.astype(jnp.bfloat16), "tensor", scatter_dimension=2, tiled=True
        ).astype(jnp.float32)
    ).astype(jnp.bfloat16)


def exchange(parts, groups):
    return lax.all_to_all(parts, "tm", split_axis=0, concat_axis=0, axis_index_groups=groups)


def frame_bias(episodes, places):
    frames = jnp.repeat(jnp.arange(episodes.shape[0], dtype=jnp.int32), places)
    owners = jnp.repeat(episodes, places)
    spots = jnp.tile(jnp.arange(places, dtype=jnp.int32), episodes.shape[0])
    allowed = (
        (spots[:, None] == spots[None, :])
        & (owners[:, None] == owners[None, :])
        & (frames[None, :] <= frames[:, None])
    )
    return jnp.where(allowed, 0.0, -1e30).astype(jnp.float32)


def body_whole_features(
    half_head,
    whole_head,
    tokens,
    action_rows,
    pair_index,
    episode_id,
    space_gain,
    space_qkv,
    space_out,
    time_gain,
    time_qkv,
    time_out,
):
    _, per_frame, width = tokens.shape
    columns = space_qkv.shape[2]
    frame_count = lax.axis_size("tm")
    tokens = tokens.reshape(per_frame, width)
    piece = width // 8
    action_pieces = exchange(
        jnp.broadcast_to(action_rows.reshape(1, 8, piece), (frame_count, 8, piece)), None
    )
    space_gain = space_gain.reshape(1, width)
    time_gain = time_gain.reshape(1, width)

    def over(group_size, head):
        groups = [
            list(range(start, start + group_size)) for start in range(0, frame_count, group_size)
        ]
        if group_size == frame_count:
            groups = None

        def places_together(count):
            places = count // group_size
            if places % 16 == 0 and group_size * 16 <= 256:
                return 16
            return 8

        start = lax.axis_index("tm") // group_size * group_size
        episodes = lax.dynamic_slice_in_dim(episode_id, start, group_size)
        biases = {
            places: frame_bias(episodes, places)
            for places in {places_together(count) for count in (head, per_frame - head)}
        }

        def turn(rows):
            parts = rows.reshape(group_size, rows.shape[0] // group_size, rows.shape[1])
            return exchange(parts, groups).reshape(rows.shape)

        def temporal(rows):
            places = places_together(rows.shape[0])
            return time_mix(
                rows, biases[places], time_qkv, time_out, group_size, places
            )

        def run():
            early_normed, middle, later_rows, keyval = first(
                tokens, action_pieces, pair_index, space_gain, time_gain, space_qkv, space_out, head
            )
            early = turn(early_normed)
            late_normed, middle = later(
                tokens, action_pieces, pair_index, time_gain, space_qkv, space_out, later_rows, keyval,
                middle, head,
            )
            late = turn(late_normed)
            early_update = turn(temporal(early))
            late_update = turn(temporal(late))
            result = add_update(late_update, add_update(early_update, middle, 0), head)
            return result.reshape(1, per_frame, width)

        return run

    half = frame_count // 2
    apart = episode_id[half - 1] != episode_id[half]
    return lax.cond(apart, over(half, half_head), over(frame_count, whole_head))


def head_rows(per_frame, group_size, share):
    unit = math.lcm(ROWS, 8 * group_size)
    return max(unit, per_frame * share // 12 // unit * unit)


def solution(mesh):
    sizes = dict(mesh.shape)

    def body(*arrays):
        frames_here, per_frame, width = arrays[0].shape
        frame_count = sizes["tm"]
        heads = [head_rows(per_frame, frame_count // 2, 6), head_rows(per_frame, frame_count, 4)]
        fits = (
            sizes["tensor"] == 1
            and frames_here == 1
            and frame_count % 2 == 0
            and per_frame % math.lcm(ROWS, 8 * frame_count) == 0
            and all(head < per_frame for head in heads)
            and width % TILE == 0
            and arrays[5].shape[2] == width
        )
        if fits:
            return body_whole_features(*heads, *arrays)
        return body_split_features(*arrays)

    return jax.shard_map(
        body,
        mesh=mesh,
        in_specs=(
            P("tm", None, "tensor"),
            P("tm", "tensor"),
            P("tm"),
            P(),
            P(),
            P(None, None, "tensor"),
            P("tensor", None),
            P(),
            P(None, None, "tensor"),
            P("tensor", None),
        ),
        out_specs=P("tm", None, "tensor"),
        check_vma=False,
    )
```

```python
import functools
import math
import jax
import jax.numpy as jnp
import numpy as np
from jax import lax
from jax.experimental import pallas as pl
from jax.experimental.pallas import tpu as pltpu
from jax.sharding import PartitionSpec as P

HEAD_DIM = 128


EPSILON = 1e-06
MIB = 1 << 20
SCALE = HEAD_DIM ** (-0.5)
TILE = 512
ROWS = 128
AHEAD = 3
SLOTS = AHEAD + 1
LIMIT = 60
HELD_LIMIT = 46
EXPONENT = SCALE / math.log(2.0)


def limits(mebibytes):
    return pltpu.CompilerParams(vmem_limit_bytes=mebibytes * MIB)


def in_hbm(count):
    return [pl.BlockSpec(memory_space=pltpu.HBM)] * count


def row_specs(pieces):
    return [
        pl.BlockSpec(pieces.shape, lambda: (0,) * pieces.ndim),
        pl.BlockSpec(memory_space=pltpu.SMEM),
    ]


def norm_rows(value, gain):
    squares = jnp.sum(value * value, -1, keepdims=True)
    factor = lax.rsqrt(squares / value.shape[1] + EPSILON)
    return (value * factor * gain).astype(jnp.bfloat16)


def attend(queries, keys, values, bias=None):
    scores = [
        lax.dot_general(query, key, (((1,), (1,)), ((), ())), preferred_element_type=jnp.float32)
        for query, key in zip(queries, keys)
    ]
    if bias is not None:
        scores = [score + bias for score in scores]
    weights = [
        jnp.exp2(score - jnp.max(score, -1, keepdims=True)).astype(jnp.bfloat16) for score in scores
    ]
    mixed = [
        jnp.dot(weight, value, preferred_element_type=jnp.float32)
        for weight, value in zip(weights, values)
    ]
    return [part[:, :HEAD_DIM] / part[:, HEAD_DIM:] for part in mixed]


def own_row(rows_ref, pair_ref):
    row = rows_ref[pair_ref[0]].astype(jnp.float32)
    return jnp.concatenate([row[piece:piece + 1, :] for piece in range(row.shape[0])], -1)


def project(rows, weight):
    return jnp.dot(rows, weight, preferred_element_type=jnp.float32)


def heads_of(width):
    return [slice(at, at + HEAD_DIM) for at in range(0, width, HEAD_DIM)]


def with_ones(value):
    return jnp.concatenate([value, jnp.ones(value.shape, value.dtype)], -1)


def tile_at(index):
    return pl.ds(pl.multiple_of(index * TILE, TILE), TILE)


def ring_of(width):
    return [pltpu.VMEM((SLOTS, width, TILE), jnp.bfloat16), pltpu.SemaphoreType.DMA((SLOTS,))]


def weight_stream(qkv_hbm, out_hbm, ring, sems, kinds):
    tiles = out_hbm.shape[1] // TILE

    def copy(source, place):
        slot = place % SLOTS
        return pltpu.make_async_copy(source, ring.at[slot], sems.at[slot])

    def fetch(place):
        for order, kind in enumerate(kinds):
            pl.when(place // tiles == order)(
                lambda: copy(qkv_hbm.at[kind, :, tile_at(place % tiles)], place).start()
            )
        pl.when(place // tiles == len(kinds))(
            lambda: copy(out_hbm.at[:, tile_at(place % tiles)], place).start()
        )

    def take(place):
        fetch(place + AHEAD)
        copy(out_hbm.at[:, tile_at(0)], place).wait()
        return ring.at[place % SLOTS]

    return fetch, take


def mix_frame(rows_ref, take, base, tiles, keys_ref, values_ref, ready, attended_ref):
    heads = heads_of(TILE)

    def tile(index, carry):
        ready(index)
        weight = take(base + index)
        query = (project(rows_ref[...], weight[...]) * EXPONENT).astype(jnp.bfloat16)
        done = attend(
            [query[:, cols] for cols in heads],
            [keys_ref[index, :, cols] for cols in heads],
            [with_ones(values_ref[index, :, cols]) for cols in heads],
        )
        attended_ref[:, tile_at(index)] = jnp.concatenate(done, -1).astype(jnp.bfloat16)
        return carry

    lax.fori_loop(0, tiles, tile, 0)


def leave_frame(
    tokens_ref, action_ref, gain_ref, attended_ref, take, base, tiles,
    time_ref, middle_ref, rounded_ref, squares_ref, time_hbm, middle_hbm, sems, offset
):
    width = middle_ref.shape[1]
    squares_ref[...] = jnp.zeros_like(squares_ref)

    def middle_copy(index):
        return pltpu.make_async_copy(
            rounded_ref.at[:, tile_at(index)],
            middle_hbm.at[pl.ds(offset, rounded_ref.shape[0]), tile_at(index)], sems.at[1],
        )

    def tile(index, carry):
        weight = take(base + index)
        cols = tile_at(index)
        start = tokens_ref[:, cols].astype(jnp.float32) + action_ref[:, cols]
        middle = start + project(attended_ref[...], weight[...])
        middle_ref[:, cols] = middle
        rounded_ref[:, cols] = middle.astype(jnp.bfloat16)
        squares_ref[...] += jnp.sum(middle * middle, -1, keepdims=True)
        middle_copy(index).start()
        return carry

    lax.fori_loop(0, tiles, tile, 0)
    blocks = time_ref.shape[0] // ROWS

    def time_copy(index):
        here = pl.ds(pl.multiple_of(index * ROWS, ROWS), ROWS)
        return pltpu.make_async_copy(time_ref.at[here, :], time_hbm.at[here, :], sems.at[0])

    def block(index, carry):
        here = pl.ds(pl.multiple_of(index * ROWS, ROWS), ROWS)
        factor = lax.rsqrt(squares_ref[here, :] / width + EPSILON)
        time_ref[here, :] = (middle_ref[here, :] * factor * gain_ref[...]).astype(jnp.bfloat16)
        time_copy(index).start()
        return carry

    lax.fori_loop(0, blocks, block, 0)
    for index in range(tiles):
        middle_copy(index).wait()
    for index in range(blocks):
        time_copy(index).wait()


def first_kernel(
    count, tokens_hbm, rows_ref, pair_ref, space_gain_ref, time_gain_ref, qkv_hbm, out_hbm,
    time_hbm, middle_hbm, normed_hbm, keyval_hbm,
    tokens, normed, ring, ring_sem, keyval, attended, time, middle, rounded, squares, action_ref,
    token_sem, keyval_sem, normed_sem, out_sem
):
    tiles = keyval.shape[1]
    blocks = tokens.shape[0] // ROWS
    fetch, take = weight_stream(qkv_hbm, out_hbm, ring, ring_sem, (1, 2, 0))

    def token_rows(index):
        return pl.ds(pl.multiple_of(index * ROWS, ROWS), ROWS)

    def token_copy(index):
        here = token_rows(index)
        return pltpu.make_async_copy(tokens_hbm.at[here, :], tokens.at[here, :], token_sem.at[index])

    def keyval_copy(kind, index):
        return pltpu.make_async_copy(
            keyval.at[kind, index], keyval_hbm.at[kind, :, tile_at(index)], keyval_sem
        )

    rest = pltpu.make_async_copy(normed.at[pl.ds(count, tokens.shape[0] - count), :], normed_hbm, normed_sem)
    for index in range(blocks):
        token_copy(index).start()
    action_ref[...] = own_row(rows_ref, pair_ref)

    def norm_block(index, carry):
        token_copy(index).wait()
        here = token_rows(index)
        normed[here, :] = norm_rows(
            tokens[here, :].astype(jnp.float32) + action_ref[...], space_gain_ref[...]
        )
        return carry

    fetch(0)
    norm_block(0, 0)
    for place in range(1, AHEAD):
        fetch(place)
    lax.fori_loop(1, blocks, norm_block, 0)
    rest.start()

    def keyval_tile(place, carry):
        kind, index = place // tiles, place % tiles
        weight = take(place)
        keyval[kind, index] = project(normed[...], weight[...]).astype(jnp.bfloat16)
        keyval_copy(kind, index).start()
        return carry

    lax.fori_loop(0, 2 * tiles, keyval_tile, 0)
    mix_frame(
        normed.at[pl.ds(0, count), :], take, 2 * tiles, tiles, keyval.at[0], keyval.at[1],
        lambda index: None, attended,
    )
    leave_frame(
        tokens.at[pl.ds(0, count), :], action_ref, time_gain_ref, attended, take, 3 * tiles, tiles,
        time, middle, rounded, squares, time_hbm, middle_hbm, out_sem, 0,
    )
    rest.wait()
    for kind in range(2):
        for index in range(tiles):
            keyval_copy(kind, index).wait()


def first(tokens, action_pieces, pair_index, space_gain, time_gain, qkv, out, count):
    frame, width = tokens.shape
    columns = qkv.shape[2]
    tiles = columns // TILE
    dma = pltpu.SemaphoreType.DMA
    row = pl.BlockSpec((1, width), lambda: (0, 0))
    return pl.pallas_call(
        functools.partial(first_kernel, count),
        in_specs=in_hbm(1) + row_specs(action_pieces) + [row] * 2 + in_hbm(2),
        out_specs=in_hbm(4),
        out_shape=[
            jax.ShapeDtypeStruct((count, width), jnp.bfloat16),
            jax.ShapeDtypeStruct((frame, width), jnp.bfloat16),
            jax.ShapeDtypeStruct((frame - count, width), jnp.bfloat16),
            jax.ShapeDtypeStruct((2, frame, columns), jnp.bfloat16),
        ],
        scratch_shapes=[
            pltpu.VMEM((frame, width), jnp.bfloat16),
            pltpu.VMEM((frame, width), jnp.bfloat16),
            *ring_of(width),
            pltpu.VMEM((2, tiles, frame, TILE), jnp.bfloat16),
            pltpu.VMEM((count, columns), jnp.bfloat16),
            pltpu.VMEM((count, width), jnp.bfloat16),
            pltpu.VMEM((count, width), jnp.float32),
            pltpu.VMEM((count, width), jnp.bfloat16),
            pltpu.VMEM((count, 1), jnp.float32),
            pltpu.VMEM((1, width), jnp.float32),
            dma((frame // ROWS,)), dma, dma, dma((2,)),
        ],
        compiler_params=limits(LIMIT),
        cost_estimate=pl.CostEstimate(
            flops=4 * frame * width * columns + 4 * count * width * columns + 8 * count * frame * columns,
            bytes_accessed=8 * width * columns, transcendentals=count * frame * columns // HEAD_DIM,
        ),
        name="space_first",
    )(tokens, action_pieces, pair_index, space_gain, time_gain, qkv, out)


def later_kernel(
    offset, tokens_hbm, rows_ref, pair_ref, time_gain_ref, qkv_hbm, out_hbm, normed_hbm, keyval_hbm, _,
    time_hbm, middle_hbm,
    tokens, normed, ring, ring_sem, keyval, attended, time, middle, rounded, squares, action_ref,
    token_sem, normed_sem, keyval_sem, out_sem
):
    tiles = keyval.shape[1]
    count = tokens.shape[0]
    fetch, take = weight_stream(qkv_hbm, out_hbm, ring, ring_sem, (0,))

    def keyval_copy(kind, index):
        return pltpu.make_async_copy(
            keyval_hbm.at[kind, :, tile_at(index)], keyval.at[kind, index], keyval_sem.at[kind, index]
        )

    normed_copy = pltpu.make_async_copy(normed_hbm, normed, normed_sem)
    token_copy = pltpu.make_async_copy(tokens_hbm.at[pl.ds(offset, count), :], tokens, token_sem)
    def fetch_keyval(index):
        for kind in range(2):
            keyval_copy(kind, index).start()

    normed_copy.start()
    fetch(0)
    fetch_keyval(0)
    action_ref[...] = own_row(rows_ref, pair_ref)
    normed_copy.wait()
    for place in range(1, AHEAD):
        fetch(place)

    def ready(index):
        for kind in range(2):
            keyval_copy(kind, index).wait()
        pl.when(index + 1 < tiles)(lambda: fetch_keyval(index + 1))
        pl.when(index == tiles - 1)(lambda: token_copy.start())

    mix_frame(normed, take, 0, tiles, keyval.at[0], keyval.at[1], ready, attended)
    token_copy.wait()
    leave_frame(
        tokens, action_ref, time_gain_ref, attended, take, tiles, tiles,
        time, middle, rounded, squares, time_hbm, middle_hbm, out_sem, offset,
    )


def later(tokens, action_pieces, pair_index, time_gain, qkv, out, normed, keyval, middle, offset):
    frame, width = tokens.shape
    count = normed.shape[0]
    columns = qkv.shape[2]
    tiles = columns // TILE
    dma = pltpu.SemaphoreType.DMA
    row = pl.BlockSpec((1, width), lambda: (0, 0))
    return pl.pallas_call(
        functools.partial(later_kernel, offset),
        in_specs=in_hbm(1) + row_specs(action_pieces) + [row] + in_hbm(5),
        out_specs=in_hbm(2),
        out_shape=[
            jax.ShapeDtypeStruct((count, width), jnp.bfloat16),
            jax.ShapeDtypeStruct((frame, width), jnp.bfloat16),
        ],
        input_output_aliases={8: 1},
        scratch_shapes=[
            pltpu.VMEM((count, width), jnp.bfloat16),
            pltpu.VMEM((count, width), jnp.bfloat16),
            *ring_of(width),
            pltpu.VMEM((2, tiles, frame, TILE), jnp.bfloat16),
            pltpu.VMEM((count, columns), jnp.bfloat16),
            pltpu.VMEM((count, width), jnp.bfloat16),
            pltpu.VMEM((count, width), jnp.float32),
            pltpu.VMEM((count, width), jnp.bfloat16),
            pltpu.VMEM((count, 1), jnp.float32),
            pltpu.VMEM((1, width), jnp.float32),
            dma, dma, dma((2, tiles)), dma((2,)),
        ],
        compiler_params=limits(LIMIT),
        cost_estimate=pl.CostEstimate(
            flops=4 * count * width * columns + 8 * count * frame * columns,
            bytes_accessed=4 * width * columns, transcendentals=count * frame * columns // HEAD_DIM,
        ),
        name="space_later",
    )(tokens, action_pieces, pair_index, time_gain, qkv, out, normed, keyval, middle)


def time_kernel(
    frames, places, received_any, bias_ref, qkv_hbm, out_hbm, _, update_hbm,
    mixed, update, weights, out_weights, update_sem, weight_sem, out_sem, *fetched
):
    received_ref = fetched[0] if fetched else received_any
    rows = received_ref.shape[0]
    per_device = rows // frames
    tiles = weights.shape[0]
    heads = heads_of(TILE)

    def weight_copies(index):
        return [
            pltpu.make_async_copy(
                qkv_hbm.at[kind, :, tile_at(index)], weights.at[index, kind], weight_sem.at[index, kind]
            )
            for kind in range(3)
        ]

    def out_copy(index):
        return pltpu.make_async_copy(
            out_hbm.at[:, tile_at(index)], out_weights.at[index], out_sem.at[index]
        )

    def update_copy(index):
        return pltpu.make_async_copy(update.at[index], update_hbm.at[:, tile_at(index)], update_sem)

    def split(value):
        return [
            jnp.concatenate(
                [value[start + at:start + at + places, :] for start in range(0, rows, per_device)], 0
            ).astype(jnp.bfloat16)
            for at in range(0, per_device, places)
        ]

    def join(parts):
        return jnp.concatenate(
            [part[at:at + places, :] for at in range(0, frames * places, places) for part in parts], 0
        )

    def mix_tile(index, carry):
        @pl.when(index + 2 < tiles)
        def _():
            for copy in weight_copies(index + 2):
                copy.start()

        @pl.when(index + 2 >= tiles)
        def _():
            for half in range(2):
                out_copy(2 * (index + 2 - tiles) + half).start()

        for copy in weight_copies(index):
            copy.wait()
        entered = received_ref[...]
        query = split(project(entered, weights[index, 0]) * EXPONENT)
        keys = split(project(entered, weights[index, 1]))
        value = split(project(entered, weights[index, 2]))
        parts = []
        for part in range(len(query)):
            done = attend(
                [query[part][:, cols] for cols in heads],
                [keys[part][:, cols] for cols in heads],
                [with_ones(value[part][:, cols]) for cols in heads],
                bias_ref[...],
            )
            parts.append(jnp.concatenate(done, -1))
        mixed[:, tile_at(index)] = join(parts).astype(jnp.bfloat16)
        return carry

    def out_tile(index, carry):
        out_copy(index).wait()
        update[index] = project(mixed[...], out_weights[index]).astype(jnp.bfloat16)
        update_copy(index).start()
        return carry

    if fetched:
        received_copy = pltpu.make_async_copy(received_any, *fetched)
        received_copy.start()
        for copy in weight_copies(0):
            copy.start()
        received_copy.wait()
        for copy in weight_copies(1):
            copy.start()
    else:
        for copy in weight_copies(0) + weight_copies(1):
            copy.start()
    lax.fori_loop(0, tiles, mix_tile, 0)
    lax.fori_loop(0, out_weights.shape[0], out_tile, 0)
    for index in range(out_weights.shape[0]):
        update_copy(index).wait()


def time_mix(received, bias, qkv, out, sent, frames, places, held):
    rows, width = received.shape
    columns = qkv.shape[2]
    block = frames * places
    tiles, out_tiles = columns // TILE, width // TILE
    dma = pltpu.SemaphoreType.DMA
    whole = pl.BlockSpec(memory_space=pltpu.VMEM)
    return pl.pallas_call(
        functools.partial(time_kernel, frames, places),
        in_specs=([whole] if held else in_hbm(1)) + [whole] + in_hbm(3),
        out_specs=in_hbm(1)[0],
        out_shape=jax.ShapeDtypeStruct((rows, width), jnp.bfloat16),
        scratch_shapes=[
            pltpu.VMEM((rows, columns), jnp.bfloat16),
            pltpu.VMEM((out_tiles, rows, TILE), jnp.bfloat16),
            pltpu.VMEM((tiles, 3, width, TILE), jnp.bfloat16),
            pltpu.VMEM((out_tiles, columns, TILE), jnp.bfloat16),
            dma, dma((tiles, 3)), dma((out_tiles,)),
        ] + ([] if held else [pltpu.VMEM((rows, width), jnp.bfloat16), dma]),
        input_output_aliases={4: 0},
        compiler_params=limits(HELD_LIMIT if held else LIMIT),
        cost_estimate=pl.CostEstimate(
            flops=8 * rows * width * columns, bytes_accessed=8 * width * columns,
            transcendentals=rows * block * columns // HEAD_DIM,
        ),
        name="time_mix",
    )(received, bias, qkv, out, sent)


def add_kernel(offset, update_ref, middle_hbm, result_hbm, middle, result, in_sem, result_sem):
    blocks = update_ref.shape[0] // ROWS

    def block_at(index, base=0):
        return pl.ds(pl.multiple_of(base + index * ROWS, ROWS), ROWS)

    def in_copy(index):
        return pltpu.make_async_copy(
            middle_hbm.at[block_at(index, offset), :], middle.at[block_at(index), :], in_sem.at[index]
        )

    def result_copy(index):
        return pltpu.make_async_copy(
            result.at[block_at(index), :], result_hbm.at[block_at(index, offset), :], result_sem
        )

    def block(index, carry):
        in_copy(index).wait()
        here = block_at(index)
        result[here, :] = (
            middle[here, :].astype(jnp.float32) + update_ref[here, :].astype(jnp.float32)
        ).astype(jnp.bfloat16)
        result_copy(index).start()
        return carry

    for index in range(blocks):
        in_copy(index).start()
    lax.fori_loop(0, blocks, block, 0)
    for index in range(blocks):
        result_copy(index).wait()


def add_update(update, middle, offset):
    rows, width = update.shape
    dma = pltpu.SemaphoreType.DMA
    return pl.pallas_call(
        functools.partial(add_kernel, offset),
        in_specs=[pl.BlockSpec(memory_space=pltpu.VMEM)] + in_hbm(1),
        out_specs=in_hbm(1)[0],
        out_shape=jax.ShapeDtypeStruct(middle.shape, jnp.bfloat16),
        scratch_shapes=[pltpu.VMEM((rows, width), jnp.bfloat16)] * 2 + [dma((rows // ROWS,)), dma],
        input_output_aliases={1: 0},
        compiler_params=limits(16),
        cost_estimate=pl.CostEstimate(
            flops=rows * width, bytes_accessed=6 * rows * width, transcendentals=0
        ),
        name="time_add",
    )(update, middle)


def fold_projection(weights, row_count, segment):
    flat_rows = segment.reshape(row_count, segment.shape[-1])
    return jnp.einsum("rc,icj->irj", flat_rows, weights, preferred_element_type=jnp.float32)


def space_frame(triple):
    query, keys, values = triple
    tokens_frame, columns = query.shape
    query = query.reshape(tokens_frame, columns // HEAD_DIM, HEAD_DIM)
    keys = keys.reshape(tokens_frame, columns // HEAD_DIM, HEAD_DIM)
    values = values.reshape(tokens_frame, columns // HEAD_DIM, HEAD_DIM)
    scores = jnp.einsum(
        "qhd,khd->hqk", query, keys, preferred_element_type=jnp.float32
    ) * HEAD_DIM ** (-0.5)
    probabilities = jax.nn.softmax(scores, -1).astype(jnp.bfloat16)
    mixture = jnp.einsum(
        "hqk,khd->qhd", probabilities, values, preferred_element_type=jnp.float32
    ).astype(jnp.bfloat16)
    return mixture.reshape(tokens_frame, columns)


def body_split_features(
    tokens,
    action_rows,
    pair_index,
    episode_id,
    space_gain,
    space_qkv,
    space_out,
    time_gain,
    time_qkv,
    time_out,
):
    frames_here, per_frame, share_width = tokens.shape
    width = share_width * lax.axis_size("tensor")
    columns = space_qkv.shape[2]
    row_count = frames_here * per_frame
    offset = lax.axis_index("tensor") * share_width
    every_row = lax.all_gather(action_rows, "tm", axis=0, tiled=True)
    frame_count = every_row.shape[0]
    picker = (pair_index[:, None] == jnp.arange(frame_count, dtype=jnp.int32)[None, :]).astype(
        jnp.bfloat16
    )
    action = jnp.dot(picker, every_row, preferred_element_type=jnp.float32)
    start = tokens.astype(jnp.float32) + action[:, None, :]
    squares = lax.psum(jnp.sum(start * start, -1), "tensor")
    factor = lax.rsqrt(squares / width + EPSILON)[..., None]
    space_normed = (
        start * factor * lax.dynamic_slice_in_dim(space_gain, offset, share_width)
    ).astype(jnp.bfloat16)
    space_proj = fold_projection(
        space_qkv, row_count, lax.all_gather(space_normed, "tensor", axis=2, tiled=True)
    ).astype(jnp.bfloat16)
    space_proj = space_proj.reshape(3, frames_here, per_frame, columns)
    attended = lax.map(space_frame, (space_proj[0], space_proj[1], space_proj[2]))
    partial_space = jnp.dot(
        attended.reshape(row_count, columns), space_out, preferred_element_type=jnp.float32
    ).reshape(frames_here, per_frame, width)
    own_part = lax.dynamic_slice_in_dim(partial_space, offset, share_width, 2) + start
    term_full = lax.dynamic_update_slice_in_dim(partial_space, own_part, offset, 2)
    summed = lax.psum(term_full.astype(jnp.bfloat16), "tensor").astype(jnp.float32)
    full_squares = jnp.sum(summed * summed, -1)
    time_normed = (
        summed * lax.rsqrt(full_squares / width + EPSILON)[..., None] * time_gain
    ).astype(jnp.bfloat16)
    time_proj = jnp.einsum(
        "rc,icj->irj",
        time_normed.reshape(row_count, width),
        time_qkv,
        preferred_element_type=jnp.float32,
    ).astype(jnp.bfloat16)
    middle = lax.dynamic_slice_in_dim(summed, offset, share_width, 2)
    time_proj = time_proj.reshape(3, frames_here, per_frame, columns)
    moved = (
        lax.all_to_all(time_proj[0], "tm", split_axis=1, concat_axis=0, tiled=True),
        lax.all_to_all(time_proj[1], "tm", split_axis=1, concat_axis=0, tiled=True),
        lax.all_to_all(time_proj[2], "tm", split_axis=1, concat_axis=0, tiled=True),
    )
    query_time, keys_time, values_time = moved
    places = query_time.shape[1]
    heads_here = columns // HEAD_DIM
    query_time = query_time.reshape(frame_count, places, heads_here, HEAD_DIM)
    keys_time = keys_time.reshape(frame_count, places, heads_here, HEAD_DIM)
    values_time = values_time.reshape(frame_count, places, heads_here, HEAD_DIM)
    scores = jnp.einsum(
        "fphd,gphd->phfg", query_time, keys_time, preferred_element_type=jnp.float32
    ) * HEAD_DIM ** (-0.5)
    order = jnp.arange(frame_count, dtype=jnp.int32)
    allowed = (episode_id[:, None] == episode_id[None, :]) & (order[None, :] <= order[:, None])
    scores = jnp.where(allowed, scores, -1e30)
    probabilities = jax.nn.softmax(scores, -1).astype(jnp.bfloat16)
    mixture = jnp.einsum(
        "phfg,gphd->fphd", probabilities, values_time, preferred_element_type=jnp.float32
    ).astype(jnp.bfloat16)
    returned = lax.all_to_all(
        mixture.reshape(frame_count, places, columns), "tm", split_axis=0, concat_axis=1, tiled=True
    )
    partial_time = jnp.dot(
        returned.reshape(row_count, columns), time_out, preferred_element_type=jnp.float32
    ).reshape(frames_here, per_frame, width)
    return (
        middle
        + lax.psum_scatter(
            partial_time.astype(jnp.bfloat16), "tensor", scatter_dimension=2, tiled=True
        ).astype(jnp.float32)
    ).astype(jnp.bfloat16)


def exchange(parts, groups):
    return lax.all_to_all(parts, "tm", split_axis=0, concat_axis=0, axis_index_groups=groups)


def frame_bias(episodes, places):
    count = episodes.shape[0] * places
    frames, spots = np.divmod(np.arange(count), places)
    earlier = (spots[:, None] == spots[None, :]) & (frames[None, :] <= frames[:, None])
    owners = jnp.broadcast_to(episodes[:, None], (episodes.shape[0], places)).reshape(count)
    return jnp.where(earlier & (owners[:, None] == owners[None, :]), 0.0, -1e30).astype(jnp.float32)


def body_whole_features(
    half_head,
    whole_head,
    tokens,
    action_rows,
    pair_index,
    episode_id,
    space_gain,
    space_qkv,
    space_out,
    time_gain,
    time_qkv,
    time_out,
):
    _, per_frame, width = tokens.shape
    columns = space_qkv.shape[2]
    frame_count = lax.axis_size("tm")
    tokens = tokens.reshape(per_frame, width)
    piece = width // 8
    action_pieces = exchange(
        jnp.broadcast_to(action_rows.reshape(1, 8, piece), (frame_count, 8, piece)), None
    )
    space_gain = space_gain.reshape(1, width)
    time_gain = time_gain.reshape(1, width)

    def over(group_size, head):
        groups = [
            list(range(start, start + group_size)) for start in range(0, frame_count, group_size)
        ]
        if group_size == frame_count:
            groups = None

        def places_together(count):
            places = count // group_size
            if places % 16 == 0 and group_size * 16 <= 256:
                return 16
            return 8

        def turn(rows):
            parts = rows.reshape(group_size, rows.shape[0] // group_size, rows.shape[1])
            return exchange(parts, groups).reshape(rows.shape)

        def temporal(rows, sent, biases):
            places = places_together(rows.shape[0])
            return time_mix(
                rows, biases[places], time_qkv, time_out, sent, group_size, places, groups is not None
            )

        def run():
            start = lax.axis_index("tm") // group_size * group_size
            episodes = lax.dynamic_slice_in_dim(episode_id, start, group_size)
            biases = {
                places: frame_bias(episodes, places)
                for places in sorted({places_together(count) for count in (head, per_frame - head)})
            }

            early_normed, middle, later_rows, keyval = first(
                tokens, action_pieces, pair_index, space_gain, time_gain, space_qkv, space_out, head
            )
            early = turn(early_normed)
            late_normed, middle = later(
                tokens, action_pieces, pair_index, time_gain, space_qkv, space_out, later_rows, keyval,
                middle, head,
            )
            late = turn(late_normed)
            early_update = turn(temporal(early, early_normed, biases))
            late_update = turn(temporal(late, late_normed, biases))
            result = add_update(late_update, add_update(early_update, middle, 0), head)
            return result.reshape(1, per_frame, width)

        return run

    half = frame_count // 2
    apart = episode_id[half - 1] != episode_id[half]
    return lax.cond(apart, over(half, half_head), over(frame_count, whole_head))


def head_rows(per_frame, group_size, share):
    unit = math.lcm(ROWS, 8 * group_size)
    return max(unit, per_frame * share // 12 // unit * unit)


def solution(mesh):
    sizes = dict(mesh.shape)

    def body(*arrays):
        frames_here, per_frame, width = arrays[0].shape
        frame_count = sizes["tm"]
        heads = [head_rows(per_frame, frame_count // 2, 6), head_rows(per_frame, frame_count, 4)]
        fits = (
            sizes["tensor"] == 1
            and frames_here == 1
            and frame_count % 2 == 0
            and per_frame % math.lcm(ROWS, 8 * frame_count) == 0
            and all(head < per_frame for head in heads)
            and width % TILE == 0
            and arrays[5].shape[2] == width
        )
        if fits:
            return body_whole_features(*heads, *arrays)
        return body_split_features(*arrays)

    return jax.shard_map(
        body,
        mesh=mesh,
        in_specs=(
            P("tm", None, "tensor"),
            P("tm", "tensor"),
            P("tm"),
            P(),
            P(),
            P(None, None, "tensor"),
            P("tensor", None),
            P(),
            P(None, None, "tensor"),
            P("tensor", None),
        ),
        out_specs=P("tm", None, "tensor"),
        check_vma=False,
    )
```

```python
import functools
import math
import jax
import jax.numpy as jnp
import numpy as np
from jax import lax
from jax.experimental import pallas as pl
from jax.experimental.pallas import tpu as pltpu
from jax.sharding import PartitionSpec as P

HEAD_DIM = 128


EPSILON = 1e-06
MIB = 1 << 20
SCALE = HEAD_DIM ** (-0.5)
TILE = 512
ROWS = 128
AHEAD = 4
SLOTS = AHEAD + 2
LIMIT = 60
HELD_LIMIT = 46
EXPONENT = SCALE / math.log(2.0)


def limits(mebibytes):
    return pltpu.CompilerParams(vmem_limit_bytes=mebibytes * MIB)


def in_hbm(count):
    return [pl.BlockSpec(memory_space=pltpu.HBM)] * count


def row_specs(pieces):
    return [
        pl.BlockSpec(pieces.shape, lambda: (0,) * pieces.ndim),
        pl.BlockSpec(memory_space=pltpu.SMEM),
    ]


def norm_rows(value, gain):
    squares = jnp.sum(value * value, -1, keepdims=True)
    factor = lax.rsqrt(squares / value.shape[1] + EPSILON)
    return (value * factor * gain).astype(jnp.bfloat16)


def attend(queries, keys, values, bias=None):
    scores = [
        lax.dot_general(query, key, (((1,), (1,)), ((), ())), preferred_element_type=jnp.float32)
        for query, key in zip(queries, keys)
    ]
    if bias is not None:
        scores = [score + bias for score in scores]
    weights = [
        jnp.exp2(score - jnp.max(score, -1, keepdims=True)).astype(jnp.bfloat16) for score in scores
    ]
    mixed = [
        jnp.dot(weight, value, preferred_element_type=jnp.float32)
        for weight, value in zip(weights, values)
    ]
    return [part[:, :HEAD_DIM] / part[:, HEAD_DIM:] for part in mixed]


def own_row(rows_ref, pair_ref):
    row = rows_ref[pair_ref[0]].astype(jnp.float32)
    return jnp.concatenate([row[piece:piece + 1, :] for piece in range(row.shape[0])], -1)


def project(rows, weight):
    return jnp.dot(rows, weight, preferred_element_type=jnp.float32)


def heads_of(width):
    return [slice(at, at + HEAD_DIM) for at in range(0, width, HEAD_DIM)]


def with_ones(value):
    return jnp.concatenate([value, jnp.ones(value.shape, value.dtype)], -1)


def tile_at(index):
    return pl.ds(pl.multiple_of(index * TILE, TILE), TILE)


def ring_of(width):
    return [pltpu.VMEM((SLOTS, width, TILE), jnp.bfloat16), pltpu.SemaphoreType.DMA((SLOTS,))]


def weight_stream(qkv_hbm, out_hbm, ring, sems, kinds):
    tiles = out_hbm.shape[1] // TILE

    def copy(source, place):
        slot = place % SLOTS
        return pltpu.make_async_copy(source, ring.at[slot], sems.at[slot])

    def fetch(place):
        for order, kind in enumerate(kinds):
            pl.when(place // tiles == order)(
                lambda: copy(qkv_hbm.at[kind, :, tile_at(place % tiles)], place).start()
            )
        pl.when(place // tiles == len(kinds))(
            lambda: copy(out_hbm.at[:, tile_at(place % tiles)], place).start()
        )

    def take(place):
        fetch(place + AHEAD)
        copy(out_hbm.at[:, tile_at(0)], place).wait()
        return ring.at[place % SLOTS]

    return fetch, take


def mix_frame(rows_ref, take, base, tiles, keys_ref, values_ref, ready, attended_ref):
    heads = heads_of(TILE)

    def tile(index, carry):
        ready(index)
        weight = take(base + index)
        query = (project(rows_ref[...], weight[...]) * EXPONENT).astype(jnp.bfloat16)
        done = attend(
            [query[:, cols] for cols in heads],
            [keys_ref[index, :, cols] for cols in heads],
            [with_ones(values_ref[index, :, cols]) for cols in heads],
        )
        attended_ref[:, tile_at(index)] = jnp.concatenate(done, -1).astype(jnp.bfloat16)
        return carry

    lax.fori_loop(0, tiles, tile, 0)


def leave_frame(
    tokens_ref, action_ref, gain_ref, attended_ref, take, base, tiles,
    time_ref, middle_ref, rounded_ref, squares_ref, time_hbm, middle_hbm, sems, offset
):
    width = middle_ref.shape[1]
    squares_ref[...] = jnp.zeros_like(squares_ref)

    def middle_copy(index):
        return pltpu.make_async_copy(
            rounded_ref.at[:, tile_at(index)],
            middle_hbm.at[pl.ds(offset, rounded_ref.shape[0]), tile_at(index)], sems.at[1],
        )

    def tile(index, carry):
        weight = take(base + index)
        cols = tile_at(index)
        start = tokens_ref[:, cols].astype(jnp.float32) + action_ref[:, cols]
        middle = start + project(attended_ref[...], weight[...])
        middle_ref[:, cols] = middle
        rounded_ref[:, cols] = middle.astype(jnp.bfloat16)
        squares_ref[...] += jnp.sum(middle * middle, -1, keepdims=True)
        middle_copy(index).start()
        return carry

    lax.fori_loop(0, tiles, tile, 0)
    blocks = time_ref.shape[0] // ROWS

    def time_copy(index):
        here = pl.ds(pl.multiple_of(index * ROWS, ROWS), ROWS)
        return pltpu.make_async_copy(time_ref.at[here, :], time_hbm.at[here, :], sems.at[0])

    def block(index, carry):
        here = pl.ds(pl.multiple_of(index * ROWS, ROWS), ROWS)
        factor = lax.rsqrt(squares_ref[here, :] / width + EPSILON)
        time_ref[here, :] = (middle_ref[here, :] * factor * gain_ref[...]).astype(jnp.bfloat16)
        time_copy(index).start()
        return carry

    lax.fori_loop(0, blocks, block, 0)
    for index in range(tiles):
        middle_copy(index).wait()
    for index in range(blocks):
        time_copy(index).wait()


def first_kernel(
    count, tokens_hbm, rows_ref, pair_ref, space_gain_hbm, time_gain_hbm, qkv_hbm, out_hbm,
    time_hbm, middle_hbm, normed_hbm, keyval_hbm,
    tokens, normed, ring, ring_sem, keyval, attended, time, middle, rounded, squares, action_ref, space_gain_ref, time_gain_ref,
    token_sem, keyval_sem, normed_sem, out_sem, gain_sem
):
    tiles = keyval.shape[1]
    blocks = tokens.shape[0] // ROWS
    fetch, take = weight_stream(qkv_hbm, out_hbm, ring, ring_sem, (1, 2, 0))

    def token_rows(index):
        return pl.ds(pl.multiple_of(index * ROWS, ROWS), ROWS)

    def token_copy(index):
        here = token_rows(index)
        return pltpu.make_async_copy(tokens_hbm.at[here, :], tokens.at[here, :], token_sem.at[index])

    def keyval_copy(kind, index):
        return pltpu.make_async_copy(
            keyval.at[kind, index], keyval_hbm.at[kind, :, tile_at(index)], keyval_sem
        )

    rest = pltpu.make_async_copy(normed.at[pl.ds(count, tokens.shape[0] - count), :], normed_hbm, normed_sem)
    gain_copies = [
        pltpu.make_async_copy(space_gain_hbm, space_gain_ref, gain_sem.at[0]),
        pltpu.make_async_copy(time_gain_hbm, time_gain_ref, gain_sem.at[1]),
    ]
    for copy in gain_copies:
        copy.start()
    for index in range(blocks):
        token_copy(index).start()
    action_ref[...] = own_row(rows_ref, pair_ref)

    def norm_block(index, carry):
        token_copy(index).wait()
        here = token_rows(index)
        normed[here, :] = norm_rows(
            tokens[here, :].astype(jnp.float32) + action_ref[...], space_gain_ref[...]
        )
        return carry

    fetch(0)
    for copy in gain_copies:
        copy.wait()
    norm_block(0, 0)
    for place in range(1, AHEAD):
        fetch(place)
    lax.fori_loop(1, blocks, norm_block, 0)
    rest.start()

    def keyval_tiles(index, carry):
        weights = [take(2 * index + step) for step in range(2)]
        places = [(place // tiles, place % tiles) for place in (2 * index, 2 * index + 1)]
        for (kind, at), weight in zip(places, weights):
            keyval[kind, at] = project(normed[...], weight[...]).astype(jnp.bfloat16)
        for kind, at in places:
            keyval_copy(kind, at).start()
        return carry

    lax.fori_loop(0, tiles, keyval_tiles, 0)
    mix_frame(
        normed.at[pl.ds(0, count), :], take, 2 * tiles, tiles, keyval.at[0], keyval.at[1],
        lambda index: None, attended,
    )
    leave_frame(
        tokens.at[pl.ds(0, count), :], action_ref, time_gain_ref, attended, take, 3 * tiles, tiles,
        time, middle, rounded, squares, time_hbm, middle_hbm, out_sem, 0,
    )
    rest.wait()
    for kind in range(2):
        for index in range(tiles):
            keyval_copy(kind, index).wait()


def first(tokens, action_pieces, pair_index, space_gain, time_gain, qkv, out, count):
    frame, width = tokens.shape
    columns = qkv.shape[2]
    tiles = columns // TILE
    dma = pltpu.SemaphoreType.DMA
    return pl.pallas_call(
        functools.partial(first_kernel, count),
        in_specs=in_hbm(1) + row_specs(action_pieces) + in_hbm(4),
        out_specs=in_hbm(4),
        out_shape=[
            jax.ShapeDtypeStruct((count, width), jnp.bfloat16),
            jax.ShapeDtypeStruct((frame, width), jnp.bfloat16),
            jax.ShapeDtypeStruct((frame - count, width), jnp.bfloat16),
            jax.ShapeDtypeStruct((2, frame, columns), jnp.bfloat16),
        ],
        scratch_shapes=[
            pltpu.VMEM((frame, width), jnp.bfloat16),
            pltpu.VMEM((frame, width), jnp.bfloat16),
            *ring_of(width),
            pltpu.VMEM((2, tiles, frame, TILE), jnp.bfloat16),
            pltpu.VMEM((count, columns), jnp.bfloat16),
            pltpu.VMEM((count, width), jnp.bfloat16),
            pltpu.VMEM((count, width), jnp.float32),
            pltpu.VMEM((count, width), jnp.bfloat16),
            pltpu.VMEM((count, 1), jnp.float32),
            *[pltpu.VMEM((1, width), jnp.float32)] * 3,
            dma((frame // ROWS,)), dma, dma, dma((2,)), dma((2,)),
        ],
        compiler_params=limits(LIMIT),
        cost_estimate=pl.CostEstimate(
            flops=4 * frame * width * columns + 4 * count * width * columns + 8 * count * frame * columns,
            bytes_accessed=8 * width * columns, transcendentals=count * frame * columns // HEAD_DIM,
        ),
        name="space_first",
    )(tokens, action_pieces, pair_index, space_gain, time_gain, qkv, out)


def later_kernel(
    offset, tokens_hbm, rows_ref, pair_ref, time_gain_ref, qkv_hbm, out_hbm, normed_hbm, keyval_hbm, _,
    time_hbm, middle_hbm,
    tokens, normed, ring, ring_sem, keyval, attended, time, middle, rounded, squares, action_ref,
    token_sem, normed_sem, keyval_sem, out_sem
):
    tiles = keyval.shape[1]
    count = tokens.shape[0]
    fetch, take = weight_stream(qkv_hbm, out_hbm, ring, ring_sem, (0,))

    def keyval_copy(kind, index):
        return pltpu.make_async_copy(
            keyval_hbm.at[kind, :, tile_at(index)], keyval.at[kind, index], keyval_sem.at[kind, index]
        )

    normed_copy = pltpu.make_async_copy(normed_hbm, normed, normed_sem)
    token_copy = pltpu.make_async_copy(tokens_hbm.at[pl.ds(offset, count), :], tokens, token_sem)
    def fetch_keyval(index):
        for kind in range(2):
            keyval_copy(kind, index).start()

    normed_copy.start()
    fetch(0)
    fetch_keyval(0)
    action_ref[...] = own_row(rows_ref, pair_ref)
    normed_copy.wait()
    for place in range(1, AHEAD):
        fetch(place)

    def ready(index):
        for kind in range(2):
            keyval_copy(kind, index).wait()
        pl.when(index + 1 < tiles)(lambda: fetch_keyval(index + 1))
        pl.when(index == tiles - 1)(lambda: token_copy.start())

    mix_frame(normed, take, 0, tiles, keyval.at[0], keyval.at[1], ready, attended)
    token_copy.wait()
    leave_frame(
        tokens, action_ref, time_gain_ref, attended, take, tiles, tiles,
        time, middle, rounded, squares, time_hbm, middle_hbm, out_sem, offset,
    )


def later(tokens, action_pieces, pair_index, time_gain, qkv, out, normed, keyval, middle, offset):
    frame, width = tokens.shape
    count = normed.shape[0]
    columns = qkv.shape[2]
    tiles = columns // TILE
    dma = pltpu.SemaphoreType.DMA
    row = pl.BlockSpec((1, width), lambda: (0, 0))
    return pl.pallas_call(
        functools.partial(later_kernel, offset),
        in_specs=in_hbm(1) + row_specs(action_pieces) + [row] + in_hbm(5),
        out_specs=in_hbm(2),
        out_shape=[
            jax.ShapeDtypeStruct((count, width), jnp.bfloat16),
            jax.ShapeDtypeStruct((frame, width), jnp.bfloat16),
        ],
        input_output_aliases={8: 1},
        scratch_shapes=[
            pltpu.VMEM((count, width), jnp.bfloat16),
            pltpu.VMEM((count, width), jnp.bfloat16),
            *ring_of(width),
            pltpu.VMEM((2, tiles, frame, TILE), jnp.bfloat16),
            pltpu.VMEM((count, columns), jnp.bfloat16),
            pltpu.VMEM((count, width), jnp.bfloat16),
            pltpu.VMEM((count, width), jnp.float32),
            pltpu.VMEM((count, width), jnp.bfloat16),
            pltpu.VMEM((count, 1), jnp.float32),
            pltpu.VMEM((1, width), jnp.float32),
            dma, dma, dma((2, tiles)), dma((2,)),
        ],
        compiler_params=limits(LIMIT),
        cost_estimate=pl.CostEstimate(
            flops=4 * count * width * columns + 8 * count * frame * columns,
            bytes_accessed=4 * width * columns, transcendentals=count * frame * columns // HEAD_DIM,
        ),
        name="space_later",
    )(tokens, action_pieces, pair_index, time_gain, qkv, out, normed, keyval, middle)


def time_kernel(
    frames, places, received_any, bias_ref, qkv_hbm, out_hbm, _, update_hbm,
    mixed, update, weights, out_weights, update_sem, weight_sem, out_sem, *fetched
):
    received_ref = fetched[0] if fetched else received_any
    rows = received_ref.shape[0]
    per_device = rows // frames
    tiles = weights.shape[0]
    heads = heads_of(TILE)

    def weight_copies(index):
        return [
            pltpu.make_async_copy(
                qkv_hbm.at[kind, :, tile_at(index)], weights.at[index, kind], weight_sem.at[index, kind]
            )
            for kind in range(3)
        ]

    def out_copy(index):
        return pltpu.make_async_copy(
            out_hbm.at[:, tile_at(index)], out_weights.at[index], out_sem.at[index]
        )

    def update_copy(index):
        return pltpu.make_async_copy(update.at[index], update_hbm.at[:, tile_at(index)], update_sem)

    def split(value):
        return [
            jnp.concatenate(
                [value[start + at:start + at + places, :] for start in range(0, rows, per_device)], 0
            ).astype(jnp.bfloat16)
            for at in range(0, per_device, places)
        ]

    def join(parts):
        return jnp.concatenate(
            [part[at:at + places, :] for at in range(0, frames * places, places) for part in parts], 0
        )

    def mix_tile(index, carry):
        @pl.when(index + 2 < tiles)
        def _():
            for copy in weight_copies(index + 2):
                copy.start()

        @pl.when(index + 2 >= tiles)
        def _():
            share = out_weights.shape[0] // 2
            for step in range(share):
                out_copy((index + 2 - tiles) * share + step).start()

        for copy in weight_copies(index):
            copy.wait()
        entered = received_ref[...]
        query = split(project(entered, weights[index, 0]) * EXPONENT)
        keys = split(project(entered, weights[index, 1]))
        value = split(project(entered, weights[index, 2]))
        parts = []
        for part in range(len(query)):
            done = attend(
                [query[part][:, cols] for cols in heads],
                [keys[part][:, cols] for cols in heads],
                [with_ones(value[part][:, cols]) for cols in heads],
                bias_ref[...],
            )
            parts.append(jnp.concatenate(done, -1))
        mixed[:, tile_at(index)] = join(parts).astype(jnp.bfloat16)
        return carry

    def out_tile(index, carry):
        out_copy(index).wait()
        update[index] = project(mixed[...], out_weights[index]).astype(jnp.bfloat16)
        update_copy(index).start()
        return carry

    if fetched:
        received_copy = pltpu.make_async_copy(received_any, *fetched)
        received_copy.start()
        for copy in weight_copies(0):
            copy.start()
        received_copy.wait()
        for copy in weight_copies(1):
            copy.start()
    else:
        for copy in weight_copies(0) + weight_copies(1):
            copy.start()
    lax.fori_loop(0, tiles, mix_tile, 0)
    lax.fori_loop(0, out_weights.shape[0], out_tile, 0)
    for index in range(out_weights.shape[0]):
        update_copy(index).wait()


def time_mix(received, bias, qkv, out, sent, frames, places, held):
    rows, width = received.shape
    columns = qkv.shape[2]
    block = frames * places
    tiles, out_tiles = columns // TILE, width // TILE
    dma = pltpu.SemaphoreType.DMA
    whole = pl.BlockSpec(memory_space=pltpu.VMEM)
    return pl.pallas_call(
        functools.partial(time_kernel, frames, places),
        in_specs=([whole] if held else in_hbm(1)) + [whole] + in_hbm(3),
        out_specs=in_hbm(1)[0],
        out_shape=jax.ShapeDtypeStruct((rows, width), jnp.bfloat16),
        scratch_shapes=[
            pltpu.VMEM((rows, columns), jnp.bfloat16),
            pltpu.VMEM((out_tiles, rows, TILE), jnp.bfloat16),
            pltpu.VMEM((tiles, 3, width, TILE), jnp.bfloat16),
            pltpu.VMEM((out_tiles, columns, TILE), jnp.bfloat16),
            dma, dma((tiles, 3)), dma((out_tiles,)),
        ] + ([] if held else [pltpu.VMEM((rows, width), jnp.bfloat16), dma]),
        input_output_aliases={4: 0},
        compiler_params=limits(HELD_LIMIT if held else LIMIT),
        cost_estimate=pl.CostEstimate(
            flops=8 * rows * width * columns, bytes_accessed=8 * width * columns,
            transcendentals=rows * block * columns // HEAD_DIM,
        ),
        name="time_mix",
    )(received, bias, qkv, out, sent)


def add_kernel(offset, update_ref, middle_hbm, result_hbm, middle, result, in_sem, result_sem):
    blocks = update_ref.shape[0] // ROWS

    def block_at(index, base=0):
        return pl.ds(pl.multiple_of(base + index * ROWS, ROWS), ROWS)

    def in_copy(index):
        return pltpu.make_async_copy(
            middle_hbm.at[block_at(index, offset), :], middle.at[block_at(index), :], in_sem.at[index]
        )

    def result_copy(index):
        return pltpu.make_async_copy(
            result.at[block_at(index), :], result_hbm.at[block_at(index, offset), :], result_sem
        )

    def block(index, carry):
        in_copy(index).wait()
        here = block_at(index)
        result[here, :] = (
            middle[here, :].astype(jnp.float32) + update_ref[here, :].astype(jnp.float32)
        ).astype(jnp.bfloat16)
        result_copy(index).start()
        return carry

    for index in range(blocks):
        in_copy(index).start()
    lax.fori_loop(0, blocks, block, 0)
    for index in range(blocks):
        result_copy(index).wait()


def add_update(update, middle, offset):
    rows, width = update.shape
    dma = pltpu.SemaphoreType.DMA
    return pl.pallas_call(
        functools.partial(add_kernel, offset),
        in_specs=[pl.BlockSpec(memory_space=pltpu.VMEM)] + in_hbm(1),
        out_specs=in_hbm(1)[0],
        out_shape=jax.ShapeDtypeStruct(middle.shape, jnp.bfloat16),
        scratch_shapes=[pltpu.VMEM((rows, width), jnp.bfloat16)] * 2 + [dma((rows // ROWS,)), dma],
        input_output_aliases={1: 0},
        compiler_params=limits(16),
        cost_estimate=pl.CostEstimate(
            flops=rows * width, bytes_accessed=6 * rows * width, transcendentals=0
        ),
        name="time_add",
    )(update, middle)


def fold_projection(weights, row_count, segment):
    flat_rows = segment.reshape(row_count, segment.shape[-1])
    return jnp.einsum("rc,icj->irj", flat_rows, weights, preferred_element_type=jnp.float32)


def space_frame(triple):
    query, keys, values = triple
    tokens_frame, columns = query.shape
    query = query.reshape(tokens_frame, columns // HEAD_DIM, HEAD_DIM)
    keys = keys.reshape(tokens_frame, columns // HEAD_DIM, HEAD_DIM)
    values = values.reshape(tokens_frame, columns // HEAD_DIM, HEAD_DIM)
    scores = jnp.einsum(
        "qhd,khd->hqk", query, keys, preferred_element_type=jnp.float32
    ) * HEAD_DIM ** (-0.5)
    probabilities = jax.nn.softmax(scores, -1).astype(jnp.bfloat16)
    mixture = jnp.einsum(
        "hqk,khd->qhd", probabilities, values, preferred_element_type=jnp.float32
    ).astype(jnp.bfloat16)
    return mixture.reshape(tokens_frame, columns)


def body_split_features(
    tokens,
    action_rows,
    pair_index,
    episode_id,
    space_gain,
    space_qkv,
    space_out,
    time_gain,
    time_qkv,
    time_out,
):
    frames_here, per_frame, share_width = tokens.shape
    width = share_width * lax.axis_size("tensor")
    columns = space_qkv.shape[2]
    row_count = frames_here * per_frame
    offset = lax.axis_index("tensor") * share_width
    every_row = lax.all_gather(action_rows, "tm", axis=0, tiled=True)
    frame_count = every_row.shape[0]
    picker = (pair_index[:, None] == jnp.arange(frame_count, dtype=jnp.int32)[None, :]).astype(
        jnp.bfloat16
    )
    action = jnp.dot(picker, every_row, preferred_element_type=jnp.float32)
    start = tokens.astype(jnp.float32) + action[:, None, :]
    squares = lax.psum(jnp.sum(start * start, -1), "tensor")
    factor = lax.rsqrt(squares / width + EPSILON)[..., None]
    space_normed = (
        start * factor * lax.dynamic_slice_in_dim(space_gain, offset, share_width)
    ).astype(jnp.bfloat16)
    space_proj = fold_projection(
        space_qkv, row_count, lax.all_gather(space_normed, "tensor", axis=2, tiled=True)
    ).astype(jnp.bfloat16)
    space_proj = space_proj.reshape(3, frames_here, per_frame, columns)
    attended = lax.map(space_frame, (space_proj[0], space_proj[1], space_proj[2]))
    partial_space = jnp.dot(
        attended.reshape(row_count, columns), space_out, preferred_element_type=jnp.float32
    ).reshape(frames_here, per_frame, width)
    own_part = lax.dynamic_slice_in_dim(partial_space, offset, share_width, 2) + start
    term_full = lax.dynamic_update_slice_in_dim(partial_space, own_part, offset, 2)
    summed = lax.psum(term_full.astype(jnp.bfloat16), "tensor").astype(jnp.float32)
    full_squares = jnp.sum(summed * summed, -1)
    time_normed = (
        summed * lax.rsqrt(full_squares / width + EPSILON)[..., None] * time_gain
    ).astype(jnp.bfloat16)
    time_proj = jnp.einsum(
        "rc,icj->irj",
        time_normed.reshape(row_count, width),
        time_qkv,
        preferred_element_type=jnp.float32,
    ).astype(jnp.bfloat16)
    middle = lax.dynamic_slice_in_dim(summed, offset, share_width, 2)
    time_proj = time_proj.reshape(3, frames_here, per_frame, columns)
    moved = (
        lax.all_to_all(time_proj[0], "tm", split_axis=1, concat_axis=0, tiled=True),
        lax.all_to_all(time_proj[1], "tm", split_axis=1, concat_axis=0, tiled=True),
        lax.all_to_all(time_proj[2], "tm", split_axis=1, concat_axis=0, tiled=True),
    )
    query_time, keys_time, values_time = moved
    places = query_time.shape[1]
    heads_here = columns // HEAD_DIM
    query_time = query_time.reshape(frame_count, places, heads_here, HEAD_DIM)
    keys_time = keys_time.reshape(frame_count, places, heads_here, HEAD_DIM)
    values_time = values_time.reshape(frame_count, places, heads_here, HEAD_DIM)
    scores = jnp.einsum(
        "fphd,gphd->phfg", query_time, keys_time, preferred_element_type=jnp.float32
    ) * HEAD_DIM ** (-0.5)
    order = jnp.arange(frame_count, dtype=jnp.int32)
    allowed = (episode_id[:, None] == episode_id[None, :]) & (order[None, :] <= order[:, None])
    scores = jnp.where(allowed, scores, -1e30)
    probabilities = jax.nn.softmax(scores, -1).astype(jnp.bfloat16)
    mixture = jnp.einsum(
        "phfg,gphd->fphd", probabilities, values_time, preferred_element_type=jnp.float32
    ).astype(jnp.bfloat16)
    returned = lax.all_to_all(
        mixture.reshape(frame_count, places, columns), "tm", split_axis=0, concat_axis=1, tiled=True
    )
    partial_time = jnp.dot(
        returned.reshape(row_count, columns), time_out, preferred_element_type=jnp.float32
    ).reshape(frames_here, per_frame, width)
    return (
        middle
        + lax.psum_scatter(
            partial_time.astype(jnp.bfloat16), "tensor", scatter_dimension=2, tiled=True
        ).astype(jnp.float32)
    ).astype(jnp.bfloat16)


def exchange(parts, groups):
    return lax.all_to_all(parts, "tm", split_axis=0, concat_axis=0, axis_index_groups=groups)


def frame_bias(episodes, places):
    count = episodes.shape[0] * places
    frames, spots = np.divmod(np.arange(count), places)
    earlier = (spots[:, None] == spots[None, :]) & (frames[None, :] <= frames[:, None])
    owners = jnp.broadcast_to(episodes[:, None], (episodes.shape[0], places)).reshape(count)
    return jnp.where(earlier & (owners[:, None] == owners[None, :]), 0.0, -1e30).astype(jnp.float32)


def body_whole_features(
    half_head,
    whole_head,
    tokens,
    action_rows,
    pair_index,
    episode_id,
    space_gain,
    space_qkv,
    space_out,
    time_gain,
    time_qkv,
    time_out,
):
    _, per_frame, width = tokens.shape
    columns = space_qkv.shape[2]
    frame_count = lax.axis_size("tm")
    tokens = tokens.reshape(per_frame, width)
    piece = width // 8
    action_pieces = exchange(
        jnp.broadcast_to(action_rows.reshape(1, 8, piece), (frame_count, 8, piece)), None
    )
    space_gain = space_gain.reshape(1, width)
    time_gain = time_gain.reshape(1, width)

    def over(group_size, head):
        groups = [
            list(range(start, start + group_size)) for start in range(0, frame_count, group_size)
        ]
        if group_size == frame_count:
            groups = None

        def places_together(count):
            places = count // group_size
            if places % 16 == 0 and group_size * 16 <= 256:
                return 16
            return 8

        def turn(rows):
            parts = rows.reshape(group_size, rows.shape[0] // group_size, rows.shape[1])
            return exchange(parts, groups).reshape(rows.shape)

        def temporal(rows, sent, biases):
            places = places_together(rows.shape[0])
            return time_mix(
                rows, biases[places], time_qkv, time_out, sent, group_size, places, groups is not None
            )

        def run():
            start = lax.axis_index("tm") // group_size * group_size
            episodes = lax.dynamic_slice_in_dim(episode_id, start, group_size)
            biases = {
                places: frame_bias(episodes, places)
                for places in sorted({places_together(count) for count in (head, per_frame - head)})
            }

            early_normed, middle, later_rows, keyval = first(
                tokens, action_pieces, pair_index, space_gain, time_gain, space_qkv, space_out, head
            )
            early = turn(early_normed)
            late_normed, middle = later(
                tokens, action_pieces, pair_index, time_gain, space_qkv, space_out, later_rows, keyval,
                middle, head,
            )
            late = turn(late_normed)
            early_update = turn(temporal(early, early_normed, biases))
            late_update = turn(temporal(late, late_normed, biases))
            result = add_update(late_update, add_update(early_update, middle, 0), head)
            return result.reshape(1, per_frame, width)

        return run

    half = frame_count // 2
    apart = episode_id[half - 1] != episode_id[half]
    return lax.cond(apart, over(half, half_head), over(frame_count, whole_head))


def head_rows(per_frame, group_size, share):
    unit = math.lcm(ROWS, 8 * group_size)
    return max(unit, per_frame * share // 12 // unit * unit)


def solution(mesh):
    sizes = dict(mesh.shape)

    def body(*arrays):
        frames_here, per_frame, width = arrays[0].shape
        frame_count = sizes["tm"]
        heads = [head_rows(per_frame, frame_count // 2, 6), head_rows(per_frame, frame_count, 4)]
        fits = (
            sizes["tensor"] == 1
            and frames_here == 1
            and frame_count % 2 == 0
            and per_frame % math.lcm(ROWS, 8 * frame_count) == 0
            and all(head < per_frame for head in heads)
            and width % (2 * TILE) == 0
            and arrays[5].shape[2] == width
        )
        if fits:
            return body_whole_features(*heads, *arrays)
        return body_split_features(*arrays)

    return jax.shard_map(
        body,
        mesh=mesh,
        in_specs=(
            P("tm", None, "tensor"),
            P("tm", "tensor"),
            P("tm"),
            P(),
            P(),
            P(None, None, "tensor"),
            P("tensor", None),
            P(),
            P(None, None, "tensor"),
            P("tensor", None),
        ),
        out_specs=P("tm", None, "tensor"),
        check_vma=False,
    )
```
